128 devices in a mesh: sx: 8 (over z, core), sy: 16 (over y, x).
Axes of the slice: x: 4, y: 4, z: 4, core: 2. Of those that a mesh axis runs over, the one named last changes fastest.
Arguments:
- features: bfloat16 [4096, 4096], P(('sx', 'sy')), may hold values from -8 to 8
- occupancy: int32 [4096, 64], P(('sx', 'sy')), may hold values 0 or 1
- adjacency: int32 [4096, 27], P(('sx', 'sy')), may hold values from -1 to 4095, as said below
- conv_one: bfloat16 [27, 64, 64], replicated, may hold values from -0.15625 to 0.15625
- conv_two: bfloat16 [27, 64, 64], replicated, may hold values from -0.15625 to 0.15625
- scale_one: float32 [64], replicated, may hold values from 0.5 to 1.5
- shift_one: float32 [64], replicated, may hold values from -2.5 to 2.5
- scale_two: float32 [64], replicated, may hold values from 0.5 to 1.5
- shift_two: float32 [64], replicated, may hold values from -2.5 to 2.5
- w_query: bfloat16 [64, 64], replicated, may hold values from -8 to 8
- w_key: bfloat16 [64, 64], replicated, may hold values from -0.75 to 0.75
- w_value: bfloat16 [64, 64], replicated, may hold values from -0.75 to 0.75
- w_out: bfloat16 [64, 64], replicated, may hold values from -0.75 to 0.75
Outputs:
- refined: bfloat16 [4096, 4096], P(('sx', 'sy'))
The draws below stay inside these ranges and needn't reach their ends.
Inputs may be any that keep to these rules, and one draw needn't show every extreme that they name: `adjacency`: brick ids are (i * 16 + j) * 32 + local index for the device at sx index i and sy index j. The scene is a grid of brick cells; that device owns the cells with x in [i * 4, (i+1) * 4), y in [j * 4, (j+1) * 4) and z in [0, 4), and holds exactly 32 occupied ones in ascending cell order (x, y, z). Entry (ox+1)*9 + (oy+1)*3 + (oz+1) is the id of the occupied cell at that offset, -1 if it is empty or outside the grid; entry 13 is the brick itself.
All inputs are finite; a program needn't handle non-finite values. No bound on the sum of `occupancy` on one device may be relied on, other than what follows from the above.
Results may differ from the reference program's by a relative error of at most 0.011.
Values may be sent and summed in bfloat16 or wider, within the bound.
No kernel may reach another device: no remote copies, remote signals or barrier semaphores. Data moves between devices by JAX's collectives and lax.ppermute only.
A program may use at most 128 MiB of HBM per device.

```python
import math
import jax
import jax.numpy as jnp
from jax import lax

C = 64
HEADS = 2
BF = 4
B_DEV = 32
GZ = 4
BRICKS = 4096
N_SX = 8
N_SY = 16
DEVICES = 128


def occupied_cells(key):
    n_cells = BF * BF * GZ
    scores = jax.random.randint(key, (DEVICES, n_cells), 0, 2 ** 16) * n_cells + jnp.arange(n_cells, dtype=jnp.int32)[None, :]
    cell_x = jnp.arange(n_cells, dtype=jnp.int32) // (BF * GZ)
    cell_y = jnp.arange(n_cells, dtype=jnp.int32) // GZ % BF
    device = jnp.arange(DEVICES, dtype=jnp.int32)[:, None]
    forced = (device == 0) & (cell_x[None, :] == BF - 1) | (device == N_SY) & (cell_x[None, :] == 0)
    forced = forced | (device == N_SY + 1) & (cell_x[None, :] == 0) & (cell_y[None, :] == 0)
    scores = scores + forced.astype(jnp.int32) * 2 ** 28
    chosen = lax.top_k(scores, B_DEV)[1]
    return jnp.sort(chosen, axis=1).astype(jnp.int32)


def brick_geometry(key):
    chosen_cells = occupied_cells(key)
    device = jnp.arange(DEVICES, dtype=jnp.int32)[:, None]
    glob_x = (device // N_SY * BF + chosen_cells // (BF * GZ)).reshape(-1)
    glob_y = (device % N_SY * BF + chosen_cells // GZ % BF).reshape(-1)
    glob_z = (chosen_cells % GZ).reshape(-1)
    span_x = BF * N_SX
    span_y = BF * N_SY
    flat_cells = (glob_x * span_y + glob_y) * GZ + glob_z
    brick_ids = jnp.arange(DEVICES * B_DEV, dtype=jnp.int32)
    cell_grid = jnp.full((span_x * span_y * GZ,), -1, jnp.int32).at[flat_cells].set(brick_ids)
    offsets = jnp.arange(27, dtype=jnp.int32)
    off_x = offsets // 9 - 1
    off_y = offsets // 3 % 3 - 1
    off_z = offsets % 3 - 1
    near_x = glob_x[:, None] + off_x[None, :]
    near_y = glob_y[:, None] + off_y[None, :]
    near_z = glob_z[:, None] + off_z[None, :]
    inside = (near_x >= 0) & (near_x < span_x) & (near_y >= 0) & (near_y < span_y) & (near_z >= 0) & (near_z < GZ)
    lookup = (jnp.clip(near_x, 0, span_x - 1) * span_y + jnp.clip(near_y, 0, span_y - 1)) * GZ + jnp.clip(near_z, 0, GZ - 1)
    return jnp.where(inside, cell_grid[lookup], -1).astype(jnp.int32)


def draw_adjacency(key, part):
    return brick_geometry(key)


def draw_features(key, part):
    key = jax.random.fold_in(key, 11)
    row_key, value_key = jax.random.split(key, 2)
    rows_total = DEVICES * B_DEV
    row_scale = jnp.exp(jax.random.uniform(row_key, (rows_total, 1), minval=-1.15, maxval=1.15))
    values = jax.random.normal(value_key, (rows_total, 64 * C))
    return jnp.clip(values * row_scale, -8.0, 8.0).astype(jnp.bfloat16)


def draw_w_query(key, part):
    key = jax.random.fold_in(key, 23)
    base_draw = jnp.clip(jax.random.normal(key, (C, C)), -5.0, 5.0) / math.sqrt(C)
    return jnp.clip(base_draw, -8.0, 8.0).astype(jnp.bfloat16)


def touch_ends(entries, own_key, smallest, high):
    dims = entries.shape
    index_at = [jax.random.randint(jax.random.fold_in(own_key, axis), (), 0, dims[axis]) for axis in range(len(dims))]
    entries = entries.at[tuple(index_at)].set(smallest)
    longest = dims.index(max(dims))
    index_at[longest] = (index_at[longest] + 1) % dims[longest]
    return entries.at[tuple(index_at)].set(high)


def gaussian(key, shape, spread, reach, kind=jnp.bfloat16):
    return jnp.clip(spread * jax.random.normal(key, shape, jnp.float32), -reach, reach).astype(kind)


def setup_inputs(seed: int = 0) -> dict:
    key_list = jax.random.split(jax.random.key(seed), 14)
    features = draw_features(jax.random.fold_in(key_list[13], 71), 0)
    occupancy = touch_ends((jax.random.randint(key_list[1], (BRICKS, 64), 0, 2) < 1).astype(jnp.int32), jax.random.fold_in(key_list[1], 1), 0, 1)
    adjacency = draw_adjacency(jax.random.fold_in(key_list[13], 71), 0)
    conv_one = gaussian(key_list[3], (27, C, C), (27 * C) ** -0.5, 0.15625)
    conv_two = gaussian(key_list[4], (27, C, C), (27 * C) ** -0.5, 0.15625)
    scale_one = jnp.clip(jax.random.uniform(key_list[5], (C,), jnp.float32, 0.5, 1.5), 0.5, 1.5)
    shift_one = gaussian(key_list[6], (C,), 0.5, 2.5, jnp.float32)
    scale_two = jnp.clip(jax.random.uniform(key_list[7], (C,), jnp.float32, 0.5, 1.5), 0.5, 1.5)
    shift_two = gaussian(key_list[8], (C,), 0.5, 2.5, jnp.float32)
    w_query = draw_w_query(jax.random.fold_in(key_list[13], 71), 0)
    w_key = gaussian(key_list[10], (C, C), C ** -0.5, 0.75)
    w_value = gaussian(key_list[11], (C, C), C ** -0.5, 0.75)
    w_out = gaussian(key_list[12], (C, C), C ** -0.5, 0.75)
    return dict(features=features, occupancy=occupancy, adjacency=adjacency, conv_one=conv_one, conv_two=conv_two, scale_one=scale_one, shift_one=shift_one, scale_two=scale_two, shift_two=shift_two, w_query=w_query, w_key=w_key, w_value=w_value, w_out=w_out)


edge_spans = ((3, 4), (0, 4), (0, 1))
epsilon = 1e-05

def assemble(fetch, channels):
    planes = []
    for i in range(3):
        rows_y = []
        for j in range(3):
            columns = []
            for l in range(3):
                brick_cube = fetch(i * 9 + j * 3 + l).reshape(-1, 4, 4, 4, channels)
                columns.append(brick_cube[:, edge_spans[i][0]:edge_spans[i][1], edge_spans[j][0]:edge_spans[j][1], edge_spans[l][0]:edge_spans[l][1], :])
            rows_y.append(jnp.concatenate(columns, axis=3))
        planes.append(jnp.concatenate(rows_y, axis=2))
    padded = jnp.concatenate(planes, axis=1)
    return padded.reshape(padded.shape[0], 6, 6, 6 * channels)

def band_weights(weight, channels):
    tap_weights = weight.astype(jnp.float32).reshape(3, 3, 3, channels, channels)
    inner_pos = jnp.arange(6)[None, :, None]
    outer_pos = jnp.arange(4)[None, None, :]
    select = (inner_pos - outer_pos == jnp.arange(3)[:, None, None]).astype(jnp.float32)
    band_matrix = jnp.einsum('xyzcd,zio->xyicod', tap_weights, select, precision=lax.Precision.HIGHEST)
    return band_matrix.reshape(3, 3, 6 * channels, 4 * channels).astype(jnp.bfloat16)

def convolve(padded, band_matrix):
    bricks = padded.shape[0]
    out_lanes = band_matrix.shape[3]
    accumulated = jnp.zeros((bricks * 16, out_lanes), jnp.float32)
    for i in range(3):
        for j in range(3):
            window = padded[:, i:i + 4, j:j + 4, :].reshape(bricks * 16, -1)
            accumulated = accumulated + jnp.dot(window, band_matrix[i, j], preferred_element_type=jnp.float32)
    return accumulated.reshape(bricks, 16 * out_lanes)

def reference(features, occupancy, adjacency, conv_one, conv_two, scale_one, shift_one, scale_two, shift_two, w_query, w_key, w_value, w_out):
    total_bricks, width_lanes = features.shape
    channels = width_lanes // 64
    voxel_cover = jnp.repeat(occupancy, channels, axis=1).astype(jnp.bfloat16)
    masked = features * voxel_cover
    brick_rows = jnp.where(adjacency < 0, total_bricks, adjacency).astype(jnp.int32)

    def sparse_conv(field, weight):
        band_matrix = band_weights(weight, channels)
        lookup_table = jnp.concatenate([field, jnp.zeros((1, width_lanes), field.dtype)], axis=0)

        def one_block(block_rows):
            padded = assemble(lambda o: jnp.take(lookup_table, block_rows[:, o], axis=0), channels)
            return convolve(padded, band_matrix)
        blocks = brick_rows.reshape(N_SX * N_SY, B_DEV, 27)
        return lax.map(one_block, blocks).reshape(total_bricks, width_lanes)
    pre_one = sparse_conv(masked, conv_one)
    first = jax.nn.relu(pre_one * jnp.tile(scale_one, 64) + jnp.tile(shift_one, 64))
    tokens = (lax.optimization_barrier(jnp.sum(masked.reshape(total_bricks, 64, channels).astype(jnp.float32), axis=1)) / 8.0).astype(jnp.bfloat16)
    queries = jnp.dot(tokens, w_query, preferred_element_type=jnp.float32).astype(jnp.bfloat16)
    key_rows = jnp.dot(tokens, w_key, preferred_element_type=jnp.float32).astype(jnp.bfloat16)
    value_rows = jnp.dot(tokens, w_value, preferred_element_type=jnp.float32).astype(jnp.bfloat16)
    head_dim = channels // HEADS
    scaling = 1.0 / math.sqrt(head_dim)
    group_size = N_SY * B_DEV

    def group_attention(block):
        query_part, key_part, value_part = block
        query_heads = query_part.astype(jnp.float32).reshape(group_size, HEADS, head_dim)
        key_heads = key_part.astype(jnp.float32).reshape(group_size, HEADS, head_dim)
        value_heads = value_part.astype(jnp.float32).reshape(group_size, HEADS, head_dim)
        logits = jnp.einsum('qhd,khd->hqk', query_heads, key_heads, precision=lax.Precision.HIGHEST) * scaling
        maxima = lax.optimization_barrier(jnp.max(logits, axis=2, keepdims=True))
        softmax_p = jnp.exp(logits - maxima)
        totals = lax.optimization_barrier(jnp.sum(softmax_p, axis=2))
        context = jnp.einsum('hqk,khd->qhd', softmax_p, value_heads, precision=lax.Precision.HIGHEST)
        context = context / jnp.transpose(totals)[:, :, None]
        return context.reshape(group_size, channels)
    context = lax.map(group_attention, (queries.reshape(N_SX, group_size, channels), key_rows.reshape(N_SX, group_size, channels), value_rows.reshape(N_SX, group_size, channels)))
    context = context.reshape(total_bricks, channels)
    attended = (context / jnp.sqrt(lax.optimization_barrier(jnp.mean(context * context, axis=1, keepdims=True)) + epsilon)).astype(jnp.bfloat16)
    global_term = jnp.dot(attended, w_out, preferred_element_type=jnp.float32)
    hidden = ((first + jnp.tile(global_term, (1, 64))) * voxel_cover).astype(jnp.bfloat16)
    pre_two = sparse_conv(hidden, conv_two)
    result = jax.nn.relu(pre_two * jnp.tile(scale_two, 64) + jnp.tile(shift_two, 64) + masked.astype(jnp.float32)) * voxel_cover
    return result.astype(jnp.bfloat16)
```

```python
import math

import jax
import jax.numpy as jnp
from jax import lax
from jax.experimental import pallas as pl
from jax.experimental.pallas import tpu as pltpu
from jax.sharding import PartitionSpec as P

HEADS = 2
C = 64
COL = 4 * C
BRICKS = 32
EPSILON = 1e-05
FAR = -(1 << 20)
VMEM_LIMIT = 48 * 1024 * 1024
f32, bf16 = jnp.float32, jnp.bfloat16


def call(kernel, out_shape, args, scratch=(), flops=0, bytes_accessed=0):
    vmem = pl.BlockSpec(memory_space=pltpu.VMEM)
    return pl.pallas_call(
        kernel,
        out_shape=out_shape,
        in_specs=[vmem] * len(args),
        out_specs=jax.tree.map(lambda _: vmem, out_shape),
        scratch_shapes=list(scratch),
        compiler_params=pltpu.CompilerParams(vmem_limit_bytes=VMEM_LIMIT),
        cost_estimate=pl.CostEstimate(
            flops=flops, bytes_accessed=bytes_accessed, transcendentals=0
        ),
    )(*args)


def shape(*dims, dtype=bf16):
    return jax.ShapeDtypeStruct(dims, dtype)


def column(x, y):
    return slice((x * 4 + y) * COL, (x * 4 + y + 1) * COL)


def face_x(ref, x):
    return ref[:, x * 4 * COL : (x + 1) * 4 * COL]


def face_y(ref, y):
    return jnp.concatenate([ref[:, column(x, y)] for x in range(4)], axis=1)


def pick(flag, a, b):
    return jnp.where(flag, a, b)


def parities():
    even_x = lax.rem(lax.axis_index("sx"), 2) == 0
    even_y = lax.rem(lax.axis_index("sy"), 2) == 0
    return even_x, even_y


def pair_exchange(value, axis, phase):
    count = lax.axis_size(axis)
    if phase == 0:
        pairs = [(s, s ^ 1) for s in range(count)]
    else:
        pairs = [(s, ((s + 1) ^ 1) - 1) for s in range(1, count - 1)]
    return lax.ppermute(value, axis, pairs)


def send_faces(field, xs0, xs1, ys0, ys1):
    even_x, even_y = parities()
    low, high = face_x(field, 0), face_x(field, 3)
    xs0[...] = pick(even_x, high, low)
    xs1[...] = pick(even_x, low, high)
    low, high = face_y(field, 0), face_y(field, 3)
    ys0[...] = pick(even_y, high, low)
    ys1[...] = pick(even_y, low, high)


def prepare_kernel(
    feat, occ, w_q, w_k, w_v, masked, cover, queries, kv, xs0, xs1, ys0, ys1
):
    occupied = occ[...].astype(f32).astype(bf16)
    row = lax.broadcasted_iota(jnp.int32, (64, COL), 0)
    voxel = lax.shift_right_logical(lax.broadcasted_iota(jnp.int32, (64, COL), 1), 6)
    total = jnp.zeros((BRICKS, 128), f32)
    for k in range(16):
        spread = (row == voxel + 4 * k).astype(f32).astype(bf16)
        cov = jnp.dot(occupied, spread, preferred_element_type=f32).astype(bf16)
        part = feat[:, k * COL : (k + 1) * COL] * cov
        cover[:, k * COL : (k + 1) * COL] = cov
        masked[:, k * COL : (k + 1) * COL] = part
        wide = part.astype(f32)
        total = total + wide[:, :128] + wide[:, 128:]
    summed = total[:, :C] + total[:, C:]
    tokens = (summed / 8.0).astype(bf16)
    q = jnp.dot(tokens, w_q[...], preferred_element_type=f32)
    k = jnp.dot(tokens, w_k[...], preferred_element_type=f32)
    v = jnp.dot(tokens, w_v[...], preferred_element_type=f32)
    wide_q = jnp.concatenate([q, jnp.zeros_like(q)], axis=1)
    lane = lax.broadcasted_iota(jnp.int32, (BRICKS, 128), 1)
    per_head = [
        jnp.where(lax.shift_right_logical(lane, 5) == h, wide_q, 0.0) for h in range(HEADS)
    ]
    queries[...] = jnp.concatenate(per_head, axis=0).astype(bf16)
    both = jnp.concatenate([k, v], axis=1).astype(bf16)
    kv[...] = jnp.broadcast_to(both[None], kv.shape)
    send_faces(masked, xs0, xs1, ys0, ys1)


def band_kernel(weight, band):
    zero = jnp.zeros((C, C), bf16)
    for t in range(9):
        for r, z_in in enumerate((0, 1, 2, 3, 4, -1)):
            blocks = []
            for z_out in range(4):
                tap = z_in - z_out + 1
                blocks.append(weight[t * 3 + tap] if 0 <= tap < 3 else zero)
            band[t, r * C : (r + 1) * C, :] = jnp.concatenate(blocks, axis=1)


def corner_kernel(ys0, ys1, r0, r1, s0, s1):
    _, even_y = parities()
    for own, out, first in ((ys0, s0, even_y), (ys1, s1, jnp.logical_not(even_y))):
        out[:, : 4 * COL] = own[...]
        for k, ref in enumerate((r0, r1)):
            out[:, (4 + k) * COL : (5 + k) * COL] = pick(first, ref[:, 3 * COL :], ref[:, :COL])


def gather_neighbours(field, halo_x, halo_y, adj_ref, padded):
    even_x, even_y = parities()
    r0, r1 = halo_x
    t0, t1 = halo_y
    ids = jnp.where(adj_ref[...] < 0, FAR, adj_ref[...])
    base = (lax.axis_index("sx") * lax.axis_size("sy") + lax.axis_index("sy")) * BRICKS
    step = {-1: -lax.axis_size("sy") * BRICKS, 0: 0, 1: lax.axis_size("sy") * BRICKS}

    def from_x(ox, y):
        lanes = slice(y * COL, (y + 1) * COL)
        a, b = (r1, r0) if ox < 0 else (r0, r1)
        return pick(even_x, a[:, lanes], b[:, lanes])

    def from_y(oy, x):
        lanes = slice(x * COL, (x + 1) * COL)
        a, b = (t1, t0) if oy < 0 else (t0, t1)
        return pick(even_y, a[:, lanes], b[:, lanes])

    def from_corner(ox, oy):
        p, q = slice(4 * COL, 5 * COL), slice(5 * COL, 6 * COL)
        a, b = (t1, t0) if oy < 0 else (t0, t1)
        u, v = (q, p) if ox < 0 else (p, q)
        return pick(
            even_y, pick(even_x, a[:, u], a[:, v]), pick(even_x, b[:, u], b[:, v])
        )

    lane_low = lax.broadcasted_iota(jnp.int32, (BRICKS, 128), 1) < C
    for ox in (-1, 0, 1):
        for oy in (-1, 0, 1):
            sources = [(0, 0)]
            if ox:
                sources.append((ox, 0))
            if oy:
                sources.append((0, oy))
            if ox and oy:
                sources.append((ox, oy))
            lane = lax.broadcasted_iota(jnp.int32, (BRICKS, 32 * len(sources)), 1)
            candidate = base + jnp.bitwise_and(lane, 31)
            for k, (dx, dy) in enumerate(sources):
                if k:
                    slot = lax.shift_right_logical(lane, 5) == k
                    candidate = candidate + jnp.where(slot, step[dx] + dy * BRICKS, 0)
            select = []
            centre = ox == 0 and oy == 0
            for oz in (1, -1) if centre else (1, -1, 0):
                o = (ox + 1) * 9 + (oy + 1) * 3 + (oz + 1)
                select.append((ids[:, o : o + 1] == candidate).astype(f32).astype(bf16))
            select = jnp.concatenate(select, axis=0)
            x_in = {-1: (3,), 0: range(4), 1: (0,)}[ox]
            y_in = {-1: (3,), 0: range(4), 1: (0,)}[oy]
            for x in x_in:
                for y in y_in:
                    parts = [field[:, column(x, y)]]
                    if ox:
                        parts.append(from_x(ox, y))
                    if oy:
                        parts.append(from_y(oy, x))
                    if ox and oy:
                        parts.append(from_corner(ox, oy))
                    table = parts[0] if len(parts) == 1 else jnp.concatenate(parts, axis=0)
                    got = jnp.dot(select, table, preferred_element_type=f32).astype(bf16)
                    above, below = got[:BRICKS, :128], got[BRICKS : 2 * BRICKS, 128:]
                    core = parts[0] if centre else got[2 * BRICKS :]
                    px = {-1: 0, 0: 1 + x, 1: 5}[ox]
                    py = {-1: 0, 0: 1 + y, 1: 5}[oy]
                    padded[px, py, :, :COL] = core
                    padded[px, py, :, COL:] = jnp.where(lane_low, above, below)


def convolve(padded, band, acc):
    for t in range(9):
        i, j = t // 3, t % 3
        window = padded[i : i + 4, j : j + 4].reshape(16 * BRICKS, 6 * C)
        part = jnp.dot(window, band[t], preferred_element_type=f32)
        if t == 0:
            acc[...] = part
        else:
            acc[...] += part


def four(ref):
    return jnp.concatenate([ref[...]] * 4, axis=1)


def attention(queries, kv_ref, w_out):
    kv = kv_ref[...].reshape(-1, 2 * C)
    logits = lax.dot_general(
        queries[...], kv, (((1,), (1,)), ((), ())), preferred_element_type=f32
    ) * (1.0 / math.sqrt(C // HEADS))
    top = jnp.max(logits, axis=1, keepdims=True)
    weight = jnp.exp(logits - top)
    total = jnp.sum(weight, axis=1, keepdims=True)
    coarse = weight.astype(bf16)
    fine = (weight - coarse.astype(f32)).astype(bf16)
    mixed = jnp.dot(coarse, kv, preferred_element_type=f32)
    mixed = mixed + jnp.dot(fine, kv, preferred_element_type=f32)
    mixed = mixed / total
    lane = lax.broadcasted_iota(jnp.int32, (BRICKS, 2 * C), 1)
    context = jnp.where(lane < C + C // 2, mixed[:BRICKS], mixed[BRICKS:])
    context = jnp.where(lane < C, 0.0, context)
    mean = jnp.sum(context * context, axis=1, keepdims=True) / C
    attended = (context / jnp.sqrt(mean + EPSILON)).astype(bf16)
    return jnp.dot(attended[:, C:], four(w_out), preferred_element_type=f32)


def first_kernel(
    masked, r0, r1, t0, t1, adj, band, scale, shift, cover, queries, kv, w_out,
    hidden, xs0, xs1, ys0, ys1, padded, acc,
):
    gather_neighbours(masked, (r0, r1), (t0, t1), adj, padded)
    convolve(padded, band, acc)
    term = attention(queries, kv, w_out)
    gain, offset = four(scale), four(shift)
    for k in range(16):
        lanes = slice(k * COL, (k + 1) * COL)
        first = jnp.maximum(acc[k * BRICKS : (k + 1) * BRICKS] * gain + offset, 0.0)
        hidden[:, lanes] = ((first + term) * cover[:, lanes].astype(f32)).astype(bf16)
    send_faces(hidden, xs0, xs1, ys0, ys1)


def second_kernel(
    hidden, r0, r1, t0, t1, adj, band, scale, shift, cover, masked, refined, padded, acc
):
    gather_neighbours(hidden, (r0, r1), (t0, t1), adj, padded)
    convolve(padded, band, acc)
    gain, offset = four(scale), four(shift)
    for k in range(16):
        lanes = slice(k * COL, (k + 1) * COL)
        value = acc[k * BRICKS : (k + 1) * BRICKS] * gain + offset
        value = jnp.maximum(value + masked[:, lanes].astype(f32), 0.0)
        refined[:, lanes] = (value * cover[:, lanes].astype(f32)).astype(bf16)


def exchange_x(xs0, xs1):
    return pair_exchange(xs0, "sx", 0), pair_exchange(xs1, "sx", 1)


def exchange_y(ys0, ys1, r0, r1):
    s0, s1 = call(
        corner_kernel, [shape(BRICKS, 6 * COL)] * 2, (ys0, ys1, r0, r1)
    )
    return pair_exchange(s0, "sy", 0), pair_exchange(s1, "sy", 1)


def local(
    features, occupancy, adjacency, conv_one, conv_two, scale_one, shift_one,
    scale_two, shift_two, w_query, w_key, w_value, w_out,
):
    n_sy = lax.axis_size("sy")
    whole, face = shape(BRICKS, 64 * C), shape(BRICKS, 4 * COL)
    band_shape = shape(9, 6 * C, COL)
    scratch = (
        pltpu.VMEM((6, 6, BRICKS, 6 * C), bf16),
        pltpu.VMEM((16 * BRICKS, COL), f32),
    )
    conv_cost = dict(flops=2 * 512 * 3456 * 256, bytes_accessed=4 << 20)
    masked, cover, queries, kv, xs0, xs1, ys0, ys1 = call(
        prepare_kernel,
        [whole, whole, shape(HEADS * BRICKS, 2 * C), shape(n_sy, BRICKS, 2 * C)] + [face] * 4,
        (features, occupancy, w_query, w_key, w_value),
        bytes_accessed=2 << 20,
    )
    r0, r1 = exchange_x(xs0, xs1)
    kv = lax.all_to_all(kv, "sy", 0, 0)
    t0, t1 = exchange_y(ys0, ys1, r0, r1)
    band_one = call(band_kernel, band_shape, (conv_one,), bytes_accessed=3 << 20)
    band_two = call(band_kernel, band_shape, (conv_two,), bytes_accessed=3 << 20)
    rows = [v.reshape(1, C) for v in (scale_one, shift_one, scale_two, shift_two)]
    hidden, xs0, xs1, ys0, ys1 = call(
        first_kernel,
        [whole] + [face] * 4,
        (masked, r0, r1, t0, t1, adjacency, band_one, rows[0], rows[1], cover, queries, kv, w_out),
        scratch,
        **conv_cost,
    )
    r0, r1 = exchange_x(xs0, xs1)
    t0, t1 = exchange_y(ys0, ys1, r0, r1)
    return call(
        second_kernel,
        whole,
        (hidden, r0, r1, t0, t1, adjacency, band_two, rows[2], rows[3], cover, masked),
        scratch,
        **conv_cost,
    )


def solution(mesh):
    split = P(("sx", "sy"), None)
    return jax.shard_map(
        local,
        mesh=mesh,
        in_specs=(split,) * 3 + (P(),) * 10,
        out_specs=split,
        check_vma=False,
    )
```

```python
import math

import jax
import jax.numpy as jnp
from jax import lax
from jax.experimental import pallas as pl
from jax.experimental.pallas import tpu as pltpu
from jax.sharding import PartitionSpec as P

HEADS = 2
C = 64
COL = 4 * C
BRICKS = 32
EPSILON = 1e-05
FAR = -(1 << 20)
VMEM_LIMIT = 16 * 1024 * 1024
f32, bf16 = jnp.float32, jnp.bfloat16


def call(kernel, out_shape, args, scratch=(), flops=0, bytes_accessed=0):
    vmem = pl.BlockSpec(memory_space=pltpu.VMEM)
    return pl.pallas_call(
        kernel,
        out_shape=out_shape,
        in_specs=[vmem] * len(args),
        out_specs=jax.tree.map(lambda _: vmem, out_shape),
        scratch_shapes=list(scratch),
        compiler_params=pltpu.CompilerParams(vmem_limit_bytes=VMEM_LIMIT),
        cost_estimate=pl.CostEstimate(
            flops=flops, bytes_accessed=bytes_accessed, transcendentals=0
        ),
    )(*args)


def shape(*dims, dtype=bf16):
    return jax.ShapeDtypeStruct(dims, dtype)


def column(x, y):
    return slice((x * 4 + y) * COL, (x * 4 + y + 1) * COL)


def face_x(ref, x):
    return ref[:, x * 4 * COL : (x + 1) * 4 * COL]


def pick(flag, a, b):
    return jnp.where(flag, a, b)


def parities():
    even_x = lax.rem(lax.axis_index("sx"), 2) == 0
    even_y = lax.rem(lax.axis_index("sy"), 2) == 0
    return even_x, even_y


def pair_exchange(value, axis, phase):
    count = lax.axis_size(axis)
    if phase == 0:
        pairs = [(s, s ^ 1) for s in range(count)]
    else:
        pairs = [(s, (((s + 1) ^ 1) - 1) % count) for s in range(count)]
    return lax.ppermute(value, axis, pairs)


def device_base():
    return (lax.axis_index("sx") * lax.axis_size("sy") + lax.axis_index("sy")) * BRICKS


def id_step(dx, dy):
    return (dx * lax.axis_size("sy") + dy) * BRICKS


def one_hot(ids, offsets, bases):
    lane = lax.broadcasted_iota(jnp.int32, (BRICKS, 32 * len(bases)), 1)
    candidate = jnp.bitwise_and(lane, 31) + bases[0]
    for k in range(1, len(bases)):
        slot = lax.shift_right_logical(lane, 5) == k
        candidate = candidate + jnp.where(slot, bases[k] - bases[0], 0)
    rows = [
        (ids[:, o : o + 1] == candidate).astype(f32).astype(bf16)
        for o in ((ox + 1) * 9 + (oy + 1) * 3 + (oz + 1) for ox, oy, oz in offsets)
    ]
    return jnp.concatenate(rows, axis=0)


def put_column(select, parts, core, store):
    table = parts[0] if len(parts) == 1 else jnp.concatenate(parts, axis=0)
    got = jnp.dot(select, table, preferred_element_type=f32).astype(bf16)
    lane_low = lax.broadcasted_iota(jnp.int32, (BRICKS, 128), 1) < C
    ends = jnp.where(lane_low, got[:BRICKS, :128], got[BRICKS : 2 * BRICKS, 128:])
    store(got[2 * BRICKS :] if core is None else core, ends)


NEAR, BEHIND, META, Y_LANES = 0, 4 * COL, 8 * COL, 9 * COL


def prepare_kernel(feat, marks, masked, cover, tokens_all, meta, ids, s0, s1):
    occupied = marks[:, :C].astype(f32).astype(bf16)
    row = lax.broadcasted_iota(jnp.int32, (64, COL), 0)
    voxel = lax.shift_right_logical(lax.broadcasted_iota(jnp.int32, (64, COL), 1), 6)
    total = jnp.zeros((BRICKS, 128), f32)
    for k in range(16):
        lanes = slice(k * COL, (k + 1) * COL)
        spread = (row == voxel + 4 * k).astype(f32).astype(bf16)
        cov = jnp.dot(occupied, spread, preferred_element_type=f32).astype(bf16)
        part = feat[:, lanes] * cov
        cover[:, lanes] = cov
        masked[:, lanes] = part
        wide = part.astype(f32)
        total = total + wide[:, :128] + wide[:, 128:]
    summed = total[:, :C] + total[:, C:]
    tokens = (summed / 8.0).astype(bf16)
    half = BRICKS // 2
    packed = jnp.concatenate([tokens[:half], tokens[half:]], axis=1)
    tokens_all[...] = jnp.broadcast_to(packed[None], tokens_all.shape)
    number = marks[:, C : C + 27]
    ids[...] = jnp.where(number < 0, FAR, number)
    number = number + 1
    high = lax.shift_right_logical(number, 6).astype(f32).astype(bf16)
    low = jnp.bitwise_and(number, 63).astype(f32).astype(bf16)
    gap = jnp.zeros((BRICKS, C - 27), bf16)
    about = jnp.concatenate([high, gap, low, gap, occupied, tokens], axis=1)
    meta[...] = about
    _, even_y = parities()

    def write(out, near, behind):
        for place, y in ((NEAR, near), (BEHIND, behind)):
            for x in range(4):
                out[:, place + x * COL : place + (x + 1) * COL] = masked[:, column(x, y)]
        out[:, META:] = about

    @pl.when(even_y)
    def _():
        write(s0, 3, 2)
        write(s1, 0, 1)

    @pl.when(jnp.logical_not(even_y))
    def _():
        write(s0, 0, 1)
        write(s1, 3, 2)


def band_kernel(weight, band):
    zero = jnp.zeros((C, C), bf16)
    for t in range(9):
        for r, z_in in enumerate((0, 1, 2, 3, 4, -1)):
            blocks = []
            for z_out in range(4):
                tap = z_in - z_out + 1
                blocks.append(weight[t * 3 + tap] if 0 <= tap < 3 else zero)
            band[t, r * C : (r + 1) * C, :] = jnp.concatenate(blocks, axis=1)


def message_kernel(masked, t0, t1, x0, x1):
    even_x, even_y = parities()

    def write(out, x):
        out[:, : 4 * COL] = face_x(masked, x)
        place = 4 * COL
        for a, b in ((t1, t0), (t0, t1)):
            for plane in (NEAR, BEHIND):
                lanes = slice(plane + x * COL, plane + (x + 1) * COL)
                out[:, place : place + COL] = pick(even_y, a[:, lanes], b[:, lanes])
                place += COL

    @pl.when(even_x)
    def _():
        write(x0, 3)
        write(x1, 0)

    @pl.when(jnp.logical_not(even_x))
    def _():
        write(x0, 0)
        write(x1, 3)


def place_x(ox, x, whole):
    return {-1: 0, 0: 1 + x, 1: 5}[ox] if whole else {-1: 0, 0: x, 1: 1}[ox]


def gather_own(field, from_x, from_y, from_corner, ids, padded, x_offsets):
    whole = len(x_offsets) == 3
    base = device_base()
    for ox in x_offsets:
        for oy in (-1, 0, 1):
            sources = [(0, 0)]
            if ox:
                sources.append((ox, 0))
            if oy:
                sources.append((0, oy))
            if ox and oy:
                sources.append((ox, oy))
            centre = ox == 0 and oy == 0
            offsets = [(ox, oy, oz) for oz in ((1, -1) if centre else (1, -1, 0))]
            select = one_hot(ids, offsets, [base + id_step(dx, dy) for dx, dy in sources])
            for x in {-1: (3,), 0: range(4), 1: (0,)}[ox]:
                for y in {-1: (3,), 0: range(4), 1: (0,)}[oy]:
                    parts = [field[:, column(x, y)]]
                    if ox:
                        parts.append(from_x(ox, y))
                    if oy:
                        parts.append(from_y(oy, x))
                    if ox and oy:
                        parts.append(from_corner(ox, oy))
                    px = place_x(ox, x, whole)
                    py = {-1: 0, 0: 1 + y, 1: 5}[oy]

                    def store(core, ends, px=px, py=py):
                        padded[px, py, :, :COL] = core
                        padded[px, py, :, COL:] = ends

                    put_column(select, parts, parts[0] if centre else None, store)


def gather_side(field, from_x, from_message, side, ids, padded, x_offsets):
    here, there = device_base(), device_base() + id_step(0, side)
    mine = {-1: 0, 1: 3}[side]
    rows = slice(0, BRICKS) if side < 0 else slice(BRICKS, 2 * BRICKS)
    for ox in x_offsets:
        x_range = {-1: (3,), 0: range(4), 1: (0,)}[ox]
        outer = [here] if ox == 0 else [here, here + id_step(ox, 0)]
        inner = [there] if ox == 0 else [there, there + id_step(ox, 0)]
        offsets = [(ox, 0, oz) for oz in ((1, -1) if ox == 0 else (1, -1, 0))]
        select_inner = one_hot(ids, offsets, inner)
        select_outer = one_hot(ids, [(ox, -side, oz) for oz in (1, -1, 0)], outer)
        for x in x_range:
            px = place_x(ox, x, len(x_offsets) == 3)
            for place, py in ((BEHIND, 1 + side), (NEAR, 1), (None, 1 - side)):

                def store(core, ends, px=px, py=py):
                    padded[py, px, rows, :COL] = core
                    padded[py, px, rows, COL:] = ends

                if place is None:
                    parts = [field[:, column(x, mine)]]
                    if ox:
                        parts.append(from_x(ox, mine))
                    put_column(select_outer, parts, None, store)
                    continue
                parts = [from_message(side, place + x * COL)]
                if ox:
                    parts.append(from_x(ox, corner_place(side, place)))
                put_column(select_inner, parts, parts[0] if ox == 0 else None, store)


def corner_place(side, plane):
    return 4 + (0 if side < 0 else 2) + (0 if plane == NEAR else 1)


def window(padded, padded_side, i, j, x_range):
    rows = len(x_range)
    first = x_range[0] + i
    own = padded[first : first + rows, j : j + 4].reshape(rows * 4 * BRICKS, 6 * C)
    if padded_side is None:
        return own
    side = padded_side[j, first : first + rows].reshape(rows * 2 * BRICKS, 6 * C)
    return jnp.concatenate([own, side], axis=0)


def own_rows(x_range):
    return slice(x_range[0] * 4 * BRICKS, (x_range[0] + len(x_range)) * 4 * BRICKS)


def convolve(padded, band, acc, padded_side):
    for t in range(9):
        lhs = window(padded, padded_side, t // 3, t % 3, range(4))
        part = jnp.dot(lhs, band[t], preferred_element_type=f32)
        if t == 0:
            acc[...] = part
        else:
            acc[...] += part


def convolve_inner(padded, band, acc):
    for t in (3, 4, 5, 0, 1, 2, 6, 7, 8):
        i, j = t // 3, t % 3
        x_range = {0: range(1, 4), 1: range(4), 2: range(3)}[i]
        part = jnp.dot(
            window(padded, None, i - 1, j, x_range), band[t], preferred_element_type=f32
        )
        if t == 3:
            acc[...] = part
        else:
            acc[own_rows(x_range)] += part


def convolve_edges(padded, band, acc):
    for i, place, x in ((0, 0, 0), (2, 1, 3)):
        total = acc[own_rows(range(x, x + 1))]
        for j in range(3):
            lhs = window(padded, None, place, j, range(1))
            total = total + jnp.dot(lhs, band[i * 3 + j], preferred_element_type=f32)
        acc[own_rows(range(x, x + 1))] = total


def four(ref):
    return jnp.concatenate([ref[...]] * 4, axis=1)


def project(tokens, weight):
    return jnp.dot(tokens, weight, preferred_element_type=f32).astype(bf16)


def attention(tokens, packed, weights):
    group = jnp.concatenate([packed[:, :C], packed[:, C:]], axis=0)
    kv = project(group, weights[:, : 2 * C])
    queries = project(tokens, weights[:, 2 * C : 3 * C])
    rows = queries.shape[0]
    wide = jnp.concatenate([queries, jnp.zeros_like(queries)], axis=1).astype(f32)
    lane = lax.broadcasted_iota(jnp.int32, (rows, 2 * C), 1)
    per_head = [jnp.where(lax.shift_right_logical(lane, 5) == h, wide, 0.0) for h in range(HEADS)]
    wide = jnp.concatenate(per_head, axis=0).astype(bf16)
    logits = lax.dot_general(
        wide, kv, (((1,), (1,)), ((), ())), preferred_element_type=f32
    ) * (1.0 / math.sqrt(C // HEADS))
    top = jnp.max(logits, axis=1, keepdims=True)
    weight = jnp.exp(logits - top)
    total = jnp.sum(weight, axis=1, keepdims=True)
    coarse = weight.astype(bf16)
    fine = (weight - coarse.astype(f32)).astype(bf16)
    mixed = jnp.dot(coarse, kv, preferred_element_type=f32)
    mixed = mixed + jnp.dot(fine, kv, preferred_element_type=f32)
    mixed = mixed / total
    context = jnp.where(lane < C + C // 2, mixed[:rows], mixed[rows:])
    context = jnp.where(lane < C, 0.0, context)
    mean = jnp.sum(context * context, axis=1, keepdims=True) / C
    attended = (context / jnp.sqrt(mean + EPSILON)).astype(bf16)
    w_out = jnp.concatenate([weights[:, 3 * C :]] * 4, axis=1)
    return jnp.dot(attended[:, C:], w_out, preferred_element_type=f32)


def y_reader(t0, t1):
    _, even_y = parities()

    def from_y(oy, place, width=COL):
        lanes = slice(place, place + width)
        a, b = (t1, t0) if oy < 0 else (t0, t1)
        return pick(even_y, a[:, lanes], b[:, lanes])

    return from_y


def x_reader(r0, r1):
    even_x, _ = parities()

    def from_x(ox, k):
        lanes = slice(k * COL, (k + 1) * COL)
        a, b = (r1, r0) if ox < 0 else (r0, r1)
        return pick(even_x, a[:, lanes], b[:, lanes])

    return from_x


def side_ids(about):
    high, low = about[:, :C].astype(f32), about[:, C : 2 * C].astype(f32)
    number = (high * 64.0 + low).astype(jnp.int32) - 1
    return jnp.where(number < 0, FAR, number)


def attention_kernel(group, weights, term):
    count = group.shape[0]
    here = lax.axis_index("sy")
    tokens = []
    for step in (0, count - 1, 1):
        packed = group[lax.rem(here + step, count)]
        tokens += [packed[:, :C], packed[:, C:]]
    packed = group[...].reshape(-1, 2 * C)
    term[...] = attention(jnp.concatenate(tokens, axis=0), packed, weights)


def first_kernel(
    masked, r0, r1, t0, t1, ids, band, scale, shift, cover, term,
    hidden, low_side, high_side, xs0, xs1, padded, padded_side, acc,
):
    even_x, _ = parities()
    from_message, from_x = y_reader(t0, t1), x_reader(r0, r1)
    every = (-1, 0, 1)
    row = lax.broadcasted_iota(jnp.int32, (64, COL), 0)
    voxel = lax.shift_right_logical(lax.broadcasted_iota(jnp.int32, (64, COL), 1), 6)
    side_cover = []
    gather_own(
        masked,
        from_x,
        lambda oy, x: from_message(oy, NEAR + x * COL),
        lambda ox, oy: from_x(ox, corner_place(oy, NEAR)),
        ids[...],
        padded,
        every,
    )
    for side in (-1, 1):
        about = from_message(side, META)
        gather_side(masked, from_x, from_message, side, side_ids(about), padded_side, every)
        occupied = about[:, 2 * C : 3 * C]
        y = 3 if side < 0 else 0
        for x in range(4):
            spread = (row == voxel + (x * 16 + y * 4)).astype(f32).astype(bf16)
            side_cover.append(jnp.dot(occupied, spread, preferred_element_type=f32))
    convolve(padded, band, acc, padded_side)
    gain, offset = four(scale), four(shift)

    def finish(rows, which, cov):
        first = jnp.maximum(acc[rows : rows + BRICKS] * gain + offset, 0.0)
        added = first + term[which * BRICKS : (which + 1) * BRICKS]
        return (added * cov.astype(f32)).astype(bf16)

    for k in range(16):
        lanes = slice(k * COL, (k + 1) * COL)
        hidden[:, lanes] = finish(k * BRICKS, 0, cover[:, lanes])
    for x in range(4):
        lanes = slice(x * COL, (x + 1) * COL)
        for k, out in enumerate((low_side, high_side)):
            out[:, lanes] = finish((16 + 2 * x + k) * BRICKS, 1 + k, side_cover[4 * k + x])

    def edge(out, x):
        lanes = slice(x * COL, (x + 1) * COL)
        out[:, : 4 * COL] = face_x(hidden, x)
        out[:, 4 * COL : 5 * COL] = low_side[:, lanes]
        out[:, 5 * COL :] = high_side[:, lanes]

    @pl.when(even_x)
    def _():
        edge(xs0, 3)
        edge(xs1, 0)

    @pl.when(jnp.logical_not(even_x))
    def _():
        edge(xs0, 0)
        edge(xs1, 3)


def side_reader(low_side, high_side):
    return lambda oy, x: (low_side if oy < 0 else high_side)[:, x * COL : (x + 1) * COL]


def second_inner_kernel(hidden, low_side, high_side, ids, band, acc, padded):
    gather_own(
        hidden, None, side_reader(low_side, high_side), None, ids[...], padded, (0,)
    )
    convolve_inner(padded, band, acc)


def second_outer_kernel(
    hidden, low_side, high_side, r0, r1, ids, band, scale, shift, cover, masked, acc_in,
    refined, padded, acc,
):
    from_x = x_reader(r0, r1)
    gather_own(
        hidden,
        from_x,
        side_reader(low_side, high_side),
        lambda ox, oy: from_x(ox, 4 if oy < 0 else 5),
        ids[...],
        padded,
        (-1, 1),
    )
    acc[...] = acc_in[...]
    convolve_edges(padded, band, acc)
    gain, offset = four(scale), four(shift)
    for k in range(16):
        lanes = slice(k * COL, (k + 1) * COL)
        value = acc[k * BRICKS : (k + 1) * BRICKS] * gain + offset
        value = jnp.maximum(value + masked[:, lanes].astype(f32), 0.0)
        refined[:, lanes] = (value * cover[:, lanes].astype(f32)).astype(bf16)


def exchange(first, second, axis):
    return pair_exchange(first, axis, 0), pair_exchange(second, axis, 1)


def local(
    features, occupancy, adjacency, conv_one, conv_two, scale_one, shift_one,
    scale_two, shift_two, w_query, w_key, w_value, w_out,
):
    n_sy = lax.axis_size("sy")
    whole, face, edge = shape(BRICKS, 64 * C), shape(BRICKS, 4 * COL), shape(BRICKS, 6 * COL)
    band_shape = shape(9, 6 * C, COL)
    padded_whole = pltpu.VMEM((6, 6, BRICKS, 6 * C), bf16)
    padded_side = pltpu.VMEM((3, 6, 2 * BRICKS, 6 * C), bf16)
    padded_inner = pltpu.VMEM((4, 6, BRICKS, 6 * C), bf16)
    padded_outer = pltpu.VMEM((2, 6, BRICKS, 6 * C), bf16)
    own_acc, both_acc = pltpu.VMEM((16 * BRICKS, COL), f32), pltpu.VMEM((24 * BRICKS, COL), f32)
    conv_cost = dict(flops=2 * 768 * 3456 * 256, bytes_accessed=4 << 20)
    inner_cost = dict(flops=2 * 512 * 3456 * 256, bytes_accessed=3 << 20)
    outer_cost = dict(flops=2 * 256 * 1152 * 256, bytes_accessed=3 << 20)
    marks = jnp.concatenate([occupancy, adjacency], axis=1)
    message = shape(BRICKS, Y_LANES)
    masked, cover, tokens, meta, ids, s0, s1 = call(
        prepare_kernel,
        [
            whole, whole, shape(n_sy, BRICKS // 2, 2 * C), shape(BRICKS, 4 * C),
            shape(BRICKS, 27, dtype=jnp.int32), message, message,
        ],
        (features, marks),
        bytes_accessed=2 << 20,
    )
    band_one = call(band_kernel, band_shape, (conv_one,), bytes_accessed=3 << 20)
    rows = [v.reshape(1, C) for v in (scale_one, shift_one, scale_two, shift_two)]
    t0, t1 = exchange(s0, s1, "sy")
    group = lax.all_to_all(tokens, "sy", 0, 0)
    x_message = shape(BRICKS, 8 * COL)
    x0, x1 = call(
        message_kernel, [x_message] * 2, (masked, t0, t1), flops=1 << 35, bytes_accessed=1 << 20
    )
    r0, r1 = exchange(x0, x1, "sx")
    weights = jnp.concatenate([w_key, w_value, w_query, w_out], axis=1)
    term = call(
        attention_kernel,
        shape(3 * BRICKS, COL, dtype=f32),
        (group, weights),
        flops=1 << 35,
        bytes_accessed=1 << 20,
    )
    hidden, low_side, high_side, xs0, xs1 = call(
        first_kernel,
        [whole, face, face, edge, edge],
        (
            masked, r0, r1, t0, t1, ids, band_one, rows[0], rows[1], cover, term,
        ),
        [padded_whole, padded_side, both_acc],
        **conv_cost,
    )
    later, hidden = lax.optimization_barrier((conv_two, hidden))
    band_two = call(band_kernel, band_shape, (later,), bytes_accessed=3 << 20)
    r0, r1 = exchange(xs0, xs1, "sx")
    acc = call(
        second_inner_kernel,
        shape(16 * BRICKS, COL, dtype=f32),
        (hidden, low_side, high_side, ids, band_two),
        [padded_inner],
        **inner_cost,
    )
    return call(
        second_outer_kernel,
        whole,
        (
            hidden, low_side, high_side, r0, r1, ids, band_two, rows[2], rows[3], cover, masked,
            acc,
        ),
        [padded_outer, own_acc],
        **outer_cost,
    )


def solution(mesh):
    split = P(("sx", "sy"), None)
    return jax.shard_map(
        local,
        mesh=mesh,
        in_specs=(split,) * 3 + (P(),) * 10,
        out_specs=split,
        check_vma=False,
    )
```

```python
import math

import jax
import jax.numpy as jnp
from jax import lax
from jax.experimental import pallas as pl
from jax.experimental.pallas import tpu as pltpu
from jax.sharding import PartitionSpec as P

HEADS = 2
C = 64
COL = 4 * C
BRICKS = 32
EPSILON = 1e-05
FAR = -(1 << 20)
VMEM_LIMIT = 16 * 1024 * 1024
f32, bf16 = jnp.float32, jnp.bfloat16


def call(kernel, out_shape, args, scratch=(), flops=0, bytes_accessed=0):
    vmem = pl.BlockSpec(memory_space=pltpu.VMEM)
    return pl.pallas_call(
        kernel,
        out_shape=out_shape,
        in_specs=[vmem] * len(args),
        out_specs=jax.tree.map(lambda _: vmem, out_shape),
        scratch_shapes=list(scratch),
        compiler_params=pltpu.CompilerParams(vmem_limit_bytes=VMEM_LIMIT),
        cost_estimate=pl.CostEstimate(
            flops=flops, bytes_accessed=bytes_accessed, transcendentals=0
        ),
    )(*args)


def shape(*dims, dtype=bf16):
    return jax.ShapeDtypeStruct(dims, dtype)


def column(x, y):
    return slice((x * 4 + y) * COL, (x * 4 + y + 1) * COL)


def face_x(ref, x):
    return ref[:, x * 4 * COL : (x + 1) * 4 * COL]


def pick(flag, a, b):
    return jnp.where(flag, a, b)


def parities():
    even_x = lax.rem(lax.axis_index("sx"), 2) == 0
    even_y = lax.rem(lax.axis_index("sy"), 2) == 0
    return even_x, even_y


def pair_exchange(value, axis, phase):
    n_x, n_y = lax.axis_size("sx"), lax.axis_size("sy")

    def partner(x, y):
        s, count = (x, n_x) if axis == "sx" else (y, n_y)
        if phase == 1 and s in (0, count - 1):
            return (x, y ^ 1) if axis == "sx" else (x ^ 1, y)
        s = s ^ 1 if phase == 0 else ((s + 1) ^ 1) - 1
        return (s, y) if axis == "sx" else (x, s)

    pairs = []
    for x in range(n_x):
        for y in range(n_y):
            there = partner(x, y)
            pairs.append((x * n_y + y, there[0] * n_y + there[1]))
    return lax.ppermute(value, ("sx", "sy"), pairs)


def device_base():
    return (lax.axis_index("sx") * lax.axis_size("sy") + lax.axis_index("sy")) * BRICKS


def id_step(dx, dy):
    return (dx * lax.axis_size("sy") + dy) * BRICKS


def one_hot(ids, offsets, bases):
    lane = lax.broadcasted_iota(jnp.int32, (BRICKS, 32 * len(bases)), 1)
    candidate = jnp.bitwise_and(lane, 31) + bases[0]
    for k in range(1, len(bases)):
        slot = lax.shift_right_logical(lane, 5) == k
        candidate = candidate + jnp.where(slot, bases[k] - bases[0], 0)
    rows = [
        (ids[:, o : o + 1] == candidate).astype(f32).astype(bf16)
        for o in ((ox + 1) * 9 + (oy + 1) * 3 + (oz + 1) for ox, oy, oz in offsets)
    ]
    return jnp.concatenate(rows, axis=0)


def put_column(select, parts, core, store):
    table = parts[0] if len(parts) == 1 else jnp.concatenate(parts, axis=0)
    got = jnp.dot(select, table, preferred_element_type=f32).astype(bf16)
    lane_low = lax.broadcasted_iota(jnp.int32, (BRICKS, 128), 1) < C
    ends = jnp.where(lane_low, got[:BRICKS, :128], got[BRICKS : 2 * BRICKS, 128:])
    store(got[2 * BRICKS :] if core is None else core, ends)


NEAR, BEHIND, META, Y_LANES = 0, 4 * COL, 8 * COL, 9 * COL


def prepare_kernel(feat, marks, masked, cover, tokens_all, meta, ids, s0, s1):
    occupied = marks[:, :C].astype(f32).astype(bf16)
    row = lax.broadcasted_iota(jnp.int32, (64, COL), 0)
    voxel = lax.shift_right_logical(lax.broadcasted_iota(jnp.int32, (64, COL), 1), 6)
    total = jnp.zeros((BRICKS, 128), f32)
    for k in range(16):
        lanes = slice(k * COL, (k + 1) * COL)
        spread = (row == voxel + 4 * k).astype(f32).astype(bf16)
        cov = jnp.dot(occupied, spread, preferred_element_type=f32).astype(bf16)
        part = feat[:, lanes] * cov
        cover[:, lanes] = cov
        masked[:, lanes] = part
        wide = part.astype(f32)
        total = total + wide[:, :128] + wide[:, 128:]
    summed = total[:, :C] + total[:, C:]
    tokens = (summed / 8.0).astype(bf16)
    half = BRICKS // 2
    packed = jnp.concatenate([tokens[:half], tokens[half:]], axis=1)
    tokens_all[...] = jnp.broadcast_to(packed[None], tokens_all.shape)
    number = marks[:, C : C + 27]
    ids[...] = jnp.where(number < 0, FAR, number)
    number = number + 1
    high = lax.shift_right_logical(number, 6).astype(f32).astype(bf16)
    low = jnp.bitwise_and(number, 63).astype(f32).astype(bf16)
    gap = jnp.zeros((BRICKS, C - 27), bf16)
    about = jnp.concatenate([high, gap, low, gap, occupied, tokens], axis=1)
    meta[...] = about
    _, even_y = parities()

    def write(out, near, behind):
        for place, y in ((NEAR, near), (BEHIND, behind)):
            for x in range(4):
                out[:, place + x * COL : place + (x + 1) * COL] = masked[:, column(x, y)]
        out[:, META:] = about

    @pl.when(even_y)
    def _():
        write(s0, 3, 2)
        write(s1, 0, 1)

    @pl.when(jnp.logical_not(even_y))
    def _():
        write(s0, 0, 1)
        write(s1, 3, 2)


def fill_band(weight, band):
    zero = jnp.zeros((C, C), bf16)
    for t in range(9):
        for r, z_in in enumerate((0, 1, 2, 3, 4, -1)):
            blocks = []
            for z_out in range(4):
                tap = z_in - z_out + 1
                blocks.append(weight[t * 3 + tap] if 0 <= tap < 3 else zero)
            band[t, r * C : (r + 1) * C, :] = jnp.concatenate(blocks, axis=1)


def message_kernel(masked, t0, t1, x0, x1):
    even_x, even_y = parities()

    def write(out, x):
        out[:, : 4 * COL] = face_x(masked, x)
        place = 4 * COL
        for a, b in ((t1, t0), (t0, t1)):
            for plane in (NEAR, BEHIND):
                lanes = slice(plane + x * COL, plane + (x + 1) * COL)
                out[:, place : place + COL] = pick(even_y, a[:, lanes], b[:, lanes])
                place += COL

    @pl.when(even_x)
    def _():
        write(x0, 3)
        write(x1, 0)

    @pl.when(jnp.logical_not(even_x))
    def _():
        write(x0, 0)
        write(x1, 3)


def place_x(ox, x):
    return x if ox == 0 else (0 if ox < 0 else 1)


def sources_of(ox, oy):
    sources = [(0, 0)]
    if ox:
        sources.append((ox, 0))
    if oy:
        sources.append((0, oy))
    if ox and oy:
        sources.append((ox, oy))
    return sources


def own_select(ids, ox, oy):
    base = device_base()
    offsets = [(ox, oy, oz) for oz in ((1, -1) if ox == 0 and oy == 0 else (1, -1, 0))]
    return one_hot(ids, offsets, [base + id_step(dx, dy) for dx, dy in sources_of(ox, oy)])


def side_select(ids, side, ox):
    here, there = device_base(), device_base() + id_step(0, side)
    outer = [here] if ox == 0 else [here, here + id_step(ox, 0)]
    inner = [there] if ox == 0 else [there, there + id_step(ox, 0)]
    offsets = [(ox, 0, oz) for oz in ((1, -1) if ox == 0 else (1, -1, 0))]
    return (
        one_hot(ids, offsets, inner),
        one_hot(ids, [(ox, -side, oz) for oz in (1, -1, 0)], outer),
    )


def gather_own(own, from_x, from_y, from_corner, select_of, padded, x_offsets):
    for ox in x_offsets:
        for oy in (-1, 0, 1):
            centre = ox == 0 and oy == 0
            select = select_of(ox, oy)
            for x in {-1: (3,), 0: range(4), 1: (0,)}[ox]:
                for y in {-1: (3,), 0: range(4), 1: (0,)}[oy]:
                    parts = [own(x, y)]
                    if ox:
                        parts.append(from_x(ox, y))
                    if oy:
                        parts.append(from_y(oy, x))
                    if ox and oy:
                        parts.append(from_corner(ox, oy))
                    px = place_x(ox, x)
                    py = {-1: 0, 0: 1 + y, 1: 5}[oy]

                    def store(core, ends, px=px, py=py):
                        padded[px, py, :, :COL] = core
                        padded[px, py, :, COL:] = ends

                    put_column(select, parts, parts[0] if centre else None, store)


def gather_side(own, from_x, from_message, side, select_of, padded, x_offsets):
    mine = {-1: 0, 1: 3}[side]
    rows = slice(0, BRICKS) if side < 0 else slice(BRICKS, 2 * BRICKS)
    for ox in x_offsets:
        select_inner, select_outer = select_of(side, ox)
        for x in {-1: (3,), 0: range(4), 1: (0,)}[ox]:
            px = place_x(ox, x)
            for place, py in ((BEHIND, 1 + side), (NEAR, 1), (None, 1 - side)):

                def store(core, ends, px=px, py=py):
                    padded[px, py, rows, :COL] = core
                    padded[px, py, rows, COL:] = ends

                if place is None:
                    parts = [own(x, mine)]
                    if ox:
                        parts.append(from_x(ox, mine))
                    put_column(select_outer, parts, None, store)
                    continue
                parts = [from_message(side, place + x * COL)]
                if ox:
                    parts.append(from_x(ox, corner_place(side, place)))
                put_column(select_inner, parts, parts[0] if ox == 0 else None, store)


def corner_place(side, plane):
    return 4 + (0 if side < 0 else 2) + (0 if plane == NEAR else 1)


TAP = 6 * C


def taps(padded, side, x_range, first, count):
    parts = []
    for t in range(first, first + count):
        i, j = t // 3, t % 3
        rows = [padded[x + i, j : j + 4].reshape(4 * BRICKS, TAP) for x in x_range]
        if side is not None:
            rows += [side[x + i, j] for x in x_range]
        parts.append(jnp.concatenate(rows, axis=0))
    return jnp.concatenate(parts, axis=1)


def product(lhs, band, first, count):
    rhs = band[first : first + count].reshape(count * TAP, COL)
    return jnp.dot(lhs, rhs, preferred_element_type=f32)


def convolve_inner(inner, side, band, store):
    store((1, 2), product(taps(inner, side, (0, 1), 0, 9), band, 0, 9))
    store((0,), product(taps(inner, side, (-1,), 3, 6), band, 3, 6))
    store((3,), product(taps(inner, side, (2,), 0, 6), band, 0, 6))


def convolve_edge(outer, side, band, x):
    i, place = (0, 0) if x == 0 else (2, 1)
    return product(taps(outer, side, (place - i,), 3 * i, 3), band, 0 if x == 0 else 3, 3)


def four(ref):
    return jnp.concatenate([ref[...]] * 4, axis=1)


def project(tokens, weight):
    return jnp.dot(tokens, weight, preferred_element_type=f32).astype(bf16)


def attention(tokens, packed, w_key, w_value, w_query, w_out):
    group = jnp.concatenate([packed[:, :C], packed[:, C:]], axis=0)
    kv = project(group, jnp.concatenate([w_key, w_value], axis=1))
    queries = project(tokens, w_query)
    rows = queries.shape[0]
    wide = jnp.concatenate([queries, jnp.zeros_like(queries)], axis=1).astype(f32)
    lane = lax.broadcasted_iota(jnp.int32, (rows, 2 * C), 1)
    per_head = [jnp.where(lax.shift_right_logical(lane, 5) == h, wide, 0.0) for h in range(HEADS)]
    wide = jnp.concatenate(per_head, axis=0).astype(bf16)
    logits = lax.dot_general(
        wide, kv, (((1,), (1,)), ((), ())), preferred_element_type=f32
    ) * (1.0 / math.sqrt(C // HEADS))
    top = jnp.max(logits, axis=1, keepdims=True)
    weight = jnp.exp(logits - top)
    total = jnp.sum(weight, axis=1, keepdims=True)
    coarse = weight.astype(bf16)
    fine = (weight - coarse.astype(f32)).astype(bf16)
    mixed = jnp.dot(coarse, kv, preferred_element_type=f32)
    mixed = mixed + jnp.dot(fine, kv, preferred_element_type=f32)
    mixed = mixed / total
    context = jnp.where(lane < C + C // 2, mixed[:rows], mixed[rows:])
    context = jnp.where(lane < C, 0.0, context)
    mean = jnp.sum(context * context, axis=1, keepdims=True) / C
    attended = (context / jnp.sqrt(mean + EPSILON)).astype(bf16)
    w_out = jnp.concatenate([w_out] * 4, axis=1)
    return jnp.dot(attended[:, C:], w_out, preferred_element_type=f32)


def y_reader(t0, t1):
    _, even_y = parities()

    def from_y(oy, place, width=COL):
        lanes = slice(place, place + width)
        a, b = (t1, t0) if oy < 0 else (t0, t1)
        return pick(even_y, a[:, lanes], b[:, lanes])

    return from_y


def x_reader(r0, r1):
    even_x, _ = parities()

    def from_x(ox, k):
        lanes = slice(k * COL, (k + 1) * COL)
        a, b = (r1, r0) if ox < 0 else (r0, r1)
        return pick(even_x, a[:, lanes], b[:, lanes])

    return from_x


def side_ids(about):
    high, low = about[:, :C].astype(f32), about[:, C : 2 * C].astype(f32)
    number = (high * 64.0 + low).astype(jnp.int32) - 1
    return jnp.where(number < 0, FAR, number)


def attention_kernel(group, w_key, w_value, w_query, w_out, term):
    count = group.shape[0]
    here = lax.axis_index("sy")
    tokens = []
    for step in (0, count - 1, 1):
        packed = group[lax.rem(here + step, count)]
        tokens += [packed[:, :C], packed[:, C:]]
    packed = group[...].reshape(-1, 2 * C)
    tokens = jnp.concatenate(tokens, axis=0)
    term[...] = attention(tokens, packed, w_key[...], w_value[...], w_query[...], w_out[...])


def near_kernel(
    masked, t0, t1, ids_ref, weight, acc, acc_side, band_edge, inner, side_inner, band
):
    from_message = y_reader(t0, t1)
    ids = ids_ref[...]

    def own(x, y):
        return masked[:, column(x, y)]

    def from_y(oy, x):
        return from_message(oy, NEAR + x * COL)

    fill_band(weight, band)
    gather_own(own, None, from_y, None, lambda ox, oy: own_select(ids, ox, oy), inner, (0,))
    for side in (-1, 1):
        number = side_ids(from_message(side, META))
        gather_side(
            own, None, from_message, side,
            lambda side, ox, number=number: side_select(number, side, ox), side_inner, (0,),
        )

    def store(x_range, value):
        count = len(x_range)
        for n, x in enumerate(x_range):
            acc[x] = value[n * 4 * BRICKS : (n + 1) * 4 * BRICKS]
            rows = (4 * count + 2 * n) * BRICKS
            acc_side[x] = value[rows : rows + 2 * BRICKS]

    convolve_inner(inner, side_inner, band, store)
    band_edge[:3] = band[:3]
    band_edge[3:] = band[6:]


def finish(acc, acc_side, x, gain, offset, cover, from_message, term, store, store_side):
    def one(part, which, cov):
        first = jnp.maximum(part * gain + offset, 0.0)
        return ((first + term[which * BRICKS : (which + 1) * BRICKS]) * cov).astype(bf16)

    row = lax.broadcasted_iota(jnp.int32, (64, COL), 0)
    voxel = lax.shift_right_logical(lax.broadcasted_iota(jnp.int32, (64, COL), 1), 6)
    for y in range(4):
        cov = cover[:, column(x, y)].astype(f32)
        store(x, y, one(acc[y * BRICKS : (y + 1) * BRICKS], 0, cov))
    for k, side in enumerate((-1, 1)):
        occupied = from_message(side, META)[:, 2 * C : 3 * C]
        spread = (row == voxel + (x * 16 + (3 - 3 * k) * 4)).astype(f32).astype(bf16)
        cov = jnp.dot(occupied, spread, preferred_element_type=f32)
        store_side(x, side, one(acc_side[k * BRICKS : (k + 1) * BRICKS], 1 + k, cov))


def first_edge_kernel(
    masked, r0, r1, t0, t1, ids_ref, band_edge, scale, shift, cover, term, acc, acc_side,
    xs0, xs1, outer, side_outer,
):
    even_x, _ = parities()
    from_message, from_x = y_reader(t0, t1), x_reader(r0, r1)
    ids = ids_ref[...]

    def own(x, y):
        return masked[:, column(x, y)]

    gather_own(
        own,
        from_x,
        lambda oy, x: from_message(oy, NEAR + x * COL),
        lambda ox, oy: from_x(ox, corner_place(oy, NEAR)),
        lambda ox, oy: own_select(ids, ox, oy),
        outer,
        (-1, 1),
    )
    for side in (-1, 1):
        number = side_ids(from_message(side, META))
        gather_side(
            own, from_x, from_message, side,
            lambda side, ox, number=number: side_select(number, side, ox), side_outer, (-1, 1),
        )

    def put(x, k, value):
        lanes = slice(k * COL, (k + 1) * COL)

        @pl.when(even_x == (x == 3))
        def _():
            xs0[:, lanes] = value

        @pl.when(even_x != (x == 3))
        def _():
            xs1[:, lanes] = value

    for x in (0, 3):
        more = convolve_edge(outer, side_outer, band_edge, x)
        finish(
            acc[x] + more[: 4 * BRICKS], acc_side[x] + more[4 * BRICKS :], x, four(scale),
            four(shift), cover, from_message, term,
            put, lambda x, side, value: put(x, 4 if side < 0 else 5, value),
        )


def edge_reader(xs0, xs1):
    even_x, _ = parities()

    def edge(x, k):
        lanes = slice(k * COL, (k + 1) * COL)
        a, b = (xs0, xs1) if x == 3 else (xs1, xs0)
        return pick(even_x, a[:, lanes], b[:, lanes])

    return edge


def middle_kernel(
    acc, acc_side, scale, shift, cover, t0, t1, term, xs0, xs1, ids_ref, weight,
    acc_out, band_edge, mid, mid_side, padded, band,
):
    edge = edge_reader(xs0, xs1)
    from_message = y_reader(t0, t1)
    ids = ids_ref[...]
    fill_band(weight, band)
    band_edge[:3] = band[:3]
    band_edge[3:] = band[6:]

    def put(x, y, value):
        mid[x - 1, y] = value

    def put_side(x, side, value):
        mid_side[x - 1, 0 if side < 0 else 1] = value

    for x in (1, 2):
        finish(
            acc[x], acc_side[x], x, four(scale), four(shift), cover, from_message, term,
            put, put_side,
        )

    def own(x, y):
        return mid[x - 1, y] if x in (1, 2) else edge(x, y)

    def from_y(oy, x):
        k = 0 if oy < 0 else 1
        return mid_side[x - 1, k] if x in (1, 2) else edge(x, 4 + k)

    gather_own(own, None, from_y, None, lambda ox, oy: own_select(ids, ox, oy), padded, (0,))

    def store(x_range, value):
        for n, x in enumerate(x_range):
            acc_out[x] = value[n * 4 * BRICKS : (n + 1) * 4 * BRICKS]

    convolve_inner(padded, None, band, store)


def second_kernel(
    xs0, xs1, r0, r1, ids_ref, band_edge, scale, shift, cover, masked, acc, refined, outer
):
    edge, from_x = edge_reader(xs0, xs1), x_reader(r0, r1)
    ids = ids_ref[...]
    gather_own(
        edge,
        from_x,
        lambda oy, x: edge(x, 4 if oy < 0 else 5),
        lambda ox, oy: from_x(ox, 4 if oy < 0 else 5),
        lambda ox, oy: own_select(ids, ox, oy),
        outer,
        (-1, 1),
    )
    gain, offset = four(scale), four(shift)
    for x in (1, 2, 0, 3):
        total = acc[x]
        if x in (0, 3):
            total = total + convolve_edge(outer, None, band_edge, x)
        for y in range(4):
            lanes = column(x, y)
            value = total[y * BRICKS : (y + 1) * BRICKS] * gain + offset
            value = jnp.maximum(value + masked[:, lanes].astype(f32), 0.0)
            refined[:, lanes] = (value * cover[:, lanes].astype(f32)).astype(bf16)


def exchange(first, second, axis):
    return pair_exchange(first, axis, 0), pair_exchange(second, axis, 1)


def local(
    features, occupancy, adjacency, conv_one, conv_two, scale_one, shift_one,
    scale_two, shift_two, w_query, w_key, w_value, w_out,
):
    n_sy = lax.axis_size("sy")
    whole, edge = shape(BRICKS, 64 * C), shape(BRICKS, 6 * COL)
    band_edge = shape(6, TAP, COL)
    own_acc, side_acc = shape(4, 4 * BRICKS, COL, dtype=f32), shape(4, 2 * BRICKS, COL, dtype=f32)
    band = pltpu.VMEM((9, TAP, COL), bf16)
    inner = pltpu.VMEM((4, 6, BRICKS, TAP), bf16)
    outer = pltpu.VMEM((2, 6, BRICKS, TAP), bf16)
    side_inner = pltpu.VMEM((4, 3, 2 * BRICKS, TAP), bf16)
    side_outer = pltpu.VMEM((2, 3, 2 * BRICKS, TAP), bf16)
    marks = jnp.concatenate([occupancy, adjacency], axis=1)
    message = shape(BRICKS, Y_LANES)
    masked, cover, tokens, meta, ids, s0, s1 = call(
        prepare_kernel,
        [
            whole, whole, shape(n_sy, BRICKS // 2, 2 * C), shape(BRICKS, 4 * C),
            shape(BRICKS, 27, dtype=jnp.int32), message, message,
        ],
        (features, marks),
        bytes_accessed=2 << 20,
    )
    rows = [v.reshape(1, C) for v in (scale_one, shift_one, scale_two, shift_two)]
    t0, t1 = exchange(s0, s1, "sy")
    group = lax.all_to_all(tokens, "sy", 0, 0)
    x_message = shape(BRICKS, 8 * COL)
    x0, x1 = call(
        message_kernel, [x_message] * 2, (masked, t0, t1), flops=1 << 35, bytes_accessed=1 << 20
    )
    r0, r1 = exchange(x0, x1, "sx")
    acc, acc_side, band_one = call(
        near_kernel,
        [own_acc, side_acc, band_edge],
        (masked, t0, t1, ids, conv_one),
        [inner, side_inner, band],
        flops=1 << 31,
        bytes_accessed=2 << 20,
    )
    group, acc = lax.optimization_barrier((group, acc))
    term = call(
        attention_kernel,
        shape(3 * BRICKS, COL, dtype=f32),
        (group, w_key, w_value, w_query, w_out),
        flops=1 << 26,
        bytes_accessed=1 << 20,
    )
    xs0, xs1 = call(
        first_edge_kernel,
        [edge, edge],
        (
            masked, r0, r1, t0, t1, ids, band_one, rows[0], rows[1], cover, term, acc, acc_side,
        ),
        [outer, side_outer],
        flops=2 * 384 * 3456 * 256,
        bytes_accessed=4 << 20,
    )
    r0, r1 = exchange(xs0, xs1, "sx")
    acc, band_two = call(
        middle_kernel,
        [own_acc, band_edge],
        (
            acc, acc_side, rows[0], rows[1], cover, t0, t1, term, xs0, xs1, ids, conv_two,
        ),
        [
            pltpu.VMEM((2, 4, BRICKS, COL), bf16),
            pltpu.VMEM((2, 2, BRICKS, COL), bf16),
            inner,
            band,
        ],
        flops=1 << 33,
        bytes_accessed=4 << 20,
    )
    return call(
        second_kernel,
        whole,
        (xs0, xs1, r0, r1, ids, band_two, rows[2], rows[3], cover, masked, acc),
        [outer],
        flops=2 * 256 * 1152 * 256,
        bytes_accessed=3 << 20,
    )


def solution(mesh):
    split = P(("sx", "sy"), None)
    return jax.shard_map(
        local,
        mesh=mesh,
        in_specs=(split,) * 3 + (P(),) * 10,
        out_specs=split,
        check_vma=False,
    )
```

```python
import math

import jax
import jax.numpy as jnp
from jax import lax
from jax.experimental import pallas as pl
from jax.experimental.pallas import tpu as pltpu
from jax.sharding import PartitionSpec as P

HEADS = 2
C = 64
COL = 4 * C
BRICKS = 32
EPSILON = 1e-05
FAR = -(1 << 20)
VMEM_LIMIT = 16 * 1024 * 1024
f32, bf16 = jnp.float32, jnp.bfloat16


def call(kernel, out_shape, args, scratch=(), flops=0, bytes_accessed=0):
    vmem = pl.BlockSpec(memory_space=pltpu.VMEM)
    return pl.pallas_call(
        kernel,
        out_shape=out_shape,
        in_specs=[vmem] * len(args),
        out_specs=jax.tree.map(lambda _: vmem, out_shape),
        scratch_shapes=list(scratch),
        compiler_params=pltpu.CompilerParams(vmem_limit_bytes=VMEM_LIMIT),
        cost_estimate=pl.CostEstimate(
            flops=flops, bytes_accessed=bytes_accessed, transcendentals=0
        ),
    )(*args)


def shape(*dims, dtype=bf16):
    return jax.ShapeDtypeStruct(dims, dtype)


def column(x, y):
    return slice((x * 4 + y) * COL, (x * 4 + y + 1) * COL)


def face_x(ref, x):
    return ref[:, x * 4 * COL : (x + 1) * 4 * COL]


def pick(flag, a, b):
    return jnp.where(flag, a, b)


def parities():
    even_x = lax.rem(lax.axis_index("sx"), 2) == 0
    even_y = lax.rem(lax.axis_index("sy"), 2) == 0
    return even_x, even_y


def pair_exchange(value, axis, phase):
    n_x, n_y = lax.axis_size("sx"), lax.axis_size("sy")

    def partner(x, y):
        s, count = (x, n_x) if axis == "sx" else (y, n_y)
        if phase == 1 and s in (0, count - 1):
            return (x, y ^ 1) if axis == "sx" else (x ^ 1, y)
        s = s ^ 1 if phase == 0 else ((s + 1) ^ 1) - 1
        return (s, y) if axis == "sx" else (x, s)

    pairs = []
    for x in range(n_x):
        for y in range(n_y):
            there = partner(x, y)
            pairs.append((x * n_y + y, there[0] * n_y + there[1]))
    return lax.ppermute(value, ("sx", "sy"), pairs)


def device_base():
    return (lax.axis_index("sx") * lax.axis_size("sy") + lax.axis_index("sy")) * BRICKS


def id_step(dx, dy):
    return (dx * lax.axis_size("sy") + dy) * BRICKS


def device_row(base):
    return jnp.bitwise_and(lax.broadcasted_iota(jnp.int32, (1, BRICKS), 1), BRICKS - 1) + base


def one_hot(ids, offsets, candidates):
    candidate = candidates[0]
    if len(candidates) > 1:
        candidate = jnp.concatenate(candidates, axis=1)
    candidate = jnp.broadcast_to(candidate, (BRICKS, candidate.shape[1]))
    rows = [
        (ids[:, o : o + 1] == candidate).astype(f32).astype(bf16)
        for o in ((ox + 1) * 9 + (oy + 1) * 3 + (oz + 1) for ox, oy, oz in offsets)
    ]
    return jnp.concatenate(rows, axis=0)


def owner_marks(ids, base):
    hit = jnp.logical_and(ids >= base, ids < base + BRICKS)
    return jnp.max(hit.astype(f32), axis=1, keepdims=True)


def compaction(marks, slots):
    row = lax.broadcasted_iota(jnp.int32, (BRICKS, BRICKS), 0)
    lane = lax.broadcasted_iota(jnp.int32, (BRICKS, BRICKS), 1)
    rank = jnp.sum(jnp.where(row < lane, marks, 0.0), axis=0, keepdims=True)
    marked = jnp.sum(jnp.where(row == lane, marks, 0.0), axis=0, keepdims=True)
    slot = lax.broadcasted_iota(jnp.int32, (slots, BRICKS), 0).astype(f32)
    return jnp.where(slot == rank, marked, 0.0)


def slot_ids(ids, base, offsets, slots):
    candidate = jnp.broadcast_to(device_row(base), (BRICKS, BRICKS))
    hit = jnp.zeros((BRICKS, BRICKS), f32)
    for ox, oy, oz in offsets:
        o = (ox + 1) * 9 + (oy + 1) * 3 + (oz + 1)
        hit = jnp.maximum(hit, (ids[:, o : o + 1] == candidate).astype(f32))
    marked = jnp.broadcast_to(jnp.max(hit, axis=0, keepdims=True), (8, BRICKS))
    row = lax.broadcasted_iota(jnp.int32, (BRICKS, BRICKS), 0)
    lane = lax.broadcasted_iota(jnp.int32, (BRICKS, BRICKS), 1)
    before = (row < lane).astype(f32).astype(bf16)
    rank = jnp.dot(marked.astype(bf16), before, preferred_element_type=f32)
    slot = lax.broadcasted_iota(jnp.int32, (slots, BRICKS), 0).astype(f32)
    pack = jnp.where(slot == rank[:1], marked[:1], 0.0).astype(bf16)
    count = lax.broadcasted_iota(jnp.int32, (8, BRICKS), 1).astype(f32) + 1.0
    local_id = lax.dot_general(
        count.astype(bf16), pack, (((1,), (1,)), ((), ())), preferred_element_type=f32
    ).astype(jnp.int32)
    return jnp.where(local_id > 0, local_id - 1 + base, 2 * FAR)


def put_column(select, parts, core, store):
    table = parts[0] if len(parts) == 1 else jnp.concatenate(parts, axis=0)
    got = jnp.dot(select, table, preferred_element_type=f32).astype(bf16)
    lane_low = lax.broadcasted_iota(jnp.int32, (BRICKS, 128), 1) < C
    ends = jnp.where(lane_low, got[:BRICKS, :128], got[BRICKS : 2 * BRICKS, 128:])
    store(got[2 * BRICKS :] if core is None else core, ends)


NEAR, BEHIND, META, Y_LANES = 0, 4 * COL, 8 * COL, 9 * COL


def prepare_kernel(feat, marks, masked, cover, tokens_all, meta, ids, s0, s1):
    occupied = marks[:, :C].astype(f32).astype(bf16)
    row = lax.broadcasted_iota(jnp.int32, (64, COL), 0)
    voxel = lax.shift_right_logical(lax.broadcasted_iota(jnp.int32, (64, COL), 1), 6)
    total = jnp.zeros((BRICKS, 128), f32)
    for k in range(16):
        lanes = slice(k * COL, (k + 1) * COL)
        spread = (row == voxel + 4 * k).astype(f32).astype(bf16)
        cov = jnp.dot(occupied, spread, preferred_element_type=f32).astype(bf16)
        part = feat[:, lanes] * cov
        cover[:, lanes] = cov
        masked[:, lanes] = part
        wide = part.astype(f32)
        total = total + wide[:, :128] + wide[:, 128:]
    summed = total[:, :C] + total[:, C:]
    tokens = (summed / 8.0).astype(bf16)
    half = BRICKS // 2
    packed = jnp.concatenate([tokens[:half], tokens[half:]], axis=1)
    tokens_all[...] = jnp.broadcast_to(packed[None], tokens_all.shape)
    number = marks[:, C : C + 27]
    ids[...] = jnp.where(number < 0, FAR, number)
    number = number + 1
    high = lax.shift_right_logical(number, 6).astype(f32).astype(bf16)
    low = jnp.bitwise_and(number, 63).astype(f32).astype(bf16)
    gap = jnp.zeros((BRICKS, C - 27), bf16)
    about = jnp.concatenate([high, gap, low, gap, occupied, tokens], axis=1)
    meta[...] = about
    _, even_y = parities()

    def write(out, near, behind):
        for place, y in ((NEAR, near), (BEHIND, behind)):
            for x in range(4):
                out[:, place + x * COL : place + (x + 1) * COL] = masked[:, column(x, y)]
        out[:, META:] = about

    @pl.when(even_y)
    def _():
        write(s0, 3, 2)
        write(s1, 0, 1)

    @pl.when(jnp.logical_not(even_y))
    def _():
        write(s0, 0, 1)
        write(s1, 3, 2)


def fill_band(weight, band):
    zero = jnp.zeros((C, C), bf16)
    for t in range(9):
        for r, z_in in enumerate((0, 1, 2, 3, 4, -1)):
            blocks = []
            for z_out in range(4):
                tap = z_in - z_out + 1
                blocks.append(weight[t * 3 + tap] if 0 <= tap < 3 else zero)
            band[t, r * C : (r + 1) * C, :] = jnp.concatenate(blocks, axis=1)


def message_kernel(masked, t0, t1, x0, x1):
    even_x, even_y = parities()

    def write(out, x):
        out[:, : 4 * COL] = face_x(masked, x)
        place = 4 * COL
        for a, b in ((t1, t0), (t0, t1)):
            for plane in (NEAR, BEHIND):
                lanes = slice(plane + x * COL, plane + (x + 1) * COL)
                out[:, place : place + COL] = pick(even_y, a[:, lanes], b[:, lanes])
                place += COL

    @pl.when(even_x)
    def _():
        write(x0, 3)
        write(x1, 0)

    @pl.when(jnp.logical_not(even_x))
    def _():
        write(x0, 0)
        write(x1, 3)


def place_x(ox, x):
    return x if ox == 0 else (0 if ox < 0 else 1)


def sources_of(ox, oy):
    sources = [(0, 0)]
    if ox:
        sources.append((ox, 0))
    if oy:
        sources.append((0, oy))
    if ox and oy:
        sources.append((ox, oy))
    return sources


def own_select(ids, ox, oy):
    base = device_base()
    offsets = [(ox, oy, oz) for oz in ((1, -1) if ox == 0 and oy == 0 else (1, -1, 0))]
    return one_hot(ids, offsets, [device_row(base + id_step(dx, dy)) for dx, dy in sources_of(ox, oy)])


def side_select(ids, side, ox):
    here, there = device_base(), device_base() + id_step(0, side)
    bases = [0] if ox == 0 else [0, id_step(ox, 0)]
    outer = [device_row(here + step) for step in bases]
    inner = [device_row(there + step) for step in bases]
    offsets = [(ox, 0, oz) for oz in ((1, -1) if ox == 0 else (1, -1, 0))]
    return (
        one_hot(ids, offsets, inner),
        one_hot(ids, [(ox, -side, oz) for oz in (1, -1, 0)], outer),
    )


def gather_own(own, from_x, from_y, from_corner, select_of, padded, x_offsets):
    for ox in x_offsets:
        for oy in (-1, 0, 1):
            centre = ox == 0 and oy == 0
            select = select_of(ox, oy)
            for x in {-1: (3,), 0: range(4), 1: (0,)}[ox]:
                for y in {-1: (3,), 0: range(4), 1: (0,)}[oy]:
                    parts = [own(x, y)]
                    if ox:
                        parts.append(from_x(ox, y))
                    if oy:
                        parts.append(from_y(oy, x))
                    if ox and oy:
                        parts.append(from_corner(ox, oy))
                    px = place_x(ox, x)
                    py = {-1: 0, 0: 1 + y, 1: 5}[oy]

                    def store(core, ends, px=px, py=py):
                        padded[px, py, :, :COL] = core
                        padded[px, py, :, COL:] = ends

                    put_column(select, parts, parts[0] if centre else None, store)


def gather_side(own, from_x, from_message, side, select_of, padded, x_offsets):
    mine = {-1: 0, 1: 3}[side]
    rows = slice(0, BRICKS) if side < 0 else slice(BRICKS, 2 * BRICKS)
    for ox in x_offsets:
        select_inner, select_outer = select_of(side, ox)
        for x in {-1: (3,), 0: range(4), 1: (0,)}[ox]:
            px = place_x(ox, x)
            for place, py in ((BEHIND, 1 + side), (NEAR, 1), (None, 1 - side)):

                def store(core, ends, px=px, py=py):
                    padded[px, py, rows, :COL] = core
                    padded[px, py, rows, COL:] = ends

                if place is None:
                    parts = [own(x, mine)]
                    if ox:
                        parts.append(from_x(ox, mine))
                    put_column(select_outer, parts, None, store)
                    continue
                parts = [from_message(side, place + x * COL)]
                if ox:
                    parts.append(from_x(ox, corner_place(side, place)))
                put_column(select_inner, parts, parts[0] if ox == 0 else None, store)


def corner_place(side, plane):
    return 4 + (0 if side < 0 else 2) + (0 if plane == NEAR else 1)


TAP = 6 * C


def taps(padded, side, x_range, first, count):
    parts = []
    for t in range(first, first + count):
        i, j = t // 3, t % 3
        rows = [padded[x + i, j : j + 4].reshape(4 * BRICKS, TAP) for x in x_range]
        if side is not None:
            rows += [side[x + i, j] for x in x_range]
        parts.append(jnp.concatenate(rows, axis=0))
    return jnp.concatenate(parts, axis=1)


def product(lhs, band, first, count):
    rhs = band[first : first + count].reshape(count * TAP, COL)
    return jnp.dot(lhs, rhs, preferred_element_type=f32)


def convolve_inner(inner, side, band, store):
    store((1, 2), product(taps(inner, side, (0, 1), 0, 9), band, 0, 9))
    store((0,), product(taps(inner, side, (-1,), 3, 6), band, 3, 6))
    store((3,), product(taps(inner, side, (2,), 0, 6), band, 0, 6))


def convolve_edge(outer, side, band, x):
    i, place = (0, 0) if x == 0 else (2, 1)
    return product(taps(outer, side, (place - i,), 3 * i, 3), band, 0 if x == 0 else 3, 3)


def four(ref):
    return jnp.concatenate([ref[...]] * 4, axis=1)


def project(tokens, weight):
    return jnp.dot(tokens, weight, preferred_element_type=f32).astype(bf16)


def attention(tokens, packed, w_key, w_value, w_query, w_out):
    group = jnp.concatenate([packed[:, :C], packed[:, C:]], axis=0)
    kv = project(group, jnp.concatenate([w_key, w_value], axis=1))
    queries = project(tokens, w_query)
    rows = queries.shape[0]
    wide = jnp.concatenate([queries, jnp.zeros_like(queries)], axis=1).astype(f32)
    lane = lax.broadcasted_iota(jnp.int32, (rows, 2 * C), 1)
    per_head = [jnp.where(lax.shift_right_logical(lane, 5) == h, wide, 0.0) for h in range(HEADS)]
    wide = jnp.concatenate(per_head, axis=0).astype(bf16)
    logits = lax.dot_general(
        wide, kv, (((1,), (1,)), ((), ())), preferred_element_type=f32
    ) * (1.0 / math.sqrt(C // HEADS))
    top = jnp.max(logits, axis=1, keepdims=True)
    weight = jnp.exp(logits - top)
    total = jnp.sum(weight, axis=1, keepdims=True)
    coarse = weight.astype(bf16)
    fine = (weight - coarse.astype(f32)).astype(bf16)
    mixed = jnp.dot(coarse, kv, preferred_element_type=f32)
    mixed = mixed + jnp.dot(fine, kv, preferred_element_type=f32)
    mixed = mixed / total
    context = jnp.where(lane < C + C // 2, mixed[:rows], mixed[rows:])
    context = jnp.where(lane < C, 0.0, context)
    mean = jnp.sum(context * context, axis=1, keepdims=True) / C
    attended = (context / jnp.sqrt(mean + EPSILON)).astype(bf16)
    w_out = jnp.concatenate([w_out] * 4, axis=1)
    return jnp.dot(attended[:, C:], w_out, preferred_element_type=f32)


def y_reader(t0, t1):
    _, even_y = parities()

    def from_y(oy, place, width=COL):
        lanes = slice(place, place + width)
        a, b = (t1, t0) if oy < 0 else (t0, t1)
        return pick(even_y, a[:, lanes], b[:, lanes])

    return from_y


def x_reader(r0, r1):
    even_x, _ = parities()

    def from_x(ox, k):
        lanes = slice(k * COL, (k + 1) * COL)
        a, b = (r1, r0) if ox < 0 else (r0, r1)
        return pick(even_x, a[:, lanes], b[:, lanes])

    return from_x


def side_ids(about):
    high, low = about[:, :C].astype(f32), about[:, C : 2 * C].astype(f32)
    number = (high * 64.0 + low).astype(jnp.int32) - 1
    return jnp.where(number < 0, FAR, number)


def global_term(group, w_key, w_value, w_query, w_out):
    count = group.shape[0]
    here = lax.axis_index("sy")
    tokens = []
    for step in (0, count - 1, 1):
        packed = group[lax.rem(here + step, count)]
        tokens += [packed[:, :C], packed[:, C:]]
    packed = group[...].reshape(-1, 2 * C)
    tokens = jnp.concatenate(tokens, axis=0)
    return attention(tokens, packed, w_key[...], w_value[...], w_query[...], w_out[...])


FACE_SLOTS, SIDE_SLOTS = 16, 8


def near_kernel(
    masked, t0, t1, ids_ref, weight, acc, acc_side, band_edge, pack, slots, inner, side_inner,
    band,
):
    from_message = y_reader(t0, t1)
    ids = ids_ref[...]

    def own(x, y):
        return masked[:, column(x, y)]

    def from_y(oy, x):
        return from_message(oy, NEAR + x * COL)

    fill_band(weight, band)
    gather_own(own, None, from_y, None, lambda ox, oy: own_select(ids, ox, oy), inner, (0,))
    numbers = {}
    for side in (-1, 1):
        number = numbers[side] = side_ids(from_message(side, META))
        gather_side(
            own, None, from_message, side,
            lambda side, ox, number=number: side_select(number, side, ox), side_inner, (0,),
        )

    base = device_base()
    for k, ox in enumerate((-1, 1)):
        face = [(ox, oy, oz) for oy in (-1, 0, 1) for oz in (-1, 0, 1)]
        parts = [slot_ids(ids, base + id_step(ox, 0), face, FACE_SLOTS)]
        for oy in (-1, 1):
            corner = [(ox, oy, oz) for oz in (-1, 0, 1)]
            parts.append(slot_ids(ids, base + id_step(ox, oy), corner, SIDE_SLOTS))
        slots[k, :, : FACE_SLOTS + 2 * SIDE_SLOTS] = jnp.concatenate(parts, axis=1)

    def store(x_range, value):
        count = len(x_range)
        for n, x in enumerate(x_range):
            acc[x] = value[n * 4 * BRICKS : (n + 1) * 4 * BRICKS]
            rows = (4 * count + 2 * n) * BRICKS
            acc_side[x] = value[rows : rows + 2 * BRICKS]

    convolve_inner(inner, side_inner, band, store)
    band_edge[:3] = band[:3]
    band_edge[3:] = band[6:]
    for k, ox in enumerate((-1, 1)):
        there = device_base() + id_step(ox, 0)
        pack[2 * k, :, :BRICKS] = compaction(owner_marks(ids, there), FACE_SLOTS).astype(bf16)
        sides = [compaction(owner_marks(numbers[side], there), SIDE_SLOTS) for side in (-1, 1)]
        gap = jnp.zeros_like(sides[0])
        low = jnp.concatenate([sides[0], gap], axis=1)
        high = jnp.concatenate([gap, sides[1]], axis=1)
        both = jnp.concatenate([low, high], axis=0)
        pack[2 * k + 1, :, : 2 * BRICKS] = both.astype(bf16)


def finish(acc, acc_side, x, gain, offset, cover, from_message, term, store, store_side):
    def one(part, which, cov):
        first = jnp.maximum(part * gain + offset, 0.0)
        return ((first + term[which * BRICKS : (which + 1) * BRICKS]) * cov).astype(bf16)

    row = lax.broadcasted_iota(jnp.int32, (64, COL), 0)
    voxel = lax.shift_right_logical(lax.broadcasted_iota(jnp.int32, (64, COL), 1), 6)
    for y in range(4):
        cov = cover[:, column(x, y)].astype(f32)
        store(x, y, one(acc[y * BRICKS : (y + 1) * BRICKS], 0, cov))
    for k, side in enumerate((-1, 1)):
        occupied = from_message(side, META)[:, 2 * C : 3 * C]
        spread = (row == voxel + (x * 16 + (3 - 3 * k) * 4)).astype(f32).astype(bf16)
        cov = jnp.dot(occupied, spread, preferred_element_type=f32)
        store_side(x, side, one(acc_side[k * BRICKS : (k + 1) * BRICKS], 1 + k, cov))


def first_edge_kernel(
    masked, r0, r1, t0, t1, ids_ref, band_edge, scale, shift, cover, acc, acc_side,
    group, w_key, w_value, w_query, w_out, pack, edges, m0, m1, term_out, outer, side_outer,
):
    even_x, _ = parities()
    from_message, from_x = y_reader(t0, t1), x_reader(r0, r1)
    ids = ids_ref[...]
    term = global_term(group, w_key, w_value, w_query, w_out)
    term_out[...] = term

    def own(x, y):
        return masked[:, column(x, y)]

    gather_own(
        own,
        from_x,
        lambda oy, x: from_message(oy, NEAR + x * COL),
        lambda ox, oy: from_x(ox, corner_place(oy, NEAR)),
        lambda ox, oy: own_select(ids, ox, oy),
        outer,
        (-1, 1),
    )
    for side in (-1, 1):
        number = side_ids(from_message(side, META))
        gather_side(
            own, from_x, from_message, side,
            lambda side, ox, number=number: side_select(number, side, ox), side_outer, (-1, 1),
        )

    def put(x, k, value):
        edges[0 if x == 0 else 1, :, k * COL : (k + 1) * COL] = value

    for x in (0, 3):
        more = convolve_edge(outer, side_outer, band_edge, x)
        finish(
            acc[x] + more[: 4 * BRICKS], acc_side[x] + more[4 * BRICKS :], x, four(scale),
            four(shift), cover, from_message, term,
            put, lambda x, side, value: put(x, 4 if side < 0 else 5, value),
        )
    messages = []
    for n in range(2):
        face = jnp.dot(
            pack[2 * n, :, :BRICKS], edges[n, :, : 4 * COL], preferred_element_type=f32
        )
        sides = jnp.concatenate(
            [edges[n, :, 4 * COL : 5 * COL], edges[n, :, 5 * COL :]], axis=0
        )
        side = jnp.dot(pack[2 * n + 1, :, : 2 * BRICKS], sides, preferred_element_type=f32)
        messages.append(jnp.concatenate([face, side], axis=1).astype(bf16))
    m0[...] = pick(even_x, messages[1], messages[0])
    m1[...] = pick(even_x, messages[0], messages[1])


def edge_reader(edges):
    return lambda x, k: edges[0 if x == 0 else 1, :, k * COL : (k + 1) * COL]


def middle_kernel(
    acc, acc_side, scale, shift, cover, t0, t1, term, edges, ids_ref, weight,
    acc_out, band_edge, mid, mid_side, padded, band,
):
    edge = edge_reader(edges)
    from_message = y_reader(t0, t1)
    ids = ids_ref[...]
    fill_band(weight, band)
    band_edge[:3] = band[:3]
    band_edge[3:] = band[6:]

    def put(x, y, value):
        mid[x - 1, y] = value

    def put_side(x, side, value):
        mid_side[x - 1, 0 if side < 0 else 1] = value

    for x in (1, 2):
        finish(
            acc[x], acc_side[x], x, four(scale), four(shift), cover, from_message, term,
            put, put_side,
        )

    def own(x, y):
        return mid[x - 1, y] if x in (1, 2) else edge(x, y)

    def from_y(oy, x):
        k = 0 if oy < 0 else 1
        return mid_side[x - 1, k] if x in (1, 2) else edge(x, 4 + k)

    gather_own(own, None, from_y, None, lambda ox, oy: own_select(ids, ox, oy), padded, (0,))

    def store(x_range, value):
        for n, x in enumerate(x_range):
            acc_out[x] = value[n * 4 * BRICKS : (n + 1) * 4 * BRICKS]

    convolve_inner(padded, None, band, store)


def second_kernel(
    edges, r0, r1, ids_ref, slots, band_edge, scale, shift, cover, masked, acc, refined, outer
):
    even_x, _ = parities()
    edge, ids = edge_reader(edges), ids_ref[...]
    base = device_base()

    def received(ox, rows, k):
        lanes = slice(k * COL, (k + 1) * COL)
        a, b = (r1, r0) if ox < 0 else (r0, r1)
        return pick(even_x, a[rows, lanes], b[rows, lanes])

    def from_corner(ox, oy):
        return received(ox, slice(None), 4)

    def select_of(ox, oy):
        known = slots[0 if ox < 0 else 1, :1, : FACE_SLOTS + 2 * SIDE_SLOTS]
        candidates = [device_row(base), known[:, :FACE_SLOTS]]
        if oy:
            candidates += [device_row(base + id_step(0, oy)), known[:, FACE_SLOTS:]]
        return one_hot(ids, [(ox, oy, oz) for oz in (1, -1, 0)], candidates)

    gather_own(
        edge,
        lambda ox, y: received(ox, slice(None), y),
        lambda oy, x: edge(x, 4 if oy < 0 else 5),
        from_corner,
        select_of,
        outer,
        (-1, 1),
    )
    gain, offset = four(scale), four(shift)
    for x in (1, 2, 0, 3):
        total = acc[x]
        if x in (0, 3):
            total = total + convolve_edge(outer, None, band_edge, x)
        for y in range(4):
            lanes = column(x, y)
            value = total[y * BRICKS : (y + 1) * BRICKS] * gain + offset
            value = jnp.maximum(value + masked[:, lanes].astype(f32), 0.0)
            refined[:, lanes] = (value * cover[:, lanes].astype(f32)).astype(bf16)


def exchange(first, second, axis):
    return pair_exchange(first, axis, 0), pair_exchange(second, axis, 1)


def local(
    features, occupancy, adjacency, conv_one, conv_two, scale_one, shift_one,
    scale_two, shift_two, w_query, w_key, w_value, w_out,
):
    n_sy = lax.axis_size("sy")
    whole = shape(BRICKS, 64 * C)
    band_edge = shape(6, TAP, COL)
    own_acc, side_acc = shape(4, 4 * BRICKS, COL, dtype=f32), shape(4, 2 * BRICKS, COL, dtype=f32)
    band = pltpu.VMEM((9, TAP, COL), bf16)
    inner = pltpu.VMEM((4, 6, BRICKS, TAP), bf16)
    outer = pltpu.VMEM((2, 6, BRICKS, TAP), bf16)
    side_inner = pltpu.VMEM((4, 3, 2 * BRICKS, TAP), bf16)
    side_outer = pltpu.VMEM((2, 3, 2 * BRICKS, TAP), bf16)
    marks = jnp.concatenate([occupancy, adjacency], axis=1)
    message = shape(BRICKS, Y_LANES)
    masked, cover, tokens, meta, ids, s0, s1 = call(
        prepare_kernel,
        [
            whole, whole, shape(n_sy, BRICKS // 2, 2 * C), shape(BRICKS, 4 * C),
            shape(BRICKS, 27, dtype=jnp.int32), message, message,
        ],
        (features, marks),
        bytes_accessed=2 << 20,
    )
    rows = [v.reshape(1, C) for v in (scale_one, shift_one, scale_two, shift_two)]
    t0, t1 = exchange(s0, s1, "sy")
    group = lax.all_to_all(tokens, "sy", 0, 0)
    x_message = shape(BRICKS, 8 * COL)
    x0, x1 = call(
        message_kernel, [x_message] * 2, (masked, t0, t1), flops=1 << 35, bytes_accessed=1 << 20
    )
    r0, r1 = exchange(x0, x1, "sx")
    acc, acc_side, band_one, pack, slots = call(
        near_kernel,
        [
            own_acc, side_acc, band_edge, shape(4, FACE_SLOTS, 128),
            shape(2, 8, 128, dtype=jnp.int32),
        ],
        (masked, t0, t1, ids, conv_one),
        [inner, side_inner, band],
        flops=1 << 33,
        bytes_accessed=2 << 20,
    )
    group, acc = lax.optimization_barrier((group, acc))
    out_message = shape(FACE_SLOTS, 5 * COL)
    edges, m0, m1, term = call(
        first_edge_kernel,
        [
            shape(2, BRICKS, 6 * COL), out_message, out_message,
            shape(3 * BRICKS, COL, dtype=f32),
        ],
        (
            masked, r0, r1, t0, t1, ids, band_one, rows[0], rows[1], cover, acc, acc_side,
            group, w_key, w_value, w_query, w_out, pack,
        ),
        [outer, side_outer],
        flops=2 * 384 * 3456 * 256,
        bytes_accessed=4 << 20,
    )
    r0, r1 = exchange(m0, m1, "sx")
    acc, band_two = call(
        middle_kernel,
        [own_acc, band_edge],
        (
            acc, acc_side, rows[0], rows[1], cover, t0, t1, term, edges, ids, conv_two,
        ),
        [
            pltpu.VMEM((2, 4, BRICKS, COL), bf16),
            pltpu.VMEM((2, 2, BRICKS, COL), bf16),
            inner,
            band,
        ],
        flops=1 << 33,
        bytes_accessed=4 << 20,
    )
    return call(
        second_kernel,
        whole,
        (
            edges, r0, r1, ids, slots, band_two, rows[2], rows[3], cover, masked, acc,
        ),
        [outer],
        flops=2 * 256 * 1152 * 256,
        bytes_accessed=3 << 20,
    )


def solution(mesh):
    split = P(("sx", "sy"), None)
    return jax.shard_map(
        local,
        mesh=mesh,
        in_specs=(split,) * 3 + (P(),) * 10,
        out_specs=split,
        check_vma=False,
    )
```

```python
import math

import jax
import jax.numpy as jnp
from jax import lax
from jax.experimental import pallas as pl
from jax.experimental.pallas import tpu as pltpu
from jax.sharding import PartitionSpec as P

HEADS = 2
C = 64
COL = 4 * C
BRICKS = 32
EPSILON = 1e-05
FAR = -(1 << 20)
VMEM_LIMIT = 16 * 1024 * 1024
f32, bf16 = jnp.float32, jnp.bfloat16


def call(kernel, out_shape, args, scratch=(), flops=0, bytes_accessed=0, hbm_out=False):
    vmem, hbm = pl.BlockSpec(memory_space=pltpu.VMEM), pl.BlockSpec(memory_space=pl.ANY)
    return pl.pallas_call(
        kernel,
        out_shape=out_shape,
        in_specs=[vmem] * len(args),
        out_specs=jax.tree.map(lambda _: hbm if hbm_out else vmem, out_shape),
        scratch_shapes=list(scratch),
        compiler_params=pltpu.CompilerParams(vmem_limit_bytes=VMEM_LIMIT),
        cost_estimate=pl.CostEstimate(
            flops=flops, bytes_accessed=bytes_accessed, transcendentals=0
        ),
    )(*args)


def shape(*dims, dtype=bf16):
    return jax.ShapeDtypeStruct(dims, dtype)


def column(x, y):
    return slice((x * 4 + y) * COL, (x * 4 + y + 1) * COL)


def face_x(ref, x):
    return ref[:, x * 4 * COL : (x + 1) * 4 * COL]


def pick(flag, a, b):
    return jnp.where(flag, a, b)


def parities():
    odd_x = lax.rem(lax.axis_index("sx"), 2) == 1
    odd_y = lax.rem(lax.axis_index("sy"), 2) == 1
    return odd_x, odd_y


def pair_exchange(value, axis, phase):
    n_x, n_y = lax.axis_size("sx"), lax.axis_size("sy")

    def partner(x, y):
        s, count = (x, n_x) if axis == "sx" else (y, n_y)
        if phase == 1 and s in (0, count - 1):
            return (x, y ^ 1) if axis == "sx" else (x ^ 1, y)
        s = s ^ 1 if phase == 0 else ((s + 1) ^ 1) - 1
        return (s, y) if axis == "sx" else (x, s)

    pairs = []
    for x in range(n_x):
        for y in range(n_y):
            there = partner(x, y)
            pairs.append((x * n_y + y, there[0] * n_y + there[1]))
    return lax.ppermute(value, ("sx", "sy"), pairs)


def device_base():
    return (lax.axis_index("sx") * lax.axis_size("sy") + lax.axis_index("sy")) * BRICKS


def id_step(dx, dy):
    return (dx * lax.axis_size("sy") + dy) * BRICKS


def device_row(base):
    return jnp.bitwise_and(lax.broadcasted_iota(jnp.int32, (1, BRICKS), 1), BRICKS - 1) + base


def one_hot(ids, offsets, candidates):
    candidate = candidates[0]
    if len(candidates) > 1:
        candidate = jnp.concatenate(candidates, axis=1)
    candidate = jnp.broadcast_to(candidate, (BRICKS, candidate.shape[1]))
    rows = [
        (ids[:, o : o + 1] == candidate).astype(f32).astype(bf16)
        for o in ((ox + 1) * 9 + (oy + 1) * 3 + (oz + 1) for ox, oy, oz in offsets)
    ]
    return jnp.concatenate(rows, axis=0)


def owner_marks(ids, base):
    hit = jnp.logical_and(ids >= base, ids < base + BRICKS)
    return jnp.max(hit.astype(f32), axis=1, keepdims=True)


def compaction(marks, slots):
    row = lax.broadcasted_iota(jnp.int32, (BRICKS, BRICKS), 0)
    lane = lax.broadcasted_iota(jnp.int32, (BRICKS, BRICKS), 1)
    rank = jnp.sum(jnp.where(row < lane, marks, 0.0), axis=0, keepdims=True)
    marked = jnp.sum(jnp.where(row == lane, marks, 0.0), axis=0, keepdims=True)
    slot = lax.broadcasted_iota(jnp.int32, (slots, BRICKS), 0).astype(f32)
    return jnp.where(slot == rank, marked, 0.0)


def slot_ids(ids, base, offsets, slots):
    candidate = jnp.broadcast_to(device_row(base), (BRICKS, BRICKS))
    hit = jnp.zeros((BRICKS, BRICKS), f32)
    for ox, oy, oz in offsets:
        o = (ox + 1) * 9 + (oy + 1) * 3 + (oz + 1)
        hit = jnp.maximum(hit, (ids[:, o : o + 1] == candidate).astype(f32))
    marked = jnp.broadcast_to(jnp.max(hit, axis=0, keepdims=True), (8, BRICKS))
    row = lax.broadcasted_iota(jnp.int32, (BRICKS, BRICKS), 0)
    lane = lax.broadcasted_iota(jnp.int32, (BRICKS, BRICKS), 1)
    before = (row < lane).astype(f32).astype(bf16)
    rank = jnp.dot(marked.astype(bf16), before, preferred_element_type=f32)
    slot = lax.broadcasted_iota(jnp.int32, (slots, BRICKS), 0).astype(f32)
    pack = jnp.where(slot == rank[:1], marked[:1], 0.0).astype(bf16)
    count = lax.broadcasted_iota(jnp.int32, (8, BRICKS), 1).astype(f32) + 1.0
    local_id = lax.dot_general(
        count.astype(bf16), pack, (((1,), (1,)), ((), ())), preferred_element_type=f32
    ).astype(jnp.int32)
    return jnp.where(local_id > 0, local_id - 1 + base, 2 * FAR)


def put_column(select, parts, core, store):
    table = parts[0] if len(parts) == 1 else jnp.concatenate(parts, axis=0)
    got = jnp.dot(select, table, preferred_element_type=f32).astype(bf16)
    lane_low = lax.broadcasted_iota(jnp.int32, (BRICKS, 128), 1) < C
    ends = jnp.where(lane_low, got[:BRICKS, :128], got[BRICKS : 2 * BRICKS, 128:])
    store(got[2 * BRICKS :] if core is None else core, ends)


NEAR, BEHIND, META, Y_LANES = 0, 4 * COL, 8 * COL, 9 * COL


def prepare_kernel(feat, marks, masked, cover, tokens_all, meta, ids, s0, s1):
    occupied = marks[:, :C].astype(f32).astype(bf16)
    row = lax.broadcasted_iota(jnp.int32, (64, COL), 0)
    voxel = lax.shift_right_logical(lax.broadcasted_iota(jnp.int32, (64, COL), 1), 6)
    total = jnp.zeros((BRICKS, 128), f32)
    for k in range(16):
        lanes = slice(k * COL, (k + 1) * COL)
        spread = (row == voxel + 4 * k).astype(f32).astype(bf16)
        cov = jnp.dot(occupied, spread, preferred_element_type=f32).astype(bf16)
        part = feat[:, lanes] * cov
        cover[:, lanes] = cov
        masked[:, lanes] = part
        wide = part.astype(f32)
        total = total + wide[:, :128] + wide[:, 128:]
    summed = total[:, :C] + total[:, C:]
    tokens = (summed / 8.0).astype(bf16)
    half = BRICKS // 2
    packed = jnp.concatenate([tokens[:half], tokens[half:]], axis=1)
    tokens_all[...] = jnp.broadcast_to(packed[None], tokens_all.shape)
    number = marks[:, C : C + 27]
    ids[...] = jnp.where(number < 0, FAR, number)
    number = number + 1
    high = lax.shift_right_logical(number, 6).astype(f32).astype(bf16)
    low = jnp.bitwise_and(number, 63).astype(f32).astype(bf16)
    gap = jnp.zeros((BRICKS, C - 27), bf16)
    about = jnp.concatenate([high, gap, low, gap, occupied, tokens], axis=1)
    meta[...] = about
    _, odd_y = parities()

    def write(out, near, behind):
        for place, y in ((NEAR, near), (BEHIND, behind)):
            for x in range(4):
                out[:, place + x * COL : place + (x + 1) * COL] = masked[:, column(x, y)]
        out[:, META:] = about

    @pl.when(odd_y)
    def _():
        write(s0, 3, 2)
        write(s1, 0, 1)

    @pl.when(jnp.logical_not(odd_y))
    def _():
        write(s0, 0, 1)
        write(s1, 3, 2)


def fill_band(weight, band):
    zero = jnp.zeros((C, C), bf16)
    for t in range(9):
        for r, z_in in enumerate((0, 1, 2, 3, 4, -1)):
            blocks = []
            for z_out in range(4):
                tap = z_in - z_out + 1
                blocks.append(weight[t * 3 + tap] if 0 <= tap < 3 else zero)
            band[t, r * C : (r + 1) * C, :] = jnp.concatenate(blocks, axis=1)


def message_kernel(masked, t0, t1, x0, x1):
    odd_x, odd_y = parities()

    def write(out, x):
        out[:, : 4 * COL] = face_x(masked, x)
        place = 4 * COL
        for a, b in ((t1, t0), (t0, t1)):
            for plane in (NEAR, BEHIND):
                lanes = slice(plane + x * COL, plane + (x + 1) * COL)
                out[:, place : place + COL] = pick(odd_y, a[:, lanes], b[:, lanes])
                place += COL

    @pl.when(odd_x)
    def _():
        write(x0, 3)
        write(x1, 0)

    @pl.when(jnp.logical_not(odd_x))
    def _():
        write(x0, 0)
        write(x1, 3)


def place_x(ox, x):
    return x if ox == 0 else (0 if ox < 0 else 1)


def sources_of(ox, oy):
    sources = [(0, 0)]
    if ox:
        sources.append((ox, 0))
    if oy:
        sources.append((0, oy))
    if ox and oy:
        sources.append((ox, oy))
    return sources


def own_select(ids, ox, oy):
    base = device_base()
    offsets = [(ox, oy, oz) for oz in ((1, -1) if ox == 0 and oy == 0 else (1, -1, 0))]
    return one_hot(ids, offsets, [device_row(base + id_step(dx, dy)) for dx, dy in sources_of(ox, oy)])


def side_select(ids, side, ox):
    here, there = device_base(), device_base() + id_step(0, side)
    bases = [0] if ox == 0 else [0, id_step(ox, 0)]
    outer = [device_row(here + step) for step in bases]
    inner = [device_row(there + step) for step in bases]
    offsets = [(ox, 0, oz) for oz in ((1, -1) if ox == 0 else (1, -1, 0))]
    return (
        one_hot(ids, offsets, inner),
        one_hot(ids, [(ox, -side, oz) for oz in (1, -1, 0)], outer),
    )


def gather_own(own, from_x, from_y, from_corner, select_of, padded, x_offsets):
    for ox in x_offsets:
        for oy in (-1, 0, 1):
            centre = ox == 0 and oy == 0
            select = select_of(ox, oy)
            for x in {-1: (3,), 0: range(4), 1: (0,)}[ox]:
                for y in {-1: (3,), 0: range(4), 1: (0,)}[oy]:
                    parts = [own(x, y)]
                    if ox:
                        parts.append(from_x(ox, y))
                    if oy:
                        parts.append(from_y(oy, x))
                    if ox and oy:
                        parts.append(from_corner(ox, oy))
                    px = place_x(ox, x)
                    py = {-1: 0, 0: 1 + y, 1: 5}[oy]

                    def store(core, ends, px=px, py=py):
                        padded[px, py, :, :COL] = core
                        padded[px, py, :, COL:] = ends

                    put_column(select, parts, parts[0] if centre else None, store)


def gather_side(own, from_x, from_message, side, select_of, padded, x_offsets):
    mine = {-1: 0, 1: 3}[side]
    rows = slice(0, BRICKS) if side < 0 else slice(BRICKS, 2 * BRICKS)
    for ox in x_offsets:
        select_inner, select_outer = select_of(side, ox)
        for x in {-1: (3,), 0: range(4), 1: (0,)}[ox]:
            px = place_x(ox, x)
            for place, py in ((BEHIND, 1 + side), (NEAR, 1), (None, 1 - side)):

                def store(core, ends, px=px, py=py):
                    padded[px, py, rows, :COL] = core
                    padded[px, py, rows, COL:] = ends

                if place is None:
                    parts = [own(x, mine)]
                    if ox:
                        parts.append(from_x(ox, mine))
                    put_column(select_outer, parts, None, store)
                    continue
                parts = [from_message(side, place + x * COL)]
                if ox:
                    parts.append(from_x(ox, corner_place(side, place)))
                put_column(select_inner, parts, parts[0] if ox == 0 else None, store)


def corner_place(side, plane):
    return 4 + (0 if side < 0 else 2) + (0 if plane == NEAR else 1)


TAP = 6 * C


def taps(padded, side, x_range, first, count):
    parts = []
    for t in range(first, first + count):
        i, j = t // 3, t % 3
        rows = [padded[x + i, j : j + 4].reshape(4 * BRICKS, TAP) for x in x_range]
        if side is not None:
            rows += [side[x + i, j] for x in x_range]
        parts.append(jnp.concatenate(rows, axis=0))
    return jnp.concatenate(parts, axis=1)


def product(lhs, band, first, count):
    rhs = band[first : first + count].reshape(count * TAP, COL)
    return jnp.dot(lhs, rhs, preferred_element_type=f32)


def convolve_inner(inner, side, band, store):
    store((1, 2), product(taps(inner, side, (0, 1), 0, 9), band, 0, 9))
    store((0,), product(taps(inner, side, (-1,), 3, 6), band, 3, 6))
    store((3,), product(taps(inner, side, (2,), 0, 6), band, 0, 6))


def convolve_edge(outer, side, band, x):
    i, place = (0, 0) if x == 0 else (2, 1)
    return product(taps(outer, side, (place - i,), 3 * i, 3), band, 0 if x == 0 else 3, 3)


def four(ref):
    return jnp.concatenate([ref[...]] * 4, axis=1)


def project(tokens, weight):
    return jnp.dot(tokens, weight, preferred_element_type=f32).astype(bf16)


def attention(tokens, packed, w_key, w_value, w_query, w_out):
    group = jnp.concatenate([packed[:, :C], packed[:, C:]], axis=0)
    kv = project(group, jnp.concatenate([w_key, w_value], axis=1))
    queries = project(tokens, w_query)
    rows = queries.shape[0]
    wide = jnp.concatenate([queries, jnp.zeros_like(queries)], axis=1).astype(f32)
    lane = lax.broadcasted_iota(jnp.int32, (rows, 2 * C), 1)
    per_head = [jnp.where(lax.shift_right_logical(lane, 5) == h, wide, 0.0) for h in range(HEADS)]
    wide = jnp.concatenate(per_head, axis=0).astype(bf16)
    logits = lax.dot_general(
        wide, kv, (((1,), (1,)), ((), ())), preferred_element_type=f32
    ) * (1.0 / math.sqrt(C // HEADS))
    top = jnp.max(logits, axis=1, keepdims=True)
    weight = jnp.exp(logits - top)
    total = jnp.sum(weight, axis=1, keepdims=True)
    coarse = weight.astype(bf16)
    fine = (weight - coarse.astype(f32)).astype(bf16)
    mixed = jnp.dot(coarse, kv, preferred_element_type=f32)
    mixed = mixed + jnp.dot(fine, kv, preferred_element_type=f32)
    mixed = mixed / total
    context = jnp.where(lane < C + C // 2, mixed[:rows], mixed[rows:])
    context = jnp.where(lane < C, 0.0, context)
    mean = jnp.sum(context * context, axis=1, keepdims=True) / C
    attended = (context / jnp.sqrt(mean + EPSILON)).astype(bf16)
    w_out = jnp.concatenate([w_out] * 4, axis=1)
    return jnp.dot(attended[:, C:], w_out, preferred_element_type=f32)


def y_reader(t0, t1):
    _, odd_y = parities()

    def from_y(oy, place, width=COL):
        lanes = slice(place, place + width)
        a, b = (t1, t0) if oy < 0 else (t0, t1)
        return pick(odd_y, a[:, lanes], b[:, lanes])

    return from_y


def x_reader(r0, r1):
    odd_x, _ = parities()

    def from_x(ox, k):
        lanes = slice(k * COL, (k + 1) * COL)
        a, b = (r1, r0) if ox < 0 else (r0, r1)
        return pick(odd_x, a[:, lanes], b[:, lanes])

    return from_x


def side_ids(about):
    high, low = about[:, :C].astype(f32), about[:, C : 2 * C].astype(f32)
    number = (high * 64.0 + low).astype(jnp.int32) - 1
    return jnp.where(number < 0, FAR, number)


def global_term(group, w_key, w_value, w_query, w_out):
    count = group.shape[0]
    here = lax.axis_index("sy")
    tokens = []
    for step in (0, count - 1, 1):
        packed = group[lax.rem(here + step, count)]
        tokens += [packed[:, :C], packed[:, C:]]
    packed = group[...].reshape(-1, 2 * C)
    tokens = jnp.concatenate(tokens, axis=0)
    return attention(tokens, packed, w_key[...], w_value[...], w_query[...], w_out[...])


FACE_SLOTS, SIDE_SLOTS = 16, 8


def near_kernel(
    masked, t0, t1, ids_ref, weight, acc, acc_side, band_edge, pack, slots, inner, side_inner,
    band,
):
    from_message = y_reader(t0, t1)
    ids = ids_ref[...]

    def own(x, y):
        return masked[:, column(x, y)]

    def from_y(oy, x):
        return from_message(oy, NEAR + x * COL)

    fill_band(weight, band)
    gather_own(own, None, from_y, None, lambda ox, oy: own_select(ids, ox, oy), inner, (0,))
    numbers = {}
    for side in (-1, 1):
        number = numbers[side] = side_ids(from_message(side, META))
        gather_side(
            own, None, from_message, side,
            lambda side, ox, number=number: side_select(number, side, ox), side_inner, (0,),
        )

    base = device_base()
    for k, ox in enumerate((-1, 1)):
        face = [(ox, oy, oz) for oy in (-1, 0, 1) for oz in (-1, 0, 1)]
        parts = [slot_ids(ids, base + id_step(ox, 0), face, FACE_SLOTS)]
        for oy in (-1, 1):
            corner = [(ox, oy, oz) for oz in (-1, 0, 1)]
            parts.append(slot_ids(ids, base + id_step(ox, oy), corner, SIDE_SLOTS))
        slots[k, :, : FACE_SLOTS + 2 * SIDE_SLOTS] = jnp.concatenate(parts, axis=1)

    def store(x_range, value):
        count = len(x_range)
        for n, x in enumerate(x_range):
            acc[x] = value[n * 4 * BRICKS : (n + 1) * 4 * BRICKS]
            rows = (4 * count + 2 * n) * BRICKS
            acc_side[x] = value[rows : rows + 2 * BRICKS]

    convolve_inner(inner, side_inner, band, store)
    band_edge[:3] = band[:3]
    band_edge[3:] = band[6:]
    for k, ox in enumerate((-1, 1)):
        there = device_base() + id_step(ox, 0)
        pack[2 * k, :, :BRICKS] = compaction(owner_marks(ids, there), FACE_SLOTS).astype(bf16)
        sides = [compaction(owner_marks(numbers[side], there), SIDE_SLOTS) for side in (-1, 1)]
        gap = jnp.zeros_like(sides[0])
        low = jnp.concatenate([sides[0], gap], axis=1)
        high = jnp.concatenate([gap, sides[1]], axis=1)
        both = jnp.concatenate([low, high], axis=0)
        pack[2 * k + 1, :, : 2 * BRICKS] = both.astype(bf16)


def finish(acc, acc_side, x, gain, offset, cover, from_message, term, store, store_side):
    def one(part, which, cov):
        first = jnp.maximum(part * gain + offset, 0.0)
        return ((first + term[which * BRICKS : (which + 1) * BRICKS]) * cov).astype(bf16)

    row = lax.broadcasted_iota(jnp.int32, (64, COL), 0)
    voxel = lax.shift_right_logical(lax.broadcasted_iota(jnp.int32, (64, COL), 1), 6)
    for y in range(4):
        cov = cover[:, column(x, y)].astype(f32)
        store(x, y, one(acc[y * BRICKS : (y + 1) * BRICKS], 0, cov))
    for k, side in enumerate((-1, 1)):
        occupied = from_message(side, META)[:, 2 * C : 3 * C]
        spread = (row == voxel + (x * 16 + (3 - 3 * k) * 4)).astype(f32).astype(bf16)
        cov = jnp.dot(occupied, spread, preferred_element_type=f32)
        store_side(x, side, one(acc_side[k * BRICKS : (k + 1) * BRICKS], 1 + k, cov))


def edge_conv_kernel(
    masked, r0, r1, t0, t1, ids_ref, band_edge, acc, acc_side, total, total_side,
    outer, side_outer,
):
    from_message, from_x = y_reader(t0, t1), x_reader(r0, r1)
    ids = ids_ref[...]

    def own(x, y):
        return masked[:, column(x, y)]

    gather_own(
        own,
        from_x,
        lambda oy, x: from_message(oy, NEAR + x * COL),
        lambda ox, oy: from_x(ox, corner_place(oy, NEAR)),
        lambda ox, oy: own_select(ids, ox, oy),
        outer,
        (-1, 1),
    )
    for side in (-1, 1):
        number = side_ids(from_message(side, META))
        gather_side(
            own, from_x, from_message, side,
            lambda side, ox, number=number: side_select(number, side, ox), side_outer, (-1, 1),
        )
    for n, x in enumerate((0, 3)):
        more = convolve_edge(outer, side_outer, band_edge, x)
        total[n] = acc[x] + more[: 4 * BRICKS]
        total_side[n] = acc_side[x] + more[4 * BRICKS :]


def edge_finish_kernel(
    group, w_key, w_value, w_query, w_out, t0, t1, scale, shift, cover, total, total_side, pack,
    edges, m0, m1, term_out,
):
    odd_x, _ = parities()
    from_message = y_reader(t0, t1)
    term = global_term(group, w_key, w_value, w_query, w_out)
    term_out[...] = term

    def put(x, k, value):
        edges[0 if x == 0 else 1, :, k * COL : (k + 1) * COL] = value

    for n, x in enumerate((0, 3)):
        finish(
            total[n], total_side[n], x, four(scale), four(shift), cover, from_message, term,
            put, lambda x, side, value: put(x, 4 if side < 0 else 5, value),
        )
    messages = []
    for n in range(2):
        face = jnp.dot(
            pack[2 * n, :, :BRICKS], edges[n, :, : 4 * COL], preferred_element_type=f32
        )
        sides = jnp.concatenate(
            [edges[n, :, 4 * COL : 5 * COL], edges[n, :, 5 * COL :]], axis=0
        )
        side = jnp.dot(pack[2 * n + 1, :, : 2 * BRICKS], sides, preferred_element_type=f32)
        messages.append(jnp.concatenate([face, side], axis=1).astype(bf16))
    m0[...] = pick(odd_x, messages[1], messages[0])
    m1[...] = pick(odd_x, messages[0], messages[1])


def edge_reader(edges):
    return lambda x, k: edges[0 if x == 0 else 1, :, k * COL : (k + 1) * COL]


def middle_kernel(
    acc, acc_side, scale, shift, cover, t0, t1, term, edges, ids_ref, weight,
    scale_two, shift_two, masked, acc_out, band_edge, result, mid, mid_side, padded, band,
):
    edge = edge_reader(edges)
    from_message = y_reader(t0, t1)
    ids = ids_ref[...]
    fill_band(weight, band)
    band_edge[:3] = band[:3]
    band_edge[3:] = band[6:]

    def put(x, y, value):
        mid[x - 1, y] = value

    def put_side(x, side, value):
        mid_side[x - 1, 0 if side < 0 else 1] = value

    for x in (1, 2):
        finish(
            acc[x], acc_side[x], x, four(scale), four(shift), cover, from_message, term,
            put, put_side,
        )

    def own(x, y):
        return mid[x - 1, y] if x in (1, 2) else edge(x, y)

    def from_y(oy, x):
        k = 0 if oy < 0 else 1
        return mid_side[x - 1, k] if x in (1, 2) else edge(x, 4 + k)

    gather_own(own, None, from_y, None, lambda ox, oy: own_select(ids, ox, oy), padded, (0,))

    def store(x_range, value):
        for n, x in enumerate(x_range):
            part = value[n * 4 * BRICKS : (n + 1) * 4 * BRICKS]
            if x in (0, 3):
                acc_out[0 if x == 0 else 1] = part
            else:
                gain, offset = four(scale_two), four(shift_two)
                put_result(part, x, gain, offset, cover, masked, result.at[x - 1])

    convolve_inner(padded, None, band, store)


def put_result(total, x, gain, offset, cover, masked, out):
    for y in range(4):
        lanes = column(x, y)
        value = total[y * BRICKS : (y + 1) * BRICKS] * gain + offset
        value = jnp.maximum(value + masked[:, lanes].astype(f32), 0.0)
        value = (value * cover[:, lanes].astype(f32)).astype(bf16)
        out[:, y * COL : (y + 1) * COL] = value


def second_kernel(
    edges, r0, r1, ids_ref, slots, band_edge, scale, shift, cover, masked, acc, middle, refined,
    outer, result, sem,
):
    copies = []

    def send(part, x):
        there = refined.at[:, x * 4 * COL : (x + 1) * 4 * COL]
        copies.append(pltpu.make_async_copy(part, there, sem.at[x]))
        copies[-1].start()

    send(middle.at[0], 1)
    send(middle.at[1], 2)
    odd_x, _ = parities()
    edge, ids = edge_reader(edges), ids_ref[...]
    base = device_base()

    def received(ox, rows, k):
        lanes = slice(k * COL, (k + 1) * COL)
        a, b = (r1, r0) if ox < 0 else (r0, r1)
        return pick(odd_x, a[rows, lanes], b[rows, lanes])

    def from_corner(ox, oy):
        return received(ox, slice(None), 4)

    def select_of(ox, oy):
        known = slots[0 if ox < 0 else 1, :1, : FACE_SLOTS + 2 * SIDE_SLOTS]
        candidates = [device_row(base), known[:, :FACE_SLOTS]]
        if oy:
            candidates += [device_row(base + id_step(0, oy)), known[:, FACE_SLOTS:]]
        return one_hot(ids, [(ox, oy, oz) for oz in (1, -1, 0)], candidates)

    gather_own(
        edge,
        lambda ox, y: received(ox, slice(None), y),
        lambda oy, x: edge(x, 4 if oy < 0 else 5),
        from_corner,
        select_of,
        outer,
        (-1, 1),
    )
    gain, offset = four(scale), four(shift)
    for n, x in enumerate((0, 3)):
        total = acc[n] + convolve_edge(outer, None, band_edge, x)
        put_result(total, x, gain, offset, cover, masked, result.at[n])
        send(result.at[n], x)
    for copy in copies:
        copy.wait()


def exchange(first, second, axis):
    return pair_exchange(first, axis, 1), pair_exchange(second, axis, 0)


def local(
    features, occupancy, adjacency, conv_one, conv_two, scale_one, shift_one,
    scale_two, shift_two, w_query, w_key, w_value, w_out,
):
    n_sy = lax.axis_size("sy")
    whole = shape(BRICKS, 64 * C)
    band_edge = shape(6, TAP, COL)
    own_acc, side_acc = shape(4, 4 * BRICKS, COL, dtype=f32), shape(4, 2 * BRICKS, COL, dtype=f32)
    band = pltpu.VMEM((9, TAP, COL), bf16)
    inner = pltpu.VMEM((4, 6, BRICKS, TAP), bf16)
    outer = pltpu.VMEM((2, 6, BRICKS, TAP), bf16)
    side_inner = pltpu.VMEM((4, 3, 2 * BRICKS, TAP), bf16)
    side_outer = pltpu.VMEM((2, 3, 2 * BRICKS, TAP), bf16)
    marks = jnp.concatenate([occupancy, adjacency], axis=1)
    message = shape(BRICKS, Y_LANES)
    masked, cover, tokens, meta, ids, s0, s1 = call(
        prepare_kernel,
        [
            whole, whole, shape(n_sy, BRICKS // 2, 2 * C), shape(BRICKS, 4 * C),
            shape(BRICKS, 27, dtype=jnp.int32), message, message,
        ],
        (features, marks),
        bytes_accessed=2 << 20,
    )
    rows = [v.reshape(1, C) for v in (scale_one, shift_one, scale_two, shift_two)]
    t0, t1 = exchange(s0, s1, "sy")
    group = lax.all_to_all(tokens, "sy", 0, 0)
    x_message = shape(BRICKS, 8 * COL)
    x0, x1 = call(
        message_kernel, [x_message] * 2, (masked, t0, t1), flops=1 << 35, bytes_accessed=1 << 20
    )
    r0, r1 = exchange(x0, x1, "sx")
    acc, acc_side, band_one, pack, slots = call(
        near_kernel,
        [
            own_acc, side_acc, band_edge, shape(4, FACE_SLOTS, 128),
            shape(2, 8, 128, dtype=jnp.int32),
        ],
        (masked, t0, t1, ids, conv_one),
        [inner, side_inner, band],
        flops=1 << 33,
        bytes_accessed=2 << 20,
    )
    total, total_side = call(
        edge_conv_kernel,
        [
            shape(2, 4 * BRICKS, COL, dtype=f32),
            shape(2, 2 * BRICKS, COL, dtype=f32),
        ],
        (masked, r0, r1, t0, t1, ids, band_one, acc, acc_side),
        [outer, side_outer],
        flops=2 * 384 * 1152 * 256,
        bytes_accessed=4 << 20,
    )
    group, total = lax.optimization_barrier((group, total))
    out_message = shape(FACE_SLOTS, 5 * COL)
    edges, m0, m1, term = call(
        edge_finish_kernel,
        [
            shape(2, BRICKS, 6 * COL), out_message, out_message,
            shape(3 * BRICKS, COL, dtype=f32),
        ],
        (
            group, w_key, w_value, w_query, w_out, t0, t1, rows[0], rows[1], cover, total,
            total_side, pack,
        ),
        flops=1 << 26,
        bytes_accessed=2 << 20,
    )
    r0, r1 = exchange(m0, m1, "sx")
    acc, band_two, half = call(
        middle_kernel,
        [shape(2, 4 * BRICKS, COL, dtype=f32), band_edge, shape(2, BRICKS, 4 * COL)],
        (
            acc, acc_side, rows[0], rows[1], cover, t0, t1, term, edges, ids, conv_two,
            rows[2], rows[3], masked,
        ),
        [
            pltpu.VMEM((2, 4, BRICKS, COL), bf16),
            pltpu.VMEM((2, 2, BRICKS, COL), bf16),
            inner,
            band,
        ],
        flops=1 << 33,
        bytes_accessed=4 << 20,
    )
    return call(
        second_kernel,
        whole,
        (
            edges, r0, r1, ids, slots, band_two, rows[2], rows[3], cover, masked, acc, half,
        ),
        [outer, pltpu.VMEM((2, BRICKS, 4 * COL), bf16), pltpu.SemaphoreType.DMA((4,))],
        flops=2 * 256 * 1152 * 256,
        bytes_accessed=3 << 20,
        hbm_out=True,
    )


def solution(mesh):
    split = P(("sx", "sy"), None)
    return jax.shard_map(
        local,
        mesh=mesh,
        in_specs=(split,) * 3 + (P(),) * 10,
        out_specs=split,
        check_vma=False,
    )
```

```python
import math

import jax
import jax.numpy as jnp
from jax import lax
from jax.experimental import pallas as pl
from jax.experimental.pallas import tpu as pltpu
from jax.sharding import PartitionSpec as P

HEADS = 2
C = 64
COL = 4 * C
BRICKS = 32
EPSILON = 1e-05
FAR = -(1 << 20)
VMEM_LIMIT = 16 * 1024 * 1024
WHOLE_VMEM = 60 * 1024 * 1024
f32, bf16 = jnp.float32, jnp.bfloat16


def call(
    kernel, out_shape, args, scratch=(), flops=0, bytes_accessed=0, hbm_in=False, hbm_out=False
):
    vmem, hbm = pl.BlockSpec(memory_space=pltpu.VMEM), pl.BlockSpec(memory_space=pl.ANY)
    return pl.pallas_call(
        kernel,
        out_shape=out_shape,
        in_specs=[hbm if hbm_in else vmem] * len(args),
        out_specs=jax.tree.map(lambda _: hbm if hbm_out else vmem, out_shape),
        scratch_shapes=list(scratch),
        compiler_params=pltpu.CompilerParams(
            vmem_limit_bytes=WHOLE_VMEM if hbm_in else VMEM_LIMIT
        ),
        cost_estimate=pl.CostEstimate(
            flops=flops, bytes_accessed=bytes_accessed, transcendentals=0
        ),
    )(*args)


def shape(*dims, dtype=bf16):
    return jax.ShapeDtypeStruct(dims, dtype)


def column(x, y):
    return slice((x * 4 + y) * COL, (x * 4 + y + 1) * COL)


def face_x(ref, x):
    return ref[:, x * 4 * COL : (x + 1) * 4 * COL]


def pick(flag, a, b):
    return jnp.where(flag, a, b)


def parities():
    odd_x = lax.rem(lax.axis_index("sx"), 2) == 1
    odd_y = lax.rem(lax.axis_index("sy"), 2) == 1
    return odd_x, odd_y


def pair_exchange(value, axis, phase):
    n_x, n_y = lax.axis_size("sx"), lax.axis_size("sy")

    def partner(x, y):
        s, count = (x, n_x) if axis == "sx" else (y, n_y)
        if phase == 1 and s in (0, count - 1):
            return (x, y ^ 1) if axis == "sx" else (x ^ 1, y)
        s = s ^ 1 if phase == 0 else ((s + 1) ^ 1) - 1
        return (s, y) if axis == "sx" else (x, s)

    pairs = []
    for x in range(n_x):
        for y in range(n_y):
            there = partner(x, y)
            pairs.append((x * n_y + y, there[0] * n_y + there[1]))
    return lax.ppermute(value, ("sx", "sy"), pairs)


def device_base():
    return (lax.axis_index("sx") * lax.axis_size("sy") + lax.axis_index("sy")) * BRICKS


def id_step(dx, dy):
    return (dx * lax.axis_size("sy") + dy) * BRICKS


def device_row(base):
    return jnp.bitwise_and(lax.broadcasted_iota(jnp.int32, (1, BRICKS), 1), BRICKS - 1) + base


def one_hot(ids, offsets, candidates):
    candidate = candidates[0]
    if len(candidates) > 1:
        candidate = jnp.concatenate(candidates, axis=1)
    candidate = jnp.broadcast_to(candidate, (BRICKS, candidate.shape[1]))
    rows = [
        (ids[:, o : o + 1] == candidate).astype(f32).astype(bf16)
        for o in ((ox + 1) * 9 + (oy + 1) * 3 + (oz + 1) for ox, oy, oz in offsets)
    ]
    return jnp.concatenate(rows, axis=0)


def owner_marks(ids, base):
    hit = jnp.logical_and(ids >= base, ids < base + BRICKS)
    return jnp.max(hit.astype(f32), axis=1, keepdims=True)


def compaction(marks, slots):
    row = lax.broadcasted_iota(jnp.int32, (BRICKS, BRICKS), 0)
    lane = lax.broadcasted_iota(jnp.int32, (BRICKS, BRICKS), 1)
    rank = jnp.sum(jnp.where(row < lane, marks, 0.0), axis=0, keepdims=True)
    marked = jnp.sum(jnp.where(row == lane, marks, 0.0), axis=0, keepdims=True)
    slot = lax.broadcasted_iota(jnp.int32, (slots, BRICKS), 0).astype(f32)
    return jnp.where(slot == rank, marked, 0.0)


def slot_ids(ids, base, offsets, slots):
    candidate = jnp.broadcast_to(device_row(base), (BRICKS, BRICKS))
    hit = jnp.zeros((BRICKS, BRICKS), f32)
    for ox, oy, oz in offsets:
        o = (ox + 1) * 9 + (oy + 1) * 3 + (oz + 1)
        hit = jnp.maximum(hit, (ids[:, o : o + 1] == candidate).astype(f32))
    marked = jnp.broadcast_to(jnp.max(hit, axis=0, keepdims=True), (8, BRICKS))
    row = lax.broadcasted_iota(jnp.int32, (BRICKS, BRICKS), 0)
    lane = lax.broadcasted_iota(jnp.int32, (BRICKS, BRICKS), 1)
    before = (row < lane).astype(f32).astype(bf16)
    rank = jnp.dot(marked.astype(bf16), before, preferred_element_type=f32)
    slot = lax.broadcasted_iota(jnp.int32, (slots, BRICKS), 0).astype(f32)
    pack = jnp.where(slot == rank[:1], marked[:1], 0.0).astype(bf16)
    count = lax.broadcasted_iota(jnp.int32, (8, BRICKS), 1).astype(f32) + 1.0
    local_id = lax.dot_general(
        count.astype(bf16), pack, (((1,), (1,)), ((), ())), preferred_element_type=f32
    ).astype(jnp.int32)
    return jnp.where(local_id > 0, local_id - 1 + base, 2 * FAR)


def put_column(select, parts, core, store):
    table = parts[0] if len(parts) == 1 else jnp.concatenate(parts, axis=0)
    got = jnp.dot(select, table, preferred_element_type=f32).astype(bf16)
    lane_low = lax.broadcasted_iota(jnp.int32, (BRICKS, 128), 1) < C
    ends = jnp.where(lane_low, got[:BRICKS, :128], got[BRICKS : 2 * BRICKS, 128:])
    store(got[2 * BRICKS :] if core is None else core, ends)


NEAR, BEHIND, META, Y_LANES = 0, 4 * COL, 8 * COL, 9 * COL


def prepare_kernel(
    feat_hbm, occ_hbm, adj_hbm, masked, cover, tokens_all, meta, ids, s0, s1, feat, occ, adj, sems
):
    pairs = ((occ_hbm, occ), (feat_hbm, feat), (adj_hbm, adj))
    copies = [pltpu.make_async_copy(a, b, sems.at[k]) for k, (a, b) in enumerate(pairs)]
    for copy in copies:
        copy.start()
    copies[0].wait()
    occupied = occ[...].astype(f32).astype(bf16)
    row = lax.broadcasted_iota(jnp.int32, (64, COL), 0)
    voxel = lax.shift_right_logical(lax.broadcasted_iota(jnp.int32, (64, COL), 1), 6)
    copies[1].wait()
    total = jnp.zeros((BRICKS, 128), f32)
    for k in range(16):
        lanes = slice(k * COL, (k + 1) * COL)
        spread = (row == voxel + 4 * k).astype(f32).astype(bf16)
        cov = jnp.dot(occupied, spread, preferred_element_type=f32).astype(bf16)
        part = feat[:, lanes] * cov
        cover[:, lanes] = cov
        masked[:, lanes] = part
        wide = part.astype(f32)
        total = total + wide[:, :128] + wide[:, 128:]
    summed = total[:, :C] + total[:, C:]
    tokens = (summed / 8.0).astype(bf16)
    half = BRICKS // 2
    packed = jnp.concatenate([tokens[:half], tokens[half:]], axis=1)
    tokens_all[...] = jnp.broadcast_to(packed[None], tokens_all.shape)
    copies[2].wait()
    number = adj[...]
    ids[...] = jnp.where(number < 0, FAR, number)
    number = number + 1
    high = lax.shift_right_logical(number, 6).astype(f32).astype(bf16)
    low = jnp.bitwise_and(number, 63).astype(f32).astype(bf16)
    gap = jnp.zeros((BRICKS, C - 27), bf16)
    about = jnp.concatenate([high, gap, low, gap, occupied, tokens], axis=1)
    meta[...] = about
    _, odd_y = parities()

    def write(out, near, behind):
        for place, y in ((NEAR, near), (BEHIND, behind)):
            for x in range(4):
                out[:, place + x * COL : place + (x + 1) * COL] = masked[:, column(x, y)]
        out[:, META:] = about

    @pl.when(odd_y)
    def _():
        write(s0, 3, 2)
        write(s1, 0, 1)

    @pl.when(jnp.logical_not(odd_y))
    def _():
        write(s0, 0, 1)
        write(s1, 3, 2)


def fill_band(weight, band):
    zero = jnp.zeros((C, C), bf16)
    for t in range(9):
        for r, z_in in enumerate((0, 1, 2, 3, 4, -1)):
            blocks = []
            for z_out in range(4):
                tap = z_in - z_out + 1
                blocks.append(weight[t * 3 + tap] if 0 <= tap < 3 else zero)
            band[t, r * C : (r + 1) * C, :] = jnp.concatenate(blocks, axis=1)


def message_kernel(masked, t0, t1, x0, x1):
    odd_x, odd_y = parities()

    def write(out, x):
        out[:, : 4 * COL] = face_x(masked, x)
        place = 4 * COL
        for a, b in ((t1, t0), (t0, t1)):
            for plane in (NEAR, BEHIND):
                lanes = slice(plane + x * COL, plane + (x + 1) * COL)
                out[:, place : place + COL] = pick(odd_y, a[:, lanes], b[:, lanes])
                place += COL

    @pl.when(odd_x)
    def _():
        write(x0, 3)
        write(x1, 0)

    @pl.when(jnp.logical_not(odd_x))
    def _():
        write(x0, 0)
        write(x1, 3)


def place_x(ox, x):
    return x if ox == 0 else (0 if ox < 0 else 1)


def sources_of(ox, oy):
    sources = [(0, 0)]
    if ox:
        sources.append((ox, 0))
    if oy:
        sources.append((0, oy))
    if ox and oy:
        sources.append((ox, oy))
    return sources


def own_select(ids, ox, oy):
    base = device_base()
    offsets = [(ox, oy, oz) for oz in ((1, -1) if ox == 0 and oy == 0 else (1, -1, 0))]
    return one_hot(ids, offsets, [device_row(base + id_step(dx, dy)) for dx, dy in sources_of(ox, oy)])


def side_select(ids, side, ox):
    here, there = device_base(), device_base() + id_step(0, side)
    bases = [0] if ox == 0 else [0, id_step(ox, 0)]
    outer = [device_row(here + step) for step in bases]
    inner = [device_row(there + step) for step in bases]
    offsets = [(ox, 0, oz) for oz in ((1, -1) if ox == 0 else (1, -1, 0))]
    return (
        one_hot(ids, offsets, inner),
        one_hot(ids, [(ox, -side, oz) for oz in (1, -1, 0)], outer),
    )


def gather_own(own, from_x, from_y, from_corner, select_of, padded, x_offsets):
    for ox in x_offsets:
        for oy in (-1, 0, 1):
            centre = ox == 0 and oy == 0
            select = select_of(ox, oy)
            for x in {-1: (3,), 0: range(4), 1: (0,)}[ox]:
                for y in {-1: (3,), 0: range(4), 1: (0,)}[oy]:
                    parts = [own(x, y)]
                    if ox:
                        parts.append(from_x(ox, y))
                    if oy:
                        parts.append(from_y(oy, x))
                    if ox and oy:
                        parts.append(from_corner(ox, oy))
                    px = place_x(ox, x)
                    py = {-1: 0, 0: 1 + y, 1: 5}[oy]

                    def store(core, ends, px=px, py=py):
                        padded[px, py, :, :COL] = core
                        padded[px, py, :, COL:] = ends

                    put_column(select, parts, parts[0] if centre else None, store)


def gather_side(own, from_x, from_message, side, select_of, padded, x_offsets):
    mine = {-1: 0, 1: 3}[side]
    rows = slice(0, BRICKS) if side < 0 else slice(BRICKS, 2 * BRICKS)
    for ox in x_offsets:
        select_inner, select_outer = select_of(side, ox)
        for x in {-1: (3,), 0: range(4), 1: (0,)}[ox]:
            px = place_x(ox, x)
            for place, py in ((BEHIND, 1 + side), (NEAR, 1), (None, 1 - side)):

                def store(core, ends, px=px, py=py):
                    padded[px, py, rows, :COL] = core
                    padded[px, py, rows, COL:] = ends

                if place is None:
                    parts = [own(x, mine)]
                    if ox:
                        parts.append(from_x(ox, mine))
                    put_column(select_outer, parts, None, store)
                    continue
                parts = [from_message(side, place + x * COL)]
                if ox:
                    parts.append(from_x(ox, corner_place(side, place)))
                put_column(select_inner, parts, parts[0] if ox == 0 else None, store)


def corner_place(side, plane):
    return 4 + (0 if side < 0 else 2) + (0 if plane == NEAR else 1)


TAP = 6 * C


def taps(padded, side, x_range, first, count):
    parts = []
    for t in range(first, first + count):
        i, j = t // 3, t % 3
        rows = [padded[x + i, j : j + 4].reshape(4 * BRICKS, TAP) for x in x_range]
        if side is not None:
            rows += [side[x + i, j] for x in x_range]
        parts.append(jnp.concatenate(rows, axis=0))
    return jnp.concatenate(parts, axis=1)


def product(lhs, band, first, count):
    rhs = band[first : first + count].reshape(count * TAP, COL)
    return jnp.dot(lhs, rhs, preferred_element_type=f32)


def convolve_inner(inner, side, band, store):
    store((1, 2), product(taps(inner, side, (0, 1), 0, 9), band, 0, 9))
    store((0,), product(taps(inner, side, (-1,), 3, 6), band, 3, 6))
    store((3,), product(taps(inner, side, (2,), 0, 6), band, 0, 6))


def convolve_edge(outer, side, band, x):
    i, place = (0, 0) if x == 0 else (2, 1)
    return product(taps(outer, side, (place - i,), 3 * i, 3), band, 0 if x == 0 else 3, 3)


def four(ref):
    return jnp.concatenate([ref[...]] * 4, axis=1)


def project(tokens, weight):
    return jnp.dot(tokens, weight, preferred_element_type=f32).astype(bf16)


def attention(tokens, packed, w_key, w_value, w_query, w_out):
    group = jnp.concatenate([packed[:, :C], packed[:, C:]], axis=0)
    kv = project(group, jnp.concatenate([w_key, w_value], axis=1))
    queries = project(tokens, w_query)
    rows = queries.shape[0]
    wide = jnp.concatenate([queries, jnp.zeros_like(queries)], axis=1).astype(f32)
    lane = lax.broadcasted_iota(jnp.int32, (rows, 2 * C), 1)
    per_head = [jnp.where(lax.shift_right_logical(lane, 5) == h, wide, 0.0) for h in range(HEADS)]
    wide = jnp.concatenate(per_head, axis=0).astype(bf16)
    logits = lax.dot_general(
        wide, kv, (((1,), (1,)), ((), ())), preferred_element_type=f32
    ) * (1.0 / math.sqrt(C // HEADS))
    top = jnp.max(logits, axis=1, keepdims=True)
    weight = jnp.exp(logits - top)
    total = jnp.sum(weight, axis=1, keepdims=True)
    coarse = weight.astype(bf16)
    fine = (weight - coarse.astype(f32)).astype(bf16)
    mixed = jnp.dot(coarse, kv, preferred_element_type=f32)
    mixed = mixed + jnp.dot(fine, kv, preferred_element_type=f32)
    mixed = mixed / total
    context = jnp.where(lane < C + C // 2, mixed[:rows], mixed[rows:])
    context = jnp.where(lane < C, 0.0, context)
    mean = jnp.sum(context * context, axis=1, keepdims=True) / C
    attended = (context / jnp.sqrt(mean + EPSILON)).astype(bf16)
    w_out = jnp.concatenate([w_out] * 4, axis=1)
    return jnp.dot(attended[:, C:], w_out, preferred_element_type=f32)


def y_reader(t0, t1):
    _, odd_y = parities()

    def from_y(oy, place, width=COL):
        lanes = slice(place, place + width)
        a, b = (t1, t0) if oy < 0 else (t0, t1)
        return pick(odd_y, a[:, lanes], b[:, lanes])

    return from_y


def x_reader(r0, r1):
    odd_x, _ = parities()

    def from_x(ox, k):
        lanes = slice(k * COL, (k + 1) * COL)
        a, b = (r1, r0) if ox < 0 else (r0, r1)
        return pick(odd_x, a[:, lanes], b[:, lanes])

    return from_x


def side_ids(about):
    high, low = about[:, :C].astype(f32), about[:, C : 2 * C].astype(f32)
    number = (high * 64.0 + low).astype(jnp.int32) - 1
    return jnp.where(number < 0, FAR, number)


def global_term(group, w_key, w_value, w_query, w_out):
    count = group.shape[0]
    here = lax.axis_index("sy")
    tokens = []
    for step in (0, count - 1, 1):
        packed = group[lax.rem(here + step, count)]
        tokens += [packed[:, :C], packed[:, C:]]
    packed = group[...].reshape(-1, 2 * C)
    tokens = jnp.concatenate(tokens, axis=0)
    return attention(tokens, packed, w_key[...], w_value[...], w_query[...], w_out[...])


FACE_SLOTS, SIDE_SLOTS = 16, 8


def near_kernel(
    masked, t0, t1, ids_ref, weight, acc, acc_side, band_edge, pack, slots, inner, side_inner,
    band,
):
    from_message = y_reader(t0, t1)
    ids = ids_ref[...]

    def own(x, y):
        return masked[:, column(x, y)]

    def from_y(oy, x):
        return from_message(oy, NEAR + x * COL)

    fill_band(weight, band)
    gather_own(own, None, from_y, None, lambda ox, oy: own_select(ids, ox, oy), inner, (0,))
    numbers = {}
    for side in (-1, 1):
        number = numbers[side] = side_ids(from_message(side, META))
        gather_side(
            own, None, from_message, side,
            lambda side, ox, number=number: side_select(number, side, ox), side_inner, (0,),
        )

    base = device_base()
    for k, ox in enumerate((-1, 1)):
        face = [(ox, oy, oz) for oy in (-1, 0, 1) for oz in (-1, 0, 1)]
        parts = [slot_ids(ids, base + id_step(ox, 0), face, FACE_SLOTS)]
        for oy in (-1, 1):
            corner = [(ox, oy, oz) for oz in (-1, 0, 1)]
            parts.append(slot_ids(ids, base + id_step(ox, oy), corner, SIDE_SLOTS))
        slots[k, :, : FACE_SLOTS + 2 * SIDE_SLOTS] = jnp.concatenate(parts, axis=1)

    def store(x_range, value):
        count = len(x_range)
        for n, x in enumerate(x_range):
            acc[x] = value[n * 4 * BRICKS : (n + 1) * 4 * BRICKS]
            rows = (4 * count + 2 * n) * BRICKS
            acc_side[x] = value[rows : rows + 2 * BRICKS]

    convolve_inner(inner, side_inner, band, store)
    band_edge[:3] = band[:3]
    band_edge[3:] = band[6:]
    for k, ox in enumerate((-1, 1)):
        there = device_base() + id_step(ox, 0)
        pack[2 * k, :, :BRICKS] = compaction(owner_marks(ids, there), FACE_SLOTS).astype(bf16)
        sides = [compaction(owner_marks(numbers[side], there), SIDE_SLOTS) for side in (-1, 1)]
        gap = jnp.zeros_like(sides[0])
        low = jnp.concatenate([sides[0], gap], axis=1)
        high = jnp.concatenate([gap, sides[1]], axis=1)
        both = jnp.concatenate([low, high], axis=0)
        pack[2 * k + 1, :, : 2 * BRICKS] = both.astype(bf16)


def finish(acc, acc_side, x, gain, offset, cover, from_message, term, store, store_side):
    def one(part, which, cov):
        first = jnp.maximum(part * gain + offset, 0.0)
        return ((first + term[which * BRICKS : (which + 1) * BRICKS]) * cov).astype(bf16)

    row = lax.broadcasted_iota(jnp.int32, (64, COL), 0)
    voxel = lax.shift_right_logical(lax.broadcasted_iota(jnp.int32, (64, COL), 1), 6)
    for y in range(4):
        cov = cover[:, column(x, y)].astype(f32)
        store(x, y, one(acc[y * BRICKS : (y + 1) * BRICKS], 0, cov))
    for k, side in enumerate((-1, 1)):
        occupied = from_message(side, META)[:, 2 * C : 3 * C]
        spread = (row == voxel + (x * 16 + (3 - 3 * k) * 4)).astype(f32).astype(bf16)
        cov = jnp.dot(occupied, spread, preferred_element_type=f32)
        store_side(x, side, one(acc_side[k * BRICKS : (k + 1) * BRICKS], 1 + k, cov))


def edge_conv_kernel(
    masked, r0, r1, t0, t1, ids_ref, band_edge, acc, acc_side, total, total_side,
    outer, side_outer,
):
    from_message, from_x = y_reader(t0, t1), x_reader(r0, r1)
    ids = ids_ref[...]

    def own(x, y):
        return masked[:, column(x, y)]

    gather_own(
        own,
        from_x,
        lambda oy, x: from_message(oy, NEAR + x * COL),
        lambda ox, oy: from_x(ox, corner_place(oy, NEAR)),
        lambda ox, oy: own_select(ids, ox, oy),
        outer,
        (-1, 1),
    )
    for side in (-1, 1):
        number = side_ids(from_message(side, META))
        gather_side(
            own, from_x, from_message, side,
            lambda side, ox, number=number: side_select(number, side, ox), side_outer, (-1, 1),
        )
    for n, x in enumerate((0, 3)):
        more = convolve_edge(outer, side_outer, band_edge, x)
        total[n] = acc[x] + more[: 4 * BRICKS]
        total_side[n] = acc_side[x] + more[4 * BRICKS :]


def edge_finish_kernel(
    group, w_key, w_value, w_query, w_out, t0, t1, scale, shift, cover, total, total_side, pack,
    edges, m0, m1, term_out,
):
    odd_x, _ = parities()
    from_message = y_reader(t0, t1)
    term = global_term(group, w_key, w_value, w_query, w_out)
    term_out[...] = term

    def put(x, k, value):
        edges[0 if x == 0 else 1, :, k * COL : (k + 1) * COL] = value

    for n, x in enumerate((0, 3)):
        finish(
            total[n], total_side[n], x, four(scale), four(shift), cover, from_message, term,
            put, lambda x, side, value: put(x, 4 if side < 0 else 5, value),
        )
    messages = []
    for n in range(2):
        face = jnp.dot(
            pack[2 * n, :, :BRICKS], edges[n, :, : 4 * COL], preferred_element_type=f32
        )
        sides = jnp.concatenate(
            [edges[n, :, 4 * COL : 5 * COL], edges[n, :, 5 * COL :]], axis=0
        )
        side = jnp.dot(pack[2 * n + 1, :, : 2 * BRICKS], sides, preferred_element_type=f32)
        messages.append(jnp.concatenate([face, side], axis=1).astype(bf16))
    m0[...] = pick(odd_x, messages[1], messages[0])
    m1[...] = pick(odd_x, messages[0], messages[1])


def edge_reader(edges):
    return lambda x, k: edges[0 if x == 0 else 1, :, k * COL : (k + 1) * COL]


def middle_kernel(
    acc, acc_side, scale, shift, cover, t0, t1, term, edges, ids_ref, weight,
    scale_two, shift_two, masked, acc_out, band_edge, result, mid, mid_side, padded, band,
):
    edge = edge_reader(edges)
    from_message = y_reader(t0, t1)
    ids = ids_ref[...]
    fill_band(weight, band)
    band_edge[:3] = band[:3]
    band_edge[3:] = band[6:]

    def put(x, y, value):
        mid[x - 1, y] = value

    def put_side(x, side, value):
        mid_side[x - 1, 0 if side < 0 else 1] = value

    for x in (1, 2):
        finish(
            acc[x], acc_side[x], x, four(scale), four(shift), cover, from_message, term,
            put, put_side,
        )

    def own(x, y):
        return mid[x - 1, y] if x in (1, 2) else edge(x, y)

    def from_y(oy, x):
        k = 0 if oy < 0 else 1
        return mid_side[x - 1, k] if x in (1, 2) else edge(x, 4 + k)

    gather_own(own, None, from_y, None, lambda ox, oy: own_select(ids, ox, oy), padded, (0,))

    def store(x_range, value):
        for n, x in enumerate(x_range):
            part = value[n * 4 * BRICKS : (n + 1) * 4 * BRICKS]
            if x in (0, 3):
                acc_out[0 if x == 0 else 1] = part
            else:
                gain, offset = four(scale_two), four(shift_two)
                put_result(part, x, gain, offset, cover, masked, result.at[x - 1])

    convolve_inner(padded, None, band, store)


def put_result(total, x, gain, offset, cover, masked, out):
    for y in range(4):
        lanes = column(x, y)
        value = total[y * BRICKS : (y + 1) * BRICKS] * gain + offset
        value = jnp.maximum(value + masked[:, lanes].astype(f32), 0.0)
        value = (value * cover[:, lanes].astype(f32)).astype(bf16)
        out[:, y * COL : (y + 1) * COL] = value


def second_kernel(
    edges, r0, r1, ids_ref, slots, band_edge, scale, shift, cover, masked, acc, middle, refined,
    outer, result, sem,
):
    copies = []

    def send(part, x):
        there = refined.at[:, x * 4 * COL : (x + 1) * 4 * COL]
        copies.append(pltpu.make_async_copy(part, there, sem.at[x]))
        copies[-1].start()

    send(middle.at[0], 1)
    send(middle.at[1], 2)
    odd_x, _ = parities()
    edge, ids = edge_reader(edges), ids_ref[...]
    base = device_base()

    def received(ox, rows, k):
        lanes = slice(k * COL, (k + 1) * COL)
        a, b = (r1, r0) if ox < 0 else (r0, r1)
        return pick(odd_x, a[rows, lanes], b[rows, lanes])

    def from_corner(ox, oy):
        return received(ox, slice(None), 4)

    def select_of(ox, oy):
        known = slots[0 if ox < 0 else 1, :1, : FACE_SLOTS + 2 * SIDE_SLOTS]
        candidates = [device_row(base), known[:, :FACE_SLOTS]]
        if oy:
            candidates += [device_row(base + id_step(0, oy)), known[:, FACE_SLOTS:]]
        return one_hot(ids, [(ox, oy, oz) for oz in (1, -1, 0)], candidates)

    gather_own(
        edge,
        lambda ox, y: received(ox, slice(None), y),
        lambda oy, x: edge(x, 4 if oy < 0 else 5),
        from_corner,
        select_of,
        outer,
        (-1, 1),
    )
    gain, offset = four(scale), four(shift)
    for n, x in enumerate((0, 3)):
        total = acc[n] + convolve_edge(outer, None, band_edge, x)
        put_result(total, x, gain, offset, cover, masked, result.at[n])
        send(result.at[n], x)
    for copy in copies:
        copy.wait()


def exchange(first, second, axis):
    return pair_exchange(first, axis, 1), pair_exchange(second, axis, 0)


def local(
    features, occupancy, adjacency, conv_one, conv_two, scale_one, shift_one,
    scale_two, shift_two, w_query, w_key, w_value, w_out,
):
    n_sy = lax.axis_size("sy")
    whole = shape(BRICKS, 64 * C)
    band_edge = shape(6, TAP, COL)
    own_acc, side_acc = shape(4, 4 * BRICKS, COL, dtype=f32), shape(4, 2 * BRICKS, COL, dtype=f32)
    band = pltpu.VMEM((9, TAP, COL), bf16)
    inner = pltpu.VMEM((4, 6, BRICKS, TAP), bf16)
    outer = pltpu.VMEM((2, 6, BRICKS, TAP), bf16)
    side_inner = pltpu.VMEM((4, 3, 2 * BRICKS, TAP), bf16)
    side_outer = pltpu.VMEM((2, 3, 2 * BRICKS, TAP), bf16)
    inputs = (features, occupancy, adjacency)
    message = shape(BRICKS, Y_LANES)
    masked, cover, tokens, meta, ids, s0, s1 = call(
        prepare_kernel,
        [
            whole, whole, shape(n_sy, BRICKS // 2, 2 * C), shape(BRICKS, 4 * C),
            shape(BRICKS, 27, dtype=jnp.int32), message, message,
        ],
        inputs,
        [pltpu.VMEM(v.shape, v.dtype) for v in inputs] + [pltpu.SemaphoreType.DMA((3,))],
        bytes_accessed=2 << 20,
        hbm_in=True,
    )
    rows = [v.reshape(1, C) for v in (scale_one, shift_one, scale_two, shift_two)]
    t0, t1 = exchange(s0, s1, "sy")
    group = lax.all_to_all(tokens, "sy", 0, 0)
    x_message = shape(BRICKS, 8 * COL)
    x0, x1 = call(
        message_kernel, [x_message] * 2, (masked, t0, t1), flops=1 << 35, bytes_accessed=1 << 20
    )
    r0, r1 = exchange(x0, x1, "sx")
    acc, acc_side, band_one, pack, slots = call(
        near_kernel,
        [
            own_acc, side_acc, band_edge, shape(4, FACE_SLOTS, 128),
            shape(2, 8, 128, dtype=jnp.int32),
        ],
        (masked, t0, t1, ids, conv_one),
        [inner, side_inner, band],
        flops=1 << 33,
        bytes_accessed=2 << 20,
    )
    total, total_side = call(
        edge_conv_kernel,
        [
            shape(2, 4 * BRICKS, COL, dtype=f32),
            shape(2, 2 * BRICKS, COL, dtype=f32),
        ],
        (masked, r0, r1, t0, t1, ids, band_one, acc, acc_side),
        [outer, side_outer],
        flops=2 * 384 * 1152 * 256,
        bytes_accessed=4 << 20,
    )
    group, total = lax.optimization_barrier((group, total))
    out_message = shape(FACE_SLOTS, 5 * COL)
    edges, m0, m1, term = call(
        edge_finish_kernel,
        [
            shape(2, BRICKS, 6 * COL), out_message, out_message,
            shape(3 * BRICKS, COL, dtype=f32),
        ],
        (
            group, w_key, w_value, w_query, w_out, t0, t1, rows[0], rows[1], cover, total,
            total_side, pack,
        ),
        flops=1 << 26,
        bytes_accessed=2 << 20,
    )
    r0, r1 = exchange(m0, m1, "sx")
    acc, band_two, half = call(
        middle_kernel,
        [shape(2, 4 * BRICKS, COL, dtype=f32), band_edge, shape(2, BRICKS, 4 * COL)],
        (
            acc, acc_side, rows[0], rows[1], cover, t0, t1, term, edges, ids, conv_two,
            rows[2], rows[3], masked,
        ),
        [
            pltpu.VMEM((2, 4, BRICKS, COL), bf16),
            pltpu.VMEM((2, 2, BRICKS, COL), bf16),
            inner,
            band,
        ],
        flops=1 << 33,
        bytes_accessed=4 << 20,
    )
    return call(
        second_kernel,
        whole,
        (
            edges, r0, r1, ids, slots, band_two, rows[2], rows[3], cover, masked, acc, half,
        ),
        [outer, pltpu.VMEM((2, BRICKS, 4 * COL), bf16), pltpu.SemaphoreType.DMA((4,))],
        flops=2 * 256 * 1152 * 256,
        bytes_accessed=3 << 20,
        hbm_out=True,
    )


def solution(mesh):
    split = P(("sx", "sy"), None)
    return jax.shard_map(
        local,
        mesh=mesh,
        in_specs=(split,) * 3 + (P(),) * 10,
        out_specs=split,
        check_vma=False,
    )
```

```python
import math

import jax
import jax.numpy as jnp
from jax import lax
from jax.experimental import pallas as pl
from jax.experimental.pallas import tpu as pltpu
from jax.sharding import PartitionSpec as P

HEADS = 2
C = 64
COL = 4 * C
BRICKS = 32
EPSILON = 1e-05
FAR = -(1 << 20)
VMEM_LIMIT = 16 * 1024 * 1024
WHOLE_VMEM = 60 * 1024 * 1024
f32, bf16 = jnp.float32, jnp.bfloat16


def call(
    kernel, out_shape, args, scratch=(), flops=0, bytes_accessed=0, hbm_in=False, hbm_out=False
):
    vmem, hbm = pl.BlockSpec(memory_space=pltpu.VMEM), pl.BlockSpec(memory_space=pl.ANY)
    return pl.pallas_call(
        kernel,
        out_shape=out_shape,
        in_specs=[hbm if hbm_in else vmem] * len(args),
        out_specs=jax.tree.map(lambda _: hbm if hbm_out else vmem, out_shape),
        scratch_shapes=list(scratch),
        compiler_params=pltpu.CompilerParams(
            vmem_limit_bytes=WHOLE_VMEM if hbm_in else VMEM_LIMIT
        ),
        cost_estimate=pl.CostEstimate(
            flops=flops, bytes_accessed=bytes_accessed, transcendentals=0
        ),
    )(*args)


def shape(*dims, dtype=bf16):
    return jax.ShapeDtypeStruct(dims, dtype)


def column(x, y):
    return slice((x * 4 + y) * COL, (x * 4 + y + 1) * COL)


def face_x(ref, x):
    return ref[:, x * 4 * COL : (x + 1) * 4 * COL]


def pick(flag, a, b):
    return jnp.where(flag, a, b)


def parities():
    odd_x = lax.rem(lax.axis_index("sx"), 2) == 1
    odd_y = lax.rem(lax.axis_index("sy"), 2) == 1
    return odd_x, odd_y


def pair_exchange(value, axis, phase):
    n_x, n_y = lax.axis_size("sx"), lax.axis_size("sy")

    def partner(x, y):
        s, count = (x, n_x) if axis == "sx" else (y, n_y)
        if phase == 1 and s in (0, count - 1):
            return (x, y ^ 1) if axis == "sx" else (x ^ 1, y)
        s = s ^ 1 if phase == 0 else ((s + 1) ^ 1) - 1
        return (s, y) if axis == "sx" else (x, s)

    pairs = []
    for x in range(n_x):
        for y in range(n_y):
            there = partner(x, y)
            pairs.append((x * n_y + y, there[0] * n_y + there[1]))
    return lax.ppermute(value, ("sx", "sy"), pairs)


def device_base():
    return (lax.axis_index("sx") * lax.axis_size("sy") + lax.axis_index("sy")) * BRICKS


def id_step(dx, dy):
    return (dx * lax.axis_size("sy") + dy) * BRICKS


def device_row(base):
    return jnp.bitwise_and(lax.broadcasted_iota(jnp.int32, (1, BRICKS), 1), BRICKS - 1) + base


def one_hot(ids, offsets, candidates):
    candidate = candidates[0]
    if len(candidates) > 1:
        candidate = jnp.concatenate(candidates, axis=1)
    candidate = jnp.broadcast_to(candidate, (BRICKS, candidate.shape[1]))
    rows = [
        (ids[:, o : o + 1] == candidate).astype(f32).astype(bf16)
        for o in ((ox + 1) * 9 + (oy + 1) * 3 + (oz + 1) for ox, oy, oz in offsets)
    ]
    return jnp.concatenate(rows, axis=0)


def owner_marks(ids, base):
    hit = jnp.logical_and(ids >= base, ids < base + BRICKS)
    return jnp.max(hit.astype(f32), axis=1, keepdims=True)


def compaction(marks, slots):
    row = lax.broadcasted_iota(jnp.int32, (BRICKS, BRICKS), 0)
    lane = lax.broadcasted_iota(jnp.int32, (BRICKS, BRICKS), 1)
    rank = jnp.sum(jnp.where(row < lane, marks, 0.0), axis=0, keepdims=True)
    marked = jnp.sum(jnp.where(row == lane, marks, 0.0), axis=0, keepdims=True)
    slot = lax.broadcasted_iota(jnp.int32, (slots, BRICKS), 0).astype(f32)
    return jnp.where(slot == rank, marked, 0.0)


def slot_ids(ids, base, offsets, slots):
    candidate = jnp.broadcast_to(device_row(base), (BRICKS, BRICKS))
    hit = jnp.zeros((BRICKS, BRICKS), f32)
    for ox, oy, oz in offsets:
        o = (ox + 1) * 9 + (oy + 1) * 3 + (oz + 1)
        hit = jnp.maximum(hit, (ids[:, o : o + 1] == candidate).astype(f32))
    marked = jnp.broadcast_to(jnp.max(hit, axis=0, keepdims=True), (8, BRICKS))
    row = lax.broadcasted_iota(jnp.int32, (BRICKS, BRICKS), 0)
    lane = lax.broadcasted_iota(jnp.int32, (BRICKS, BRICKS), 1)
    before = (row < lane).astype(f32).astype(bf16)
    rank = jnp.dot(marked.astype(bf16), before, preferred_element_type=f32)
    slot = lax.broadcasted_iota(jnp.int32, (slots, BRICKS), 0).astype(f32)
    pack = jnp.where(slot == rank[:1], marked[:1], 0.0).astype(bf16)
    count = lax.broadcasted_iota(jnp.int32, (8, BRICKS), 1).astype(f32) + 1.0
    local_id = lax.dot_general(
        count.astype(bf16), pack, (((1,), (1,)), ((), ())), preferred_element_type=f32
    ).astype(jnp.int32)
    return jnp.where(local_id > 0, local_id - 1 + base, 2 * FAR)


def put_column(select, parts, core, store):
    table = parts[0] if len(parts) == 1 else jnp.concatenate(parts, axis=0)
    got = jnp.dot(select, table, preferred_element_type=f32).astype(bf16)
    lane_low = lax.broadcasted_iota(jnp.int32, (BRICKS, 128), 1) < C
    ends = jnp.where(lane_low, got[:BRICKS, :128], got[BRICKS : 2 * BRICKS, 128:])
    store(got[2 * BRICKS :] if core is None else core, ends)


NEAR, BEHIND, META, Y_LANES = 0, 4 * COL, 8 * COL, 9 * COL


def prepare_kernel(
    feat_hbm, occ_hbm, adj_hbm,
    masked_hbm, cover_hbm, tokens_hbm, meta_hbm, ids_hbm, s0_hbm, s1_hbm,
    masked, cover, tokens_all, meta, ids, s0, s1, feat, occ, adj, in_sems, out_sems,
):
    planes = [slice(x * 4 * COL, (x + 1) * 4 * COL) for x in range(4)]
    pairs = [(occ_hbm, occ), (adj_hbm, adj)]
    pairs += [(feat_hbm.at[:, lanes], feat.at[:, lanes]) for lanes in planes]
    copies = [pltpu.make_async_copy(a, b, in_sems.at[k]) for k, (a, b) in enumerate(pairs)]
    for copy in copies:
        copy.start()
    sent = []

    def send(source, target):
        sent.append(pltpu.make_async_copy(source, target, out_sems.at[len(sent)]))
        sent[-1].start()

    copies[0].wait()
    occupied = occ[...].astype(f32).astype(bf16)
    row = lax.broadcasted_iota(jnp.int32, (64, COL), 0)
    voxel = lax.shift_right_logical(lax.broadcasted_iota(jnp.int32, (64, COL), 1), 6)
    for k in range(16):
        spread = (row == voxel + 4 * k).astype(f32).astype(bf16)
        cov = jnp.dot(occupied, spread, preferred_element_type=f32).astype(bf16)
        cover[:, k * COL : (k + 1) * COL] = cov
    send(cover, cover_hbm)
    copies[1].wait()
    number = adj[...]
    ids[...] = jnp.where(number < 0, FAR, number)
    send(ids, ids_hbm)
    total = jnp.zeros((BRICKS, 128), f32)
    for x in range(4):
        copies[2 + x].wait()
        for y in range(4):
            lanes = column(x, y)
            part = feat[:, lanes] * cover[:, lanes]
            masked[:, lanes] = part
            wide = part.astype(f32)
            total = total + wide[:, :128] + wide[:, 128:]
        send(masked.at[:, planes[x]], masked_hbm.at[:, planes[x]])
    summed = total[:, :C] + total[:, C:]
    tokens = (summed / 8.0).astype(bf16)
    half = BRICKS // 2
    packed = jnp.concatenate([tokens[:half], tokens[half:]], axis=1)
    tokens_all[...] = jnp.broadcast_to(packed[None], tokens_all.shape)
    send(tokens_all, tokens_hbm)
    number = number + 1
    high = lax.shift_right_logical(number, 6).astype(f32).astype(bf16)
    low = jnp.bitwise_and(number, 63).astype(f32).astype(bf16)
    gap = jnp.zeros((BRICKS, C - 27), bf16)
    about = jnp.concatenate([high, gap, low, gap, occupied, tokens], axis=1)
    meta[...] = about
    send(meta, meta_hbm)
    _, odd_y = parities()

    def write(out, near, behind):
        for place, y in ((NEAR, near), (BEHIND, behind)):
            for x in range(4):
                out[:, place + x * COL : place + (x + 1) * COL] = masked[:, column(x, y)]
        out[:, META:] = about

    @pl.when(odd_y)
    def _():
        write(s0, 3, 2)
        write(s1, 0, 1)

    @pl.when(jnp.logical_not(odd_y))
    def _():
        write(s0, 0, 1)
        write(s1, 3, 2)

    send(s0, s0_hbm)
    send(s1, s1_hbm)
    for copy in sent:
        copy.wait()


def fill_band(weight, band):
    zero = jnp.zeros((C, C), bf16)
    for t in range(9):
        for r, z_in in enumerate((0, 1, 2, 3, 4, -1)):
            blocks = []
            for z_out in range(4):
                tap = z_in - z_out + 1
                blocks.append(weight[t * 3 + tap] if 0 <= tap < 3 else zero)
            band[t, r * C : (r + 1) * C, :] = jnp.concatenate(blocks, axis=1)


def message_kernel(masked, t0, t1, x0, x1):
    odd_x, odd_y = parities()

    def write(out, x):
        out[:, : 4 * COL] = face_x(masked, x)
        place = 4 * COL
        for a, b in ((t1, t0), (t0, t1)):
            for plane in (NEAR, BEHIND):
                lanes = slice(plane + x * COL, plane + (x + 1) * COL)
                out[:, place : place + COL] = pick(odd_y, a[:, lanes], b[:, lanes])
                place += COL

    @pl.when(odd_x)
    def _():
        write(x0, 3)
        write(x1, 0)

    @pl.when(jnp.logical_not(odd_x))
    def _():
        write(x0, 0)
        write(x1, 3)


def place_x(ox, x):
    return x if ox == 0 else (0 if ox < 0 else 1)


def sources_of(ox, oy):
    sources = [(0, 0)]
    if ox:
        sources.append((ox, 0))
    if oy:
        sources.append((0, oy))
    if ox and oy:
        sources.append((ox, oy))
    return sources


def own_select(ids, ox, oy):
    base = device_base()
    offsets = [(ox, oy, oz) for oz in ((1, -1) if ox == 0 and oy == 0 else (1, -1, 0))]
    return one_hot(ids, offsets, [device_row(base + id_step(dx, dy)) for dx, dy in sources_of(ox, oy)])


def side_select(ids, side, ox):
    here, there = device_base(), device_base() + id_step(0, side)
    bases = [0] if ox == 0 else [0, id_step(ox, 0)]
    outer = [device_row(here + step) for step in bases]
    inner = [device_row(there + step) for step in bases]
    offsets = [(ox, 0, oz) for oz in ((1, -1) if ox == 0 else (1, -1, 0))]
    return (
        one_hot(ids, offsets, inner),
        one_hot(ids, [(ox, -side, oz) for oz in (1, -1, 0)], outer),
    )


def gather_own(own, from_x, from_y, from_corner, select_of, padded, x_offsets):
    for ox in x_offsets:
        for oy in (-1, 0, 1):
            centre = ox == 0 and oy == 0
            select = select_of(ox, oy)
            for x in {-1: (3,), 0: range(4), 1: (0,)}[ox]:
                for y in {-1: (3,), 0: range(4), 1: (0,)}[oy]:
                    parts = [own(x, y)]
                    if ox:
                        parts.append(from_x(ox, y))
                    if oy:
                        parts.append(from_y(oy, x))
                    if ox and oy:
                        parts.append(from_corner(ox, oy))
                    px = place_x(ox, x)
                    py = {-1: 0, 0: 1 + y, 1: 5}[oy]

                    def store(core, ends, px=px, py=py):
                        padded[px, py, :, :COL] = core
                        padded[px, py, :, COL:] = ends

                    put_column(select, parts, parts[0] if centre else None, store)


def gather_side(own, from_x, from_message, side, select_of, padded, x_offsets):
    mine = {-1: 0, 1: 3}[side]
    rows = slice(0, BRICKS) if side < 0 else slice(BRICKS, 2 * BRICKS)
    for ox in x_offsets:
        select_inner, select_outer = select_of(side, ox)
        for x in {-1: (3,), 0: range(4), 1: (0,)}[ox]:
            px = place_x(ox, x)
            for place, py in ((BEHIND, 1 + side), (NEAR, 1), (None, 1 - side)):

                def store(core, ends, px=px, py=py):
                    padded[px, py, rows, :COL] = core
                    padded[px, py, rows, COL:] = ends

                if place is None:
                    parts = [own(x, mine)]
                    if ox:
                        parts.append(from_x(ox, mine))
                    put_column(select_outer, parts, None, store)
                    continue
                parts = [from_message(side, place + x * COL)]
                if ox:
                    parts.append(from_x(ox, corner_place(side, place)))
                put_column(select_inner, parts, parts[0] if ox == 0 else None, store)


def corner_place(side, plane):
    return 4 + (0 if side < 0 else 2) + (0 if plane == NEAR else 1)


TAP = 6 * C


def taps(padded, side, x_range, first, count):
    parts = []
    for t in range(first, first + count):
        i, j = t // 3, t % 3
        rows = [padded[x + i, j : j + 4].reshape(4 * BRICKS, TAP) for x in x_range]
        if side is not None:
            rows += [side[x + i, j] for x in x_range]
        parts.append(jnp.concatenate(rows, axis=0))
    return jnp.concatenate(parts, axis=1)


def product(lhs, band, first, count):
    rhs = band[first : first + count].reshape(count * TAP, COL)
    return jnp.dot(lhs, rhs, preferred_element_type=f32)


def convolve_inner(inner, side, band, store):
    store((1, 2), product(taps(inner, side, (0, 1), 0, 9), band, 0, 9))
    store((0,), product(taps(inner, side, (-1,), 3, 6), band, 3, 6))
    store((3,), product(taps(inner, side, (2,), 0, 6), band, 0, 6))


def convolve_edge(outer, side, band, x):
    i, place = (0, 0) if x == 0 else (2, 1)
    return product(taps(outer, side, (place - i,), 3 * i, 3), band, 0 if x == 0 else 3, 3)


def four(ref):
    return jnp.concatenate([ref[...]] * 4, axis=1)


def project(tokens, weight):
    return jnp.dot(tokens, weight, preferred_element_type=f32).astype(bf16)


def attention(tokens, packed, w_key, w_value, w_query, w_out):
    group = jnp.concatenate([packed[:, :C], packed[:, C:]], axis=0)
    kv = project(group, jnp.concatenate([w_key, w_value], axis=1))
    queries = project(tokens, w_query)
    rows = queries.shape[0]
    wide = jnp.concatenate([queries, jnp.zeros_like(queries)], axis=1).astype(f32)
    lane = lax.broadcasted_iota(jnp.int32, (rows, 2 * C), 1)
    per_head = [jnp.where(lax.shift_right_logical(lane, 5) == h, wide, 0.0) for h in range(HEADS)]
    wide = jnp.concatenate(per_head, axis=0).astype(bf16)
    logits = lax.dot_general(
        wide, kv, (((1,), (1,)), ((), ())), preferred_element_type=f32
    ) * (1.0 / math.sqrt(C // HEADS))
    top = jnp.max(logits, axis=1, keepdims=True)
    weight = jnp.exp(logits - top)
    total = jnp.sum(weight, axis=1, keepdims=True)
    coarse = weight.astype(bf16)
    fine = (weight - coarse.astype(f32)).astype(bf16)
    mixed = jnp.dot(coarse, kv, preferred_element_type=f32)
    mixed = mixed + jnp.dot(fine, kv, preferred_element_type=f32)
    mixed = mixed / total
    context = jnp.where(lane < C + C // 2, mixed[:rows], mixed[rows:])
    context = jnp.where(lane < C, 0.0, context)
    mean = jnp.sum(context * context, axis=1, keepdims=True) / C
    attended = (context / jnp.sqrt(mean + EPSILON)).astype(bf16)
    w_out = jnp.concatenate([w_out] * 4, axis=1)
    return jnp.dot(attended[:, C:], w_out, preferred_element_type=f32)


def y_reader(t0, t1):
    _, odd_y = parities()

    def from_y(oy, place, width=COL):
        lanes = slice(place, place + width)
        a, b = (t1, t0) if oy < 0 else (t0, t1)
        return pick(odd_y, a[:, lanes], b[:, lanes])

    return from_y


def x_reader(r0, r1):
    odd_x, _ = parities()

    def from_x(ox, k):
        lanes = slice(k * COL, (k + 1) * COL)
        a, b = (r1, r0) if ox < 0 else (r0, r1)
        return pick(odd_x, a[:, lanes], b[:, lanes])

    return from_x


def side_ids(about):
    high, low = about[:, :C].astype(f32), about[:, C : 2 * C].astype(f32)
    number = (high * 64.0 + low).astype(jnp.int32) - 1
    return jnp.where(number < 0, FAR, number)


def global_term(group, w_key, w_value, w_query, w_out):
    count = group.shape[0]
    here = lax.axis_index("sy")
    tokens = []
    for step in (0, count - 1, 1):
        packed = group[lax.rem(here + step, count)]
        tokens += [packed[:, :C], packed[:, C:]]
    packed = group[...].reshape(-1, 2 * C)
    tokens = jnp.concatenate(tokens, axis=0)
    return attention(tokens, packed, w_key[...], w_value[...], w_query[...], w_out[...])


FACE_SLOTS, SIDE_SLOTS = 16, 8


def near_kernel(
    masked, t0, t1, ids_ref, weight, acc, acc_side, band_edge, pack, slots, inner, side_inner,
    band,
):
    from_message = y_reader(t0, t1)
    ids = ids_ref[...]

    def own(x, y):
        return masked[:, column(x, y)]

    def from_y(oy, x):
        return from_message(oy, NEAR + x * COL)

    fill_band(weight, band)
    gather_own(own, None, from_y, None, lambda ox, oy: own_select(ids, ox, oy), inner, (0,))
    numbers = {}
    for side in (-1, 1):
        number = numbers[side] = side_ids(from_message(side, META))
        gather_side(
            own, None, from_message, side,
            lambda side, ox, number=number: side_select(number, side, ox), side_inner, (0,),
        )

    base = device_base()
    for k, ox in enumerate((-1, 1)):
        face = [(ox, oy, oz) for oy in (-1, 0, 1) for oz in (-1, 0, 1)]
        parts = [slot_ids(ids, base + id_step(ox, 0), face, FACE_SLOTS)]
        for oy in (-1, 1):
            corner = [(ox, oy, oz) for oz in (-1, 0, 1)]
            parts.append(slot_ids(ids, base + id_step(ox, oy), corner, SIDE_SLOTS))
        slots[k, :, : FACE_SLOTS + 2 * SIDE_SLOTS] = jnp.concatenate(parts, axis=1)

    def store(x_range, value):
        count = len(x_range)
        for n, x in enumerate(x_range):
            acc[x] = value[n * 4 * BRICKS : (n + 1) * 4 * BRICKS]
            rows = (4 * count + 2 * n) * BRICKS
            acc_side[x] = value[rows : rows + 2 * BRICKS]

    convolve_inner(inner, side_inner, band, store)
    band_edge[:3] = band[:3]
    band_edge[3:] = band[6:]
    for k, ox in enumerate((-1, 1)):
        there = device_base() + id_step(ox, 0)
        pack[2 * k, :, :BRICKS] = compaction(owner_marks(ids, there), FACE_SLOTS).astype(bf16)
        sides = [compaction(owner_marks(numbers[side], there), SIDE_SLOTS) for side in (-1, 1)]
        gap = jnp.zeros_like(sides[0])
        low = jnp.concatenate([sides[0], gap], axis=1)
        high = jnp.concatenate([gap, sides[1]], axis=1)
        both = jnp.concatenate([low, high], axis=0)
        pack[2 * k + 1, :, : 2 * BRICKS] = both.astype(bf16)


def finish(acc, acc_side, x, gain, offset, cover, from_message, term, store, store_side):
    def one(part, which, cov):
        first = jnp.maximum(part * gain + offset, 0.0)
        return ((first + term[which * BRICKS : (which + 1) * BRICKS]) * cov).astype(bf16)

    row = lax.broadcasted_iota(jnp.int32, (64, COL), 0)
    voxel = lax.shift_right_logical(lax.broadcasted_iota(jnp.int32, (64, COL), 1), 6)
    for y in range(4):
        cov = cover[:, column(x, y)].astype(f32)
        store(x, y, one(acc[y * BRICKS : (y + 1) * BRICKS], 0, cov))
    for k, side in enumerate((-1, 1)):
        occupied = from_message(side, META)[:, 2 * C : 3 * C]
        spread = (row == voxel + (x * 16 + (3 - 3 * k) * 4)).astype(f32).astype(bf16)
        cov = jnp.dot(occupied, spread, preferred_element_type=f32)
        store_side(x, side, one(acc_side[k * BRICKS : (k + 1) * BRICKS], 1 + k, cov))


def edge_conv_kernel(
    masked, r0, r1, t0, t1, ids_ref, band_edge, acc, acc_side, total, total_side,
    outer, side_outer,
):
    from_message, from_x = y_reader(t0, t1), x_reader(r0, r1)
    ids = ids_ref[...]

    def own(x, y):
        return masked[:, column(x, y)]

    gather_own(
        own,
        from_x,
        lambda oy, x: from_message(oy, NEAR + x * COL),
        lambda ox, oy: from_x(ox, corner_place(oy, NEAR)),
        lambda ox, oy: own_select(ids, ox, oy),
        outer,
        (-1, 1),
    )
    for side in (-1, 1):
        number = side_ids(from_message(side, META))
        gather_side(
            own, from_x, from_message, side,
            lambda side, ox, number=number: side_select(number, side, ox), side_outer, (-1, 1),
        )
    for n, x in enumerate((0, 3)):
        more = convolve_edge(outer, side_outer, band_edge, x)
        total[n] = acc[x] + more[: 4 * BRICKS]
        total_side[n] = acc_side[x] + more[4 * BRICKS :]


def edge_finish_kernel(
    group, w_key, w_value, w_query, w_out, t0, t1, scale, shift, cover, total, total_side, pack,
    edges, m0, m1, term_out,
):
    odd_x, _ = parities()
    from_message = y_reader(t0, t1)
    term = global_term(group, w_key, w_value, w_query, w_out)
    term_out[...] = term

    def put(x, k, value):
        edges[0 if x == 0 else 1, :, k * COL : (k + 1) * COL] = value

    for n, x in enumerate((0, 3)):
        finish(
            total[n], total_side[n], x, four(scale), four(shift), cover, from_message, term,
            put, lambda x, side, value: put(x, 4 if side < 0 else 5, value),
        )
    messages = []
    for n in range(2):
        face = jnp.dot(
            pack[2 * n, :, :BRICKS], edges[n, :, : 4 * COL], preferred_element_type=f32
        )
        sides = jnp.concatenate(
            [edges[n, :, 4 * COL : 5 * COL], edges[n, :, 5 * COL :]], axis=0
        )
        side = jnp.dot(pack[2 * n + 1, :, : 2 * BRICKS], sides, preferred_element_type=f32)
        messages.append(jnp.concatenate([face, side], axis=1).astype(bf16))
    m0[...] = pick(odd_x, messages[1], messages[0])
    m1[...] = pick(odd_x, messages[0], messages[1])


def edge_reader(edges):
    return lambda x, k: edges[0 if x == 0 else 1, :, k * COL : (k + 1) * COL]


def middle_kernel(
    acc, acc_side, scale, shift, cover, t0, t1, term, edges, ids_ref, weight,
    scale_two, shift_two, masked, acc_out, band_edge, result, mid, mid_side, padded, band,
):
    edge = edge_reader(edges)
    from_message = y_reader(t0, t1)
    ids = ids_ref[...]
    fill_band(weight, band)
    band_edge[:3] = band[:3]
    band_edge[3:] = band[6:]

    def put(x, y, value):
        mid[x - 1, y] = value

    def put_side(x, side, value):
        mid_side[x - 1, 0 if side < 0 else 1] = value

    for x in (1, 2):
        finish(
            acc[x], acc_side[x], x, four(scale), four(shift), cover, from_message, term,
            put, put_side,
        )

    def own(x, y):
        return mid[x - 1, y] if x in (1, 2) else edge(x, y)

    def from_y(oy, x):
        k = 0 if oy < 0 else 1
        return mid_side[x - 1, k] if x in (1, 2) else edge(x, 4 + k)

    gather_own(own, None, from_y, None, lambda ox, oy: own_select(ids, ox, oy), padded, (0,))

    def store(x_range, value):
        for n, x in enumerate(x_range):
            part = value[n * 4 * BRICKS : (n + 1) * 4 * BRICKS]
            if x in (0, 3):
                acc_out[0 if x == 0 else 1] = part
            else:
                gain, offset = four(scale_two), four(shift_two)
                put_result(part, x, gain, offset, cover, masked, result.at[x - 1])

    convolve_inner(padded, None, band, store)


def put_result(total, x, gain, offset, cover, masked, out):
    for y in range(4):
        lanes = column(x, y)
        value = total[y * BRICKS : (y + 1) * BRICKS] * gain + offset
        value = jnp.maximum(value + masked[:, lanes].astype(f32), 0.0)
        value = (value * cover[:, lanes].astype(f32)).astype(bf16)
        out[:, y * COL : (y + 1) * COL] = value


def second_kernel(
    edges, r0, r1, ids_ref, slots, band_edge, scale, shift, cover, masked, acc, middle, refined,
    outer, result, sem,
):
    copies = []

    def send(part, x):
        there = refined.at[:, x * 4 * COL : (x + 1) * 4 * COL]
        copies.append(pltpu.make_async_copy(part, there, sem.at[x]))
        copies[-1].start()

    send(middle.at[0], 1)
    send(middle.at[1], 2)
    odd_x, _ = parities()
    edge, ids = edge_reader(edges), ids_ref[...]
    base = device_base()

    def received(ox, rows, k):
        lanes = slice(k * COL, (k + 1) * COL)
        a, b = (r1, r0) if ox < 0 else (r0, r1)
        return pick(odd_x, a[rows, lanes], b[rows, lanes])

    def from_corner(ox, oy):
        return received(ox, slice(None), 4)

    def select_of(ox, oy):
        known = slots[0 if ox < 0 else 1, :1, : FACE_SLOTS + 2 * SIDE_SLOTS]
        candidates = [device_row(base), known[:, :FACE_SLOTS]]
        if oy:
            candidates += [device_row(base + id_step(0, oy)), known[:, FACE_SLOTS:]]
        return one_hot(ids, [(ox, oy, oz) for oz in (1, -1, 0)], candidates)

    gather_own(
        edge,
        lambda ox, y: received(ox, slice(None), y),
        lambda oy, x: edge(x, 4 if oy < 0 else 5),
        from_corner,
        select_of,
        outer,
        (-1, 1),
    )
    gain, offset = four(scale), four(shift)
    for n, x in enumerate((0, 3)):
        total = acc[n] + convolve_edge(outer, None, band_edge, x)
        put_result(total, x, gain, offset, cover, masked, result.at[n])
        send(result.at[n], x)
    for copy in copies:
        copy.wait()


def exchange(first, second, axis):
    return pair_exchange(first, axis, 1), pair_exchange(second, axis, 0)


def local(
    features, occupancy, adjacency, conv_one, conv_two, scale_one, shift_one,
    scale_two, shift_two, w_query, w_key, w_value, w_out,
):
    n_sy = lax.axis_size("sy")
    whole = shape(BRICKS, 64 * C)
    band_edge = shape(6, TAP, COL)
    own_acc, side_acc = shape(4, 4 * BRICKS, COL, dtype=f32), shape(4, 2 * BRICKS, COL, dtype=f32)
    band = pltpu.VMEM((9, TAP, COL), bf16)
    inner = pltpu.VMEM((4, 6, BRICKS, TAP), bf16)
    outer = pltpu.VMEM((2, 6, BRICKS, TAP), bf16)
    side_inner = pltpu.VMEM((4, 3, 2 * BRICKS, TAP), bf16)
    side_outer = pltpu.VMEM((2, 3, 2 * BRICKS, TAP), bf16)
    inputs = (features, occupancy, adjacency)
    message = shape(BRICKS, Y_LANES)
    prepared = [
        whole, whole, shape(n_sy, BRICKS // 2, 2 * C), shape(BRICKS, 4 * C),
        shape(BRICKS, 27, dtype=jnp.int32), message, message,
    ]
    masked, cover, tokens, meta, ids, s0, s1 = call(
        prepare_kernel,
        prepared,
        inputs,
        [pltpu.VMEM(v.shape, v.dtype) for v in (*prepared, *inputs)]
        + [pltpu.SemaphoreType.DMA((6,)), pltpu.SemaphoreType.DMA((10,))],
        bytes_accessed=2 << 20,
        hbm_in=True,
        hbm_out=True,
    )
    rows = [v.reshape(1, C) for v in (scale_one, shift_one, scale_two, shift_two)]
    t0, t1 = exchange(s0, s1, "sy")
    group = lax.all_to_all(tokens, "sy", 0, 0)
    x_message = shape(BRICKS, 8 * COL)
    x0, x1 = call(
        message_kernel, [x_message] * 2, (masked, t0, t1), flops=1 << 35, bytes_accessed=1 << 20
    )
    r0, r1 = exchange(x0, x1, "sx")
    acc, acc_side, band_one, pack, slots = call(
        near_kernel,
        [
            own_acc, side_acc, band_edge, shape(4, FACE_SLOTS, 128),
            shape(2, 8, 128, dtype=jnp.int32),
        ],
        (masked, t0, t1, ids, conv_one),
        [inner, side_inner, band],
        flops=1 << 33,
        bytes_accessed=2 << 20,
    )
    total, total_side = call(
        edge_conv_kernel,
        [
            shape(2, 4 * BRICKS, COL, dtype=f32),
            shape(2, 2 * BRICKS, COL, dtype=f32),
        ],
        (masked, r0, r1, t0, t1, ids, band_one, acc, acc_side),
        [outer, side_outer],
        flops=2 * 384 * 1152 * 256,
        bytes_accessed=4 << 20,
    )
    group, total = lax.optimization_barrier((group, total))
    out_message = shape(FACE_SLOTS, 5 * COL)
    edges, m0, m1, term = call(
        edge_finish_kernel,
        [
            shape(2, BRICKS, 6 * COL), out_message, out_message,
            shape(3 * BRICKS, COL, dtype=f32),
        ],
        (
            group, w_key, w_value, w_query, w_out, t0, t1, rows[0], rows[1], cover, total,
            total_side, pack,
        ),
        flops=1 << 26,
        bytes_accessed=2 << 20,
    )
    r0, r1 = exchange(m0, m1, "sx")
    acc, band_two, half = call(
        middle_kernel,
        [shape(2, 4 * BRICKS, COL, dtype=f32), band_edge, shape(2, BRICKS, 4 * COL)],
        (
            acc, acc_side, rows[0], rows[1], cover, t0, t1, term, edges, ids, conv_two,
            rows[2], rows[3], masked,
        ),
        [
            pltpu.VMEM((2, 4, BRICKS, COL), bf16),
            pltpu.VMEM((2, 2, BRICKS, COL), bf16),
            inner,
            band,
        ],
        flops=1 << 33,
        bytes_accessed=4 << 20,
    )
    return call(
        second_kernel,
        whole,
        (
            edges, r0, r1, ids, slots, band_two, rows[2], rows[3], cover, masked, acc, half,
        ),
        [outer, pltpu.VMEM((2, BRICKS, 4 * COL), bf16), pltpu.SemaphoreType.DMA((4,))],
        flops=2 * 256 * 1152 * 256,
        bytes_accessed=3 << 20,
        hbm_out=True,
    )


def solution(mesh):
    split = P(("sx", "sy"), None)
    return jax.shard_map(
        local,
        mesh=mesh,
        in_specs=(split,) * 3 + (P(),) * 10,
        out_specs=split,
        check_vma=False,
    )
```

```python
import math

import jax
import jax.numpy as jnp
from jax import lax
from jax.experimental import pallas as pl
from jax.experimental.pallas import tpu as pltpu
from jax.sharding import PartitionSpec as P

HEADS = 2
C = 64
COL = 4 * C
BRICKS = 32
EPSILON = 1e-05
FAR = -(1 << 20)
VMEM_LIMIT = 16 * 1024 * 1024
WHOLE_VMEM = 60 * 1024 * 1024
f32, bf16 = jnp.float32, jnp.bfloat16


def call(
    kernel, out_shape, args, scratch=(), flops=0, bytes_accessed=0, hbm_in=False, hbm_out=False
):
    vmem, hbm = pl.BlockSpec(memory_space=pltpu.VMEM), pl.BlockSpec(memory_space=pl.ANY)
    return pl.pallas_call(
        kernel,
        out_shape=out_shape,
        in_specs=[hbm if hbm_in else vmem] * len(args),
        out_specs=jax.tree.map(lambda _: hbm if hbm_out else vmem, out_shape),
        scratch_shapes=list(scratch),
        compiler_params=pltpu.CompilerParams(
            vmem_limit_bytes=WHOLE_VMEM if hbm_in else VMEM_LIMIT
        ),
        cost_estimate=pl.CostEstimate(
            flops=flops, bytes_accessed=bytes_accessed, transcendentals=0
        ),
    )(*args)


def shape(*dims, dtype=bf16):
    return jax.ShapeDtypeStruct(dims, dtype)


def column(x, y):
    return slice((x * 4 + y) * COL, (x * 4 + y + 1) * COL)


def face_x(ref, x):
    return ref[:, x * 4 * COL : (x + 1) * 4 * COL]


def pick(flag, a, b):
    return jnp.where(flag, a, b)


def parities():
    odd_x = lax.rem(lax.axis_index("sx"), 2) == 1
    odd_y = lax.rem(lax.axis_index("sy"), 2) == 1
    return odd_x, odd_y


def pair_exchange(value, axis, phase):
    n_x, n_y = lax.axis_size("sx"), lax.axis_size("sy")

    def partner(x, y):
        s, count = (x, n_x) if axis == "sx" else (y, n_y)
        if phase == 1 and s in (0, count - 1):
            return (x, y ^ 1) if axis == "sx" else (x ^ 1, y)
        s = s ^ 1 if phase == 0 else ((s + 1) ^ 1) - 1
        return (s, y) if axis == "sx" else (x, s)

    pairs = []
    for x in range(n_x):
        for y in range(n_y):
            there = partner(x, y)
            pairs.append((x * n_y + y, there[0] * n_y + there[1]))
    return lax.ppermute(value, ("sx", "sy"), pairs)


def device_base():
    return (lax.axis_index("sx") * lax.axis_size("sy") + lax.axis_index("sy")) * BRICKS


def id_step(dx, dy):
    return (dx * lax.axis_size("sy") + dy) * BRICKS


def device_row(base):
    return jnp.bitwise_and(lax.broadcasted_iota(jnp.int32, (1, BRICKS), 1), BRICKS - 1) + base


def one_hot(ids, offsets, candidates):
    candidate = candidates[0]
    if len(candidates) > 1:
        candidate = jnp.concatenate(candidates, axis=1)
    candidate = jnp.broadcast_to(candidate, (BRICKS, candidate.shape[1]))
    rows = [
        (ids[:, o : o + 1] == candidate).astype(f32).astype(bf16)
        for o in ((ox + 1) * 9 + (oy + 1) * 3 + (oz + 1) for ox, oy, oz in offsets)
    ]
    return jnp.concatenate(rows, axis=0)


def owner_marks(ids, base):
    hit = jnp.logical_and(ids >= base, ids < base + BRICKS)
    return jnp.max(hit.astype(f32), axis=1, keepdims=True)


def compaction(marks, slots):
    row = lax.broadcasted_iota(jnp.int32, (BRICKS, BRICKS), 0)
    lane = lax.broadcasted_iota(jnp.int32, (BRICKS, BRICKS), 1)
    rank = jnp.sum(jnp.where(row < lane, marks, 0.0), axis=0, keepdims=True)
    marked = jnp.sum(jnp.where(row == lane, marks, 0.0), axis=0, keepdims=True)
    slot = lax.broadcasted_iota(jnp.int32, (slots, BRICKS), 0).astype(f32)
    return jnp.where(slot == rank, marked, 0.0)


def slot_ids(ids, base, offsets, slots):
    candidate = jnp.broadcast_to(device_row(base), (BRICKS, BRICKS))
    hit = jnp.zeros((BRICKS, BRICKS), f32)
    for ox, oy, oz in offsets:
        o = (ox + 1) * 9 + (oy + 1) * 3 + (oz + 1)
        hit = jnp.maximum(hit, (ids[:, o : o + 1] == candidate).astype(f32))
    marked = jnp.broadcast_to(jnp.max(hit, axis=0, keepdims=True), (8, BRICKS))
    row = lax.broadcasted_iota(jnp.int32, (BRICKS, BRICKS), 0)
    lane = lax.broadcasted_iota(jnp.int32, (BRICKS, BRICKS), 1)
    before = (row < lane).astype(f32).astype(bf16)
    rank = jnp.dot(marked.astype(bf16), before, preferred_element_type=f32)
    slot = lax.broadcasted_iota(jnp.int32, (slots, BRICKS), 0).astype(f32)
    pack = jnp.where(slot == rank[:1], marked[:1], 0.0).astype(bf16)
    count = lax.broadcasted_iota(jnp.int32, (8, BRICKS), 1).astype(f32) + 1.0
    local_id = lax.dot_general(
        count.astype(bf16), pack, (((1,), (1,)), ((), ())), preferred_element_type=f32
    ).astype(jnp.int32)
    return jnp.where(local_id > 0, local_id - 1 + base, 2 * FAR)


def put_column(select, parts, core, store):
    table = parts[0] if len(parts) == 1 else jnp.concatenate(parts, axis=0)
    got = jnp.dot(select, table, preferred_element_type=f32).astype(bf16)
    lane_low = lax.broadcasted_iota(jnp.int32, (BRICKS, 128), 1) < C
    ends = jnp.where(lane_low, got[:BRICKS, :128], got[BRICKS : 2 * BRICKS, 128:])
    store(got[2 * BRICKS :] if core is None else core, ends)


NEAR, BEHIND, META, Y_LANES = 0, 4 * COL, 8 * COL, 9 * COL


def prepare_kernel(
    feat_hbm, occ_hbm, adj_hbm,
    masked_hbm, cover_hbm, tokens_hbm, meta_hbm, ids_hbm, s0_hbm, s1_hbm,
    masked, cover, tokens_all, meta, ids, s0, s1, feat, occ, adj, in_sems, out_sems,
):
    planes = [slice(x * 4 * COL, (x + 1) * 4 * COL) for x in range(4)]
    pairs = [(occ_hbm, occ), (adj_hbm, adj)]
    pairs += [(feat_hbm.at[:, lanes], feat.at[:, lanes]) for lanes in planes]
    copies = [pltpu.make_async_copy(a, b, in_sems.at[k]) for k, (a, b) in enumerate(pairs)]
    for copy in copies:
        copy.start()
    sent = []

    def send(source, target):
        sent.append(pltpu.make_async_copy(source, target, out_sems.at[len(sent)]))
        sent[-1].start()

    copies[0].wait()
    occupied = occ[...].astype(f32).astype(bf16)
    row = lax.broadcasted_iota(jnp.int32, (64, COL), 0)
    voxel = lax.shift_right_logical(lax.broadcasted_iota(jnp.int32, (64, COL), 1), 6)
    for k in range(16):
        spread = (row == voxel + 4 * k).astype(f32).astype(bf16)
        cov = jnp.dot(occupied, spread, preferred_element_type=f32).astype(bf16)
        cover[:, k * COL : (k + 1) * COL] = cov
    send(cover, cover_hbm)
    copies[1].wait()
    number = adj[...]
    ids[...] = jnp.where(number < 0, FAR, number)
    send(ids, ids_hbm)
    total = jnp.zeros((BRICKS, 128), f32)
    for x in range(4):
        copies[2 + x].wait()
        for y in range(4):
            lanes = column(x, y)
            part = feat[:, lanes] * cover[:, lanes]
            masked[:, lanes] = part
            wide = part.astype(f32)
            total = total + wide[:, :128] + wide[:, 128:]
        send(masked.at[:, planes[x]], masked_hbm.at[:, planes[x]])
    summed = total[:, :C] + total[:, C:]
    tokens = (summed / 8.0).astype(bf16)
    half = BRICKS // 2
    packed = jnp.concatenate([tokens[:half], tokens[half:]], axis=1)
    tokens_all[...] = jnp.broadcast_to(packed[None], tokens_all.shape)
    send(tokens_all, tokens_hbm)
    number = number + 1
    high = lax.shift_right_logical(number, 6).astype(f32).astype(bf16)
    low = jnp.bitwise_and(number, 63).astype(f32).astype(bf16)
    gap = jnp.zeros((BRICKS, C - 27), bf16)
    about = jnp.concatenate([high, gap, low, gap, occupied, tokens], axis=1)
    meta[...] = about
    send(meta, meta_hbm)
    _, odd_y = parities()

    def write(out, near, behind):
        for place, y in ((NEAR, near), (BEHIND, behind)):
            for x in range(4):
                out[:, place + x * COL : place + (x + 1) * COL] = masked[:, column(x, y)]
        out[:, META:] = about

    @pl.when(odd_y)
    def _():
        write(s0, 3, 2)
        write(s1, 0, 1)

    @pl.when(jnp.logical_not(odd_y))
    def _():
        write(s0, 0, 1)
        write(s1, 3, 2)

    send(s0, s0_hbm)
    send(s1, s1_hbm)
    for copy in sent:
        copy.wait()


def fill_band(weight, band):
    zero = jnp.zeros((C, C), bf16)
    for t in range(9):
        for r, z_in in enumerate((0, 1, 2, 3, 4, -1)):
            blocks = []
            for z_out in range(4):
                tap = z_in - z_out + 1
                blocks.append(weight[t * 3 + tap] if 0 <= tap < 3 else zero)
            band[t, r * C : (r + 1) * C, :] = jnp.concatenate(blocks, axis=1)


def message_kernel(masked, t0, t1, x0, x1):
    odd_x, odd_y = parities()

    def write(out, x):
        out[:, : 4 * COL] = face_x(masked, x)
        place = 4 * COL
        for a, b in ((t1, t0), (t0, t1)):
            for plane in (NEAR, BEHIND):
                lanes = slice(plane + x * COL, plane + (x + 1) * COL)
                out[:, place : place + COL] = pick(odd_y, a[:, lanes], b[:, lanes])
                place += COL

    @pl.when(odd_x)
    def _():
        write(x0, 3)
        write(x1, 0)

    @pl.when(jnp.logical_not(odd_x))
    def _():
        write(x0, 0)
        write(x1, 3)


def place_x(ox, x):
    return x if ox == 0 else (0 if ox < 0 else 1)


def sources_of(ox, oy):
    sources = [(0, 0)]
    if ox:
        sources.append((ox, 0))
    if oy:
        sources.append((0, oy))
    if ox and oy:
        sources.append((ox, oy))
    return sources


def own_select(ids, ox, oy):
    base = device_base()
    offsets = [(ox, oy, oz) for oz in ((1, -1) if ox == 0 and oy == 0 else (1, -1, 0))]
    return one_hot(ids, offsets, [device_row(base + id_step(dx, dy)) for dx, dy in sources_of(ox, oy)])


def side_select(ids, side, ox):
    here, there = device_base(), device_base() + id_step(0, side)
    bases = [0] if ox == 0 else [0, id_step(ox, 0)]
    outer = [device_row(here + step) for step in bases]
    inner = [device_row(there + step) for step in bases]
    offsets = [(ox, 0, oz) for oz in ((1, -1) if ox == 0 else (1, -1, 0))]
    return (
        one_hot(ids, offsets, inner),
        one_hot(ids, [(ox, -side, oz) for oz in (1, -1, 0)], outer),
    )


def gather_own(own, from_x, from_y, from_corner, select_of, padded, x_offsets):
    for ox in x_offsets:
        for oy in (-1, 0, 1):
            centre = ox == 0 and oy == 0
            select = select_of(ox, oy)
            for x in {-1: (3,), 0: range(4), 1: (0,)}[ox]:
                for y in {-1: (3,), 0: range(4), 1: (0,)}[oy]:
                    parts = [own(x, y)]
                    if ox:
                        parts.append(from_x(ox, y))
                    if oy:
                        parts.append(from_y(oy, x))
                    if ox and oy:
                        parts.append(from_corner(ox, oy))
                    px = place_x(ox, x)
                    py = {-1: 0, 0: 1 + y, 1: 5}[oy]

                    def store(core, ends, px=px, py=py):
                        padded[px, py, :, :COL] = core
                        padded[px, py, :, COL:] = ends

                    put_column(select, parts, parts[0] if centre else None, store)


def gather_side(own, from_x, from_message, side, select_of, padded, x_offsets):
    mine = {-1: 0, 1: 3}[side]
    rows = slice(0, BRICKS) if side < 0 else slice(BRICKS, 2 * BRICKS)
    for ox in x_offsets:
        select_inner, select_outer = select_of(side, ox)
        for x in {-1: (3,), 0: range(4), 1: (0,)}[ox]:
            px = place_x(ox, x)
            for place, py in ((BEHIND, 1 + side), (NEAR, 1), (None, 1 - side)):

                def store(core, ends, px=px, py=py):
                    padded[px, py, rows, :COL] = core
                    padded[px, py, rows, COL:] = ends

                if place is None:
                    parts = [own(x, mine)]
                    if ox:
                        parts.append(from_x(ox, mine))
                    put_column(select_outer, parts, None, store)
                    continue
                parts = [from_message(side, place + x * COL)]
                if ox:
                    parts.append(from_x(ox, corner_place(side, place)))
                put_column(select_inner, parts, parts[0] if ox == 0 else None, store)


def corner_place(side, plane):
    return 4 + (0 if side < 0 else 2) + (0 if plane == NEAR else 1)


TAP = 6 * C


def taps(padded, side, x_range, first, count):
    parts = []
    for t in range(first, first + count):
        i, j = t // 3, t % 3
        rows = [padded[x + i, j : j + 4].reshape(4 * BRICKS, TAP) for x in x_range]
        if side is not None:
            rows += [side[x + i, j] for x in x_range]
        parts.append(jnp.concatenate(rows, axis=0))
    return jnp.concatenate(parts, axis=1)


def product(lhs, band, first, count):
    rhs = band[first : first + count].reshape(count * TAP, COL)
    return jnp.dot(lhs, rhs, preferred_element_type=f32)


def convolve_inner(inner, side, band, store):
    store((1, 2), product(taps(inner, side, (0, 1), 0, 9), band, 0, 9))
    store((0,), product(taps(inner, side, (-1,), 3, 6), band, 3, 6))
    store((3,), product(taps(inner, side, (2,), 0, 6), band, 0, 6))


def convolve_edge(outer, side, band, x):
    i, place = (0, 0) if x == 0 else (2, 1)
    return product(taps(outer, side, (place - i,), 3 * i, 3), band, 0 if x == 0 else 3, 3)


def four(ref):
    return jnp.concatenate([ref[...]] * 4, axis=1)


def project(tokens, weight):
    return jnp.dot(tokens, weight, preferred_element_type=f32).astype(bf16)


def attention(tokens, packed, w_key, w_value, w_query, w_out):
    group = jnp.concatenate([packed[:, :C], packed[:, C:]], axis=0)
    kv = project(group, jnp.concatenate([w_key, w_value], axis=1))
    queries = project(tokens, w_query)
    rows = queries.shape[0]
    wide = jnp.concatenate([queries, jnp.zeros_like(queries)], axis=1).astype(f32)
    lane = lax.broadcasted_iota(jnp.int32, (rows, 2 * C), 1)
    per_head = [jnp.where(lax.shift_right_logical(lane, 5) == h, wide, 0.0) for h in range(HEADS)]
    wide = jnp.concatenate(per_head, axis=0).astype(bf16)
    logits = lax.dot_general(
        wide, kv, (((1,), (1,)), ((), ())), preferred_element_type=f32
    ) * (1.0 / math.sqrt(C // HEADS))
    top = jnp.max(logits, axis=1, keepdims=True)
    weight = jnp.exp(logits - top)
    total = jnp.sum(weight, axis=1, keepdims=True)
    coarse = weight.astype(bf16)
    fine = (weight - coarse.astype(f32)).astype(bf16)
    mixed = jnp.dot(coarse, kv, preferred_element_type=f32)
    mixed = mixed + jnp.dot(fine, kv, preferred_element_type=f32)
    mixed = mixed / total
    context = jnp.where(lane < C + C // 2, mixed[:rows], mixed[rows:])
    context = jnp.where(lane < C, 0.0, context)
    mean = jnp.sum(context * context, axis=1, keepdims=True) / C
    attended = (context / jnp.sqrt(mean + EPSILON)).astype(bf16)
    w_out = jnp.concatenate([w_out] * 4, axis=1)
    return jnp.dot(attended[:, C:], w_out, preferred_element_type=f32)


def y_reader(t0, t1):
    _, odd_y = parities()

    def from_y(oy, place, width=COL):
        lanes = slice(place, place + width)
        a, b = (t1, t0) if oy < 0 else (t0, t1)
        return pick(odd_y, a[:, lanes], b[:, lanes])

    return from_y


def x_reader(r0, r1):
    odd_x, _ = parities()

    def from_x(ox, k):
        lanes = slice(k * COL, (k + 1) * COL)
        a, b = (r1, r0) if ox < 0 else (r0, r1)
        return pick(odd_x, a[:, lanes], b[:, lanes])

    return from_x


def side_ids(about):
    high, low = about[:, :C].astype(f32), about[:, C : 2 * C].astype(f32)
    number = (high * 64.0 + low).astype(jnp.int32) - 1
    return jnp.where(number < 0, FAR, number)


def global_term(group, w_key, w_value, w_query, w_out):
    count = group.shape[0]
    here = lax.axis_index("sy")
    tokens = []
    for step in (0, count - 1, 1):
        packed = group[lax.rem(here + step, count)]
        tokens += [packed[:, :C], packed[:, C:]]
    packed = group[...].reshape(-1, 2 * C)
    tokens = jnp.concatenate(tokens, axis=0)
    return attention(tokens, packed, w_key[...], w_value[...], w_query[...], w_out[...])


FACE_SLOTS, SIDE_SLOTS = 16, 8


def near_kernel(
    masked, t0, t1, ids_ref, weight, acc, acc_side, band_edge, pack, selects, inner, side_inner,
    band,
):
    from_message = y_reader(t0, t1)
    ids = ids_ref[...]

    def own(x, y):
        return masked[:, column(x, y)]

    def from_y(oy, x):
        return from_message(oy, NEAR + x * COL)

    fill_band(weight, band)
    gather_own(own, None, from_y, None, lambda ox, oy: own_select(ids, ox, oy), inner, (0,))
    numbers = {}
    for side in (-1, 1):
        number = numbers[side] = side_ids(from_message(side, META))
        gather_side(
            own, None, from_message, side,
            lambda side, ox, number=number: side_select(number, side, ox), side_inner, (0,),
        )

    base = device_base()
    for k, ox in enumerate((-1, 1)):
        face = [(ox, oy, oz) for oy in (-1, 0, 1) for oz in (-1, 0, 1)]
        parts = [slot_ids(ids, base + id_step(ox, 0), face, FACE_SLOTS)]
        for oy in (-1, 1):
            corner = [(ox, oy, oz) for oz in (-1, 0, 1)]
            parts.append(slot_ids(ids, base + id_step(ox, oy), corner, SIDE_SLOTS))
        known = jnp.concatenate(parts, axis=1)[:1]
        for n, oy in enumerate((-1, 0, 1)):
            candidates = [device_row(base), known[:, :FACE_SLOTS]]
            if oy:
                candidates += [device_row(base + id_step(0, oy)), known[:, FACE_SLOTS:]]
            value = one_hot(ids, [(ox, oy, oz) for oz in (1, -1, 0)], candidates)
            selects[3 * k + n, :, : value.shape[1]] = value

    def store(x_range, value):
        count = len(x_range)
        for n, x in enumerate(x_range):
            acc[x] = value[n * 4 * BRICKS : (n + 1) * 4 * BRICKS]
            rows = (4 * count + 2 * n) * BRICKS
            acc_side[x] = value[rows : rows + 2 * BRICKS]

    convolve_inner(inner, side_inner, band, store)
    band_edge[:3] = band[:3]
    band_edge[3:] = band[6:]
    for k, ox in enumerate((-1, 1)):
        there = device_base() + id_step(ox, 0)
        pack[2 * k, :, :BRICKS] = compaction(owner_marks(ids, there), FACE_SLOTS).astype(bf16)
        sides = [compaction(owner_marks(numbers[side], there), SIDE_SLOTS) for side in (-1, 1)]
        gap = jnp.zeros_like(sides[0])
        low = jnp.concatenate([sides[0], gap], axis=1)
        high = jnp.concatenate([gap, sides[1]], axis=1)
        both = jnp.concatenate([low, high], axis=0)
        pack[2 * k + 1, :, : 2 * BRICKS] = both.astype(bf16)


def finish(acc, acc_side, x, gain, offset, cover, from_message, term, store, store_side):
    def one(part, which, cov):
        first = jnp.maximum(part * gain + offset, 0.0)
        return ((first + term[which * BRICKS : (which + 1) * BRICKS]) * cov).astype(bf16)

    row = lax.broadcasted_iota(jnp.int32, (64, COL), 0)
    voxel = lax.shift_right_logical(lax.broadcasted_iota(jnp.int32, (64, COL), 1), 6)
    for y in range(4):
        cov = cover[:, column(x, y)].astype(f32)
        store(x, y, one(acc[y * BRICKS : (y + 1) * BRICKS], 0, cov))
    for k, side in enumerate((-1, 1)):
        occupied = from_message(side, META)[:, 2 * C : 3 * C]
        spread = (row == voxel + (x * 16 + (3 - 3 * k) * 4)).astype(f32).astype(bf16)
        cov = jnp.dot(occupied, spread, preferred_element_type=f32)
        store_side(x, side, one(acc_side[k * BRICKS : (k + 1) * BRICKS], 1 + k, cov))


def edge_conv_kernel(
    masked, r0, r1, t0, t1, ids_ref, band_edge, acc, acc_side, total, total_side,
    outer, side_outer,
):
    from_message, from_x = y_reader(t0, t1), x_reader(r0, r1)
    ids = ids_ref[...]

    def own(x, y):
        return masked[:, column(x, y)]

    gather_own(
        own,
        from_x,
        lambda oy, x: from_message(oy, NEAR + x * COL),
        lambda ox, oy: from_x(ox, corner_place(oy, NEAR)),
        lambda ox, oy: own_select(ids, ox, oy),
        outer,
        (-1, 1),
    )
    for side in (-1, 1):
        number = side_ids(from_message(side, META))
        gather_side(
            own, from_x, from_message, side,
            lambda side, ox, number=number: side_select(number, side, ox), side_outer, (-1, 1),
        )
    for n, x in enumerate((0, 3)):
        more = convolve_edge(outer, side_outer, band_edge, x)
        total[n] = acc[x] + more[: 4 * BRICKS]
        total_side[n] = acc_side[x] + more[4 * BRICKS :]


def edge_finish_kernel(
    group, w_key, w_value, w_query, w_out, t0, t1, scale, shift, cover, total, total_side, pack,
    edges, m0, m1, term_out,
):
    odd_x, _ = parities()
    from_message = y_reader(t0, t1)
    term = global_term(group, w_key, w_value, w_query, w_out)
    term_out[...] = term

    def put(x, k, value):
        edges[0 if x == 0 else 1, :, k * COL : (k + 1) * COL] = value

    for n, x in enumerate((0, 3)):
        finish(
            total[n], total_side[n], x, four(scale), four(shift), cover, from_message, term,
            put, lambda x, side, value: put(x, 4 if side < 0 else 5, value),
        )
    messages = []
    for n in range(2):
        face = jnp.dot(
            pack[2 * n, :, :BRICKS], edges[n, :, : 4 * COL], preferred_element_type=f32
        )
        sides = jnp.concatenate(
            [edges[n, :, 4 * COL : 5 * COL], edges[n, :, 5 * COL :]], axis=0
        )
        side = jnp.dot(pack[2 * n + 1, :, : 2 * BRICKS], sides, preferred_element_type=f32)
        messages.append(jnp.concatenate([face, side], axis=1).astype(bf16))
    m0[...] = pick(odd_x, messages[1], messages[0])
    m1[...] = pick(odd_x, messages[0], messages[1])


def edge_reader(edges):
    return lambda x, k: edges[0 if x == 0 else 1, :, k * COL : (k + 1) * COL]


def middle_kernel(
    acc, acc_side, scale, shift, cover, t0, t1, term, edges, ids_ref, weight,
    scale_two, shift_two, masked, acc_out, band_edge, result, mid, mid_side, padded, band,
):
    edge = edge_reader(edges)
    from_message = y_reader(t0, t1)
    ids = ids_ref[...]
    fill_band(weight, band)
    band_edge[:3] = band[:3]
    band_edge[3:] = band[6:]

    def put(x, y, value):
        mid[x - 1, y] = value

    def put_side(x, side, value):
        mid_side[x - 1, 0 if side < 0 else 1] = value

    for x in (1, 2):
        finish(
            acc[x], acc_side[x], x, four(scale), four(shift), cover, from_message, term,
            put, put_side,
        )

    def own(x, y):
        return mid[x - 1, y] if x in (1, 2) else edge(x, y)

    def from_y(oy, x):
        k = 0 if oy < 0 else 1
        return mid_side[x - 1, k] if x in (1, 2) else edge(x, 4 + k)

    gather_own(own, None, from_y, None, lambda ox, oy: own_select(ids, ox, oy), padded, (0,))

    def store(x_range, value):
        for n, x in enumerate(x_range):
            part = value[n * 4 * BRICKS : (n + 1) * 4 * BRICKS]
            if x in (0, 3):
                acc_out[0 if x == 0 else 1] = part
            else:
                gain, offset = four(scale_two), four(shift_two)
                put_result(part, x, gain, offset, cover, masked, result.at[x - 1])

    convolve_inner(padded, None, band, store)


def put_result(total, x, gain, offset, cover, masked, out):
    for y in range(4):
        lanes = column(x, y)
        value = total[y * BRICKS : (y + 1) * BRICKS] * gain + offset
        value = jnp.maximum(value + masked[:, lanes].astype(f32), 0.0)
        value = (value * cover[:, lanes].astype(f32)).astype(bf16)
        out[:, y * COL : (y + 1) * COL] = value


def second_kernel(
    edges, r0, r1, selects, band_edge, scale, shift, cover, masked, acc, middle, refined,
    outer, result, sem,
):
    copies = []

    def send(part, x):
        there = refined.at[:, x * 4 * COL : (x + 1) * 4 * COL]
        copies.append(pltpu.make_async_copy(part, there, sem.at[x]))
        copies[-1].start()

    send(middle.at[0], 1)
    send(middle.at[1], 2)
    odd_x, _ = parities()
    edge = edge_reader(edges)

    def received(ox, rows, k):
        lanes = slice(k * COL, (k + 1) * COL)
        a, b = (r1, r0) if ox < 0 else (r0, r1)
        return pick(odd_x, a[rows, lanes], b[rows, lanes])

    def from_corner(ox, oy):
        return received(ox, slice(None), 4)

    def select_of(ox, oy):
        width = BRICKS + FACE_SLOTS + (BRICKS + 2 * SIDE_SLOTS if oy else 0)
        return selects[(0 if ox < 0 else 3) + oy + 1, :, :width]

    gather_own(
        edge,
        lambda ox, y: received(ox, slice(None), y),
        lambda oy, x: edge(x, 4 if oy < 0 else 5),
        from_corner,
        select_of,
        outer,
        (-1, 1),
    )
    gain, offset = four(scale), four(shift)
    for n, x in enumerate((0, 3)):
        total = acc[n] + convolve_edge(outer, None, band_edge, x)
        put_result(total, x, gain, offset, cover, masked, result.at[n])
        send(result.at[n], x)
    for copy in copies:
        copy.wait()


def exchange(first, second, axis):
    return pair_exchange(first, axis, 1), pair_exchange(second, axis, 0)


def local(
    features, occupancy, adjacency, conv_one, conv_two, scale_one, shift_one,
    scale_two, shift_two, w_query, w_key, w_value, w_out,
):
    n_sy = lax.axis_size("sy")
    whole = shape(BRICKS, 64 * C)
    band_edge = shape(6, TAP, COL)
    own_acc, side_acc = shape(4, 4 * BRICKS, COL, dtype=f32), shape(4, 2 * BRICKS, COL, dtype=f32)
    band = pltpu.VMEM((9, TAP, COL), bf16)
    inner = pltpu.VMEM((4, 6, BRICKS, TAP), bf16)
    outer = pltpu.VMEM((2, 6, BRICKS, TAP), bf16)
    side_inner = pltpu.VMEM((4, 3, 2 * BRICKS, TAP), bf16)
    side_outer = pltpu.VMEM((2, 3, 2 * BRICKS, TAP), bf16)
    inputs = (features, occupancy, adjacency)
    message = shape(BRICKS, Y_LANES)
    prepared = [
        whole, whole, shape(n_sy, BRICKS // 2, 2 * C), shape(BRICKS, 4 * C),
        shape(BRICKS, 27, dtype=jnp.int32), message, message,
    ]
    masked, cover, tokens, meta, ids, s0, s1 = call(
        prepare_kernel,
        prepared,
        inputs,
        [pltpu.VMEM(v.shape, v.dtype) for v in (*prepared, *inputs)]
        + [pltpu.SemaphoreType.DMA((6,)), pltpu.SemaphoreType.DMA((10,))],
        bytes_accessed=2 << 20,
        hbm_in=True,
        hbm_out=True,
    )
    rows = [v.reshape(1, C) for v in (scale_one, shift_one, scale_two, shift_two)]
    t0, t1 = exchange(s0, s1, "sy")
    group = lax.all_to_all(tokens, "sy", 0, 0)
    x_message = shape(BRICKS, 8 * COL)
    x0, x1 = call(
        message_kernel, [x_message] * 2, (masked, t0, t1), flops=1 << 35, bytes_accessed=1 << 20
    )
    r0, r1 = exchange(x0, x1, "sx")
    acc, acc_side, band_one, pack, selects = call(
        near_kernel,
        [
            own_acc, side_acc, band_edge, shape(4, FACE_SLOTS, 128),
            shape(6, 3 * BRICKS, 128),
        ],
        (masked, t0, t1, ids, conv_one),
        [inner, side_inner, band],
        flops=1 << 33,
        bytes_accessed=2 << 20,
    )
    total, total_side = call(
        edge_conv_kernel,
        [
            shape(2, 4 * BRICKS, COL, dtype=f32),
            shape(2, 2 * BRICKS, COL, dtype=f32),
        ],
        (masked, r0, r1, t0, t1, ids, band_one, acc, acc_side),
        [outer, side_outer],
        flops=2 * 384 * 1152 * 256,
        bytes_accessed=4 << 20,
    )
    group, total = lax.optimization_barrier((group, total))
    out_message = shape(FACE_SLOTS, 5 * COL)
    edges, m0, m1, term = call(
        edge_finish_kernel,
        [
            shape(2, BRICKS, 6 * COL), out_message, out_message,
            shape(3 * BRICKS, COL, dtype=f32),
        ],
        (
            group, w_key, w_value, w_query, w_out, t0, t1, rows[0], rows[1], cover, total,
            total_side, pack,
        ),
        flops=1 << 26,
        bytes_accessed=2 << 20,
    )
    r0, r1 = exchange(m0, m1, "sx")
    acc, band_two, half = call(
        middle_kernel,
        [shape(2, 4 * BRICKS, COL, dtype=f32), band_edge, shape(2, BRICKS, 4 * COL)],
        (
            acc, acc_side, rows[0], rows[1], cover, t0, t1, term, edges, ids, conv_two,
            rows[2], rows[3], masked,
        ),
        [
            pltpu.VMEM((2, 4, BRICKS, COL), bf16),
            pltpu.VMEM((2, 2, BRICKS, COL), bf16),
            inner,
            band,
        ],
        flops=1 << 33,
        bytes_accessed=4 << 20,
    )
    return call(
        second_kernel,
        whole,
        (
            edges, r0, r1, selects, band_two, rows[2], rows[3], cover, masked, acc, half,
        ),
        [outer, pltpu.VMEM((2, BRICKS, 4 * COL), bf16), pltpu.SemaphoreType.DMA((4,))],
        flops=2 * 256 * 1152 * 256,
        bytes_accessed=3 << 20,
        hbm_out=True,
    )


def solution(mesh):
    split = P(("sx", "sy"), None)
    return jax.shard_map(
        local,
        mesh=mesh,
        in_specs=(split,) * 3 + (P(),) * 10,
        out_specs=split,
        check_vma=False,
    )
```
